128 devices in a mesh: seq: 4 (over y), head: 8 (over x, z_hi), dp: 4 (over z_lo, core).
Axes of the slice: x: 4, y: 4, z: 4 (z_hi: 2, z_lo: 2; z = z_hi * 2 + z_lo), core: 2. Of those that a mesh axis runs over, the one named last changes fastest.
Arguments:
- tokens: bfloat16 [8192, 3072], P(('dp', 'seq', 'head')), parts along dimension 0, may hold values from -6 to 6
- norm_gain: float32 [2, 3072], replicated, may hold values from 0.5 to 1.5
- qkv_weight: bfloat16 [2, 3072, 9216], P(None, None, 'head'), may hold values from -0.109375 to 0.109375
- rate_weight: bfloat16 [2, 3072, 48], P(None, None, 'head'), may hold values from -0.109375 to 0.109375
- rate_base: float32 [2, 48], P(None, 'head'), may hold values from 0.003 to 0.03
- fast_first: float32 [2, 48, 64, 256], P(None, 'head'), may hold values from -0.75 to 0.75
- fast_second: float32 [2, 48, 64, 256], P(None, 'head'), may hold values from -0.375 to 0.375
- inner_gain: float32 [2, 48, 64], P(None, 'head'), may hold values from 0.1 to 1.9
- out_weight: bfloat16 [2, 3072, 3072], P(None, 'head'), may hold values from -0.109375 to 0.109375
Outputs:
- stream_out: bfloat16 [8192, 3072], P(('dp', 'seq', 'head')), parts along dimension 0
The draws below stay inside these ranges and needn't reach their ends.
There are 4 independent parts, one for each index of `dp`. The reference program is written for one: setup_inputs(seed, part) draws one part's arguments, and reference() takes and returns one part's arrays. A program takes and returns all parts, laid end to end along the dimension named above; an argument that names none is the same for every part. Nothing has to cross between parts.
All inputs are finite; a program needn't handle non-finite values.
Results may differ from the reference program's by a relative error of at most 0.027.
Values may be sent and summed in bfloat16 or wider, within the bound.
No kernel may reach another device: no remote copies, remote signals or barrier semaphores. Data moves between devices by JAX's collectives and lax.ppermute only.
A program may use at most 192 MiB of HBM per device.

```python
import math
from functools import partial
import jax
import jax.numpy as jnp
from jax import lax

D = 3072
HEADS = 48
HEAD_DIM = 64
INNER = 256
MB = 64
LAYERS = 2
TOKENS = 2048


def steps_of(own_key, dims, cuts, least, largest):
    gain = 1.0
    for dim, shards_of in cuts:
        steps = jax.random.uniform(jax.random.fold_in(jax.random.fold_in(own_key, 6), dim), (shards_of,), jnp.float32, least / len(cuts), largest / len(cuts))
        gain = gain * jnp.repeat(jnp.exp(steps), dims[dim] // shards_of).reshape((-1,) + (1,) * (len(dims) - 1 - dim))
    return gain


def noise(stream_key, extent, width, most, pieces=(), kind=jnp.bfloat16):
    factor_of = steps_of(stream_key, extent, pieces, -0.22, 0.18) if pieces else 1.0
    drawn = jax.random.normal(stream_key, extent, jnp.float32) * width * factor_of
    return jnp.minimum(jnp.maximum(drawn, -most), most).astype(kind)


def setup_inputs(seed: int = 0, part: int = 0) -> dict:
    key_list = jax.random.split(jax.random.key(seed), 10)
    part_keys = jax.random.split(jax.random.fold_in(key_list[9], part), 10)
    tokens = noise(part_keys[0], (TOKENS, D), 1.0, 6.0, ((0, 32),))
    norm_gain = jnp.clip(1.0 + 0.1 * jax.random.normal(key_list[1], (LAYERS, D), jnp.float32), 0.5, 1.5)
    qkv_weight = noise(key_list[2], (LAYERS, D, HEADS * 3 * HEAD_DIM), D ** -0.5, 0.109375, ((2, 8),))
    rate_weight = noise(key_list[3], (LAYERS, D, HEADS), D ** -0.5, 0.109375, ((2, 8),))
    rate_base = jnp.clip(jnp.exp(math.log(0.03) - 2.3025851 * jax.random.uniform(key_list[4], (LAYERS, HEADS), jnp.float32) ** steps_of(key_list[4], (LAYERS, HEADS), ((1, 8),), -0.2, 0.2)), 0.003, 0.03)
    fast_first = noise(key_list[5], (LAYERS, HEADS, HEAD_DIM, INNER), HEAD_DIM ** -0.5, 0.75, ((1, 8),), jnp.float32)
    fast_second = noise(key_list[6], (LAYERS, HEADS, HEAD_DIM, INNER), INNER ** -0.5, 0.375, ((1, 8),), jnp.float32)
    inner_gain = jnp.clip(1.0 + 0.18 * jax.random.normal(key_list[7], (LAYERS, HEADS, HEAD_DIM), jnp.float32), 0.1, 1.9)
    out_weight = noise(key_list[8], (LAYERS, HEADS * HEAD_DIM, D), (HEADS * HEAD_DIM) ** -0.5, 0.109375, ((1, 8),))
    return {"tokens": tokens, "norm_gain": norm_gain, "qkv_weight": qkv_weight, "rate_weight": rate_weight, "rate_base": rate_base, "fast_first": fast_first, "fast_second": fast_second, "inner_gain": inner_gain, "out_weight": out_weight}


def narrow_product(form, left, right):
    return jnp.einsum(form, left.astype(jnp.bfloat16), right.astype(jnp.bfloat16), preferred_element_type=jnp.float32)

def inner_apply(first_mat, second_mat, gain_rows, inputs):
    hidden = jax.nn.gelu(narrow_product('hnd,hdf->hnf', inputs, first_mat))
    result = narrow_product('hnf,hdf->hnd', hidden, second_mat)
    centre = result - lax.optimization_barrier(jnp.mean(result, axis=-1, keepdims=True))
    spread = lax.optimization_barrier(jnp.mean(centre * centre, axis=-1, keepdims=True))
    return centre * lax.rsqrt(spread + 1e-05) * gain_rows[:, None, :]

def inner_loss(weights, gain_rows, key_rows, target_rows, gate_rates):
    predicted = inner_apply(weights[0], weights[1], gain_rows, key_rows)
    differ = predicted - target_rows
    return jnp.sum(gate_rates[..., None] * differ * differ) * (0.5 / key_rows.shape[1])

def update(gain_rows, weights, batch_rows):
    queries, key_rows, value_rows, gate_rates = batch_rows
    gradient = jax.grad(inner_loss)(weights, gain_rows, key_rows, value_rows - key_rows, gate_rates)
    renewed = (weights[0] - gradient[0].astype(jnp.float32), weights[1] - gradient[1].astype(jnp.float32))
    return (renewed, queries + inner_apply(renewed[0], renewed[1], gain_rows, queries))

def project_inputs(stream, gain_vector, qkv_cols, rate_cols, rate_scale):
    widened = stream.astype(jnp.float32)
    mean_square = lax.optimization_barrier(jnp.mean(widened * widened, axis=-1, keepdims=True))
    normed = (widened * lax.rsqrt(mean_square + 1e-06) * gain_vector).astype(jnp.bfloat16)
    packed = jnp.dot(normed, qkv_cols, preferred_element_type=jnp.float32)
    token_count = stream.shape[0]
    head_count = rate_cols.shape[1]
    packed = packed.reshape(token_count // MB, MB, head_count, 3, -1).transpose(0, 2, 3, 1, 4)
    gate_rates = rate_scale[None, :] * jax.nn.sigmoid(jnp.dot(normed, rate_cols, preferred_element_type=jnp.float32))
    gate_rates = gate_rates.reshape(token_count // MB, MB, head_count).transpose(0, 2, 1)
    return (packed[:, :, 0], packed[:, :, 1], packed[:, :, 2], gate_rates)

def reference(tokens, norm_gain, qkv_weight, rate_weight, rate_base, fast_first, fast_second, inner_gain, out_weight):
    stream = tokens
    for layer_index in range(LAYERS):
        batches = project_inputs(stream, norm_gain[layer_index], qkv_weight[layer_index], rate_weight[layer_index], rate_base[layer_index])
        initial = (fast_first[layer_index], fast_second[layer_index])
        unused, outputs = lax.scan(partial(update, inner_gain[layer_index]), initial, batches)
        mixed = outputs.transpose(0, 2, 1, 3).reshape(TOKENS, HEADS * HEAD_DIM).astype(jnp.bfloat16)
        projected = jnp.dot(mixed, out_weight[layer_index], preferred_element_type=jnp.float32)
        stream = (stream.astype(jnp.float32) + projected).astype(jnp.bfloat16)
    return stream
```

```python
import functools

import jax
import jax.numpy as jnp
from jax import lax
from jax.experimental import pallas as pl
from jax.experimental.pallas import tpu as pltpu
from jax.sharding import PartitionSpec as P

F32 = jnp.float32
B16 = jnp.bfloat16
MB = 64
GELU_A = 0.7978845608028654
GELU_B = 0.044715
NN = (((1,), (0,)), ((), ()))
NT = (((1,), (1,)), ((), ()))


def dot(left, right, dims=NN):
    return lax.dot_general(left, right, dims, preferred_element_type=F32)


def first_half(shape):
    return lax.broadcasted_iota(jnp.int32, shape, len(shape) - 1) < 64


def spread(x):
    mask = first_half(x.shape)
    zero = jnp.zeros_like(x)
    return jnp.concatenate([jnp.where(mask, x, zero), jnp.where(mask, zero, x)], axis=0)


def flip(x):
    y = spread(x).T
    return y[:64] + y[64:]


def fold(y):
    return jnp.where(first_half((64, 128)), y[:64], y[64:])


def mean0(x):
    return jnp.sum(x, axis=0, keepdims=True) * (1.0 / 64)


def normalise(y):
    centre = y - mean0(y)
    scale = lax.rsqrt(mean0(centre * centre) + 1e-5)
    return centre * scale, scale


def gelu_parts(h):
    square = h * h
    t = jnp.tanh(h * (GELU_A + (GELU_A * GELU_B) * square))
    half = 0.5 * h
    return square, t, half, half + half * t


def chain_steps(pairs, batches, qkv, rate, gain, w1, w2, out, rows, target):
    def block(b):
        return pl.ds(pl.multiple_of(b * MB, MB), MB)

    def tiles(b, p):
        return [qkv[block(b), p * 384 + j * 128 : p * 384 + (j + 1) * 128] for j in range(3)]

    def queries(b, p):
        t0, t1, _ = tiles(b, p)
        return jnp.where(first_half(t0.shape), t0, t1)

    def prepare_keys(b):
        for p in range(pairs):
            t0, t1, t2 = tiles(b, p)
            mask = first_half(t0.shape)
            keys = pltpu.roll(jnp.where(mask, t2, t0), 64, 1)
            values = jnp.where(mask, t1, t2)
            rows[p, 0:128] = spread(keys).astype(B16)
            target[p] = flip(values - keys)

    def prepare_queries(b):
        for p in range(pairs):
            rows[p, 128:256] = spread(queries(b, p)).astype(B16)

    def put(b, p, y):
        result = queries(b, p) + flip(normalise(y)[0] * gain[p])
        out[block(b), p * 128 : (p + 1) * 128] = result.astype(B16)

    prepare_keys(0)
    rows[:, 128:256] = jnp.zeros((pairs, 128, 128), B16)

    def step(b, carry):
        first = [w1[p].astype(B16) for p in range(pairs)]
        second = [w2[p].astype(B16) for p in range(pairs)]
        hidden = [dot(first[p], rows[p], NT) for p in range(pairs)]
        act, slope, act_q = [], [], []
        for p in range(pairs):
            square, t, half, a = gelu_parts(hidden[p][:, :128])
            slope.append(0.5 + 0.5 * t + half * (1.0 - t * t) * (GELU_A + (3 * GELU_A * GELU_B) * square))
            act.append(a.astype(B16))
        for p in range(pairs):
            act_q.append(gelu_parts(hidden[p][:, 128:])[3].astype(B16))
        result, result_q = [], []
        for p in range(pairs):
            turned = second[p].T
            result.append(fold(dot(turned, act[p])))
            result_q.append(fold(dot(turned, act_q[p])))
        cotangent = []
        for p in range(pairs):
            y, scale = normalise(result[p])
            dy = (y * gain[p] - target[p]) * rate[b, p] * gain[p]
            dy = scale * (dy - mean0(dy) - y * mean0(dy * y))
            cotangent.append(spread(dy).astype(B16))
        for p in range(pairs):
            down = (dot(second[p], cotangent[p]) * slope[p]).astype(B16)
            w1[p] = w1[p] - dot(down, rows[p, 0:128])
            w2[p] = w2[p] - dot(act[p], cotangent[p], NT)
        for p in range(pairs):
            put(jnp.maximum(b - 1, 0), p, result_q[p])
        prepare_keys(jnp.minimum(b + 1, batches - 1))
        prepare_queries(b)
        return carry

    lax.fori_loop(0, batches, step, 0)
    for p in range(pairs):
        hidden = dot(w1[p].astype(B16), rows[p, 128:256], NT)
        a = gelu_parts(hidden)[3].astype(B16)
        put(batches - 1, p, fold(dot(w2[p].astype(B16).T, a)))


def chain_kernel(pairs, batches, turn, *refs):
    active, qkv, rate, gain, state = refs[:5]
    out, state_out = refs[-13:-11] if turn == 0 else refs[-12:-10]
    scratch = refs[-11:] if turn == 0 else refs[-10:]
    qkv_v, rate_v, gain_v, state_v, out_v, w1, w2, rows, target, sems = scratch[-10:]
    final = scratch[0] if turn == 0 else state_v

    @pl.when(active[0] == turn)
    def _():
        moves = [
            pltpu.make_async_copy(a, b, sems.at[i])
            for i, (a, b) in enumerate([(qkv, qkv_v), (rate, rate_v), (gain, gain_v), (state, state_v)])
        ]
        for move in moves:
            move.start()
        for move in moves:
            move.wait()
        w1[...] = state_v[0].astype(F32)
        w2[...] = state_v[1].astype(F32)
        chain_steps(pairs, batches, qkv_v, rate_v, gain_v, w1, w2, out_v, rows, target)
        final[0] = w1[...].astype(B16)
        final[1] = w2[...].astype(B16)
        back = [
            pltpu.make_async_copy(final, state_out, sems.at[0]),
            pltpu.make_async_copy(out_v, out, sems.at[1]),
        ]
        for move in back:
            move.start()
        for move in back:
            move.wait()


def run_chain(turn, place, qkv, rate, gain, state, out):
    tokens = qkv.shape[0]
    pairs = state.shape[1]
    batches = tokens // MB
    first = turn == 0
    anywhere = pl.BlockSpec(memory_space=pl.ANY)
    scratch = [
        pltpu.VMEM(qkv.shape, F32),
        pltpu.VMEM(rate.shape, F32),
        pltpu.VMEM(gain.shape, F32),
        pltpu.VMEM(state.shape, state.dtype),
        pltpu.VMEM((tokens, pairs * 128), B16),
        pltpu.VMEM(state.shape[1:], F32),
        pltpu.VMEM(state.shape[1:], F32),
        pltpu.VMEM((pairs, 256, 128), B16),
        pltpu.VMEM((pairs, 64, 128), F32),
        pltpu.SemaphoreType.DMA((4,)),
    ]
    if first:
        scratch = [pltpu.VMEM(state.shape, B16)] + scratch
    operands = [place, qkv, rate, gain, state] + ([] if first else [out])
    return pl.pallas_call(
        functools.partial(chain_kernel, pairs, batches, turn),
        out_shape=[
            jax.ShapeDtypeStruct((tokens, pairs * 128), B16),
            jax.ShapeDtypeStruct(state.shape, B16),
        ],
        in_specs=[pl.BlockSpec(memory_space=pltpu.SMEM)] + [anywhere] * (len(operands) - 1),
        out_specs=[anywhere, anywhere],
        scratch_shapes=scratch,
        input_output_aliases={} if first else {5: 0},
        compiler_params=pltpu.CompilerParams(vmem_limit_bytes=32 << 20),
        name=f"chain_{turn}",
    )(*operands)


def product_kernel(left, right, out):
    out[...] = dot(left[...], right[0]).astype(out.dtype)


def product(left, stack, layer, tile, kind):
    rows, depth = left.shape
    columns = stack.shape[2]
    return pl.pallas_call(
        product_kernel,
        grid=(columns // tile,),
        out_shape=jax.ShapeDtypeStruct((rows, columns), kind),
        in_specs=[
            pl.BlockSpec((rows, depth), lambda i: (0, 0)),
            pl.BlockSpec((1, depth, tile), lambda i: (layer, 0, i)),
        ],
        out_specs=pl.BlockSpec((rows, tile), lambda i: (0, i)),
        compiler_params=pltpu.CompilerParams(vmem_limit_bytes=32 << 20),
        name="product",
    )(left, stack)


def to_head_order(block):
    count = lax.axis_size("head")
    return lax.all_to_all(jnp.broadcast_to(block[None], (count,) + block.shape), "head", 0, 0, tiled=True)


def body(tokens, norm_gain, qkv_weight, rate_weight, rate_base, fast_first, fast_second, inner_gain, out_weight):
    seq_count = lax.axis_size("seq")
    place = lax.axis_index("seq").astype(jnp.int32).reshape(1)
    layers, heads = rate_base.shape
    pairs = heads // 2

    def turned(weights):
        return weights.reshape(layers, pairs, 128, 256).swapaxes(2, 3)

    initial = jnp.stack([turned(fast_first), turned(fast_second)], axis=1)
    gains = jnp.repeat(inner_gain.reshape(layers, pairs, 2, 64).swapaxes(2, 3), MB, axis=3)
    stream = tokens.astype(F32)
    for layer in range(layers):
        mean_square = jnp.mean(stream * stream, axis=-1, keepdims=True)
        normed = (stream * lax.rsqrt(mean_square + 1e-06) * norm_gain[layer]).astype(B16)
        rows = to_head_order(normed).reshape(-1, normed.shape[1])
        qkv = product(rows, qkv_weight, layer, 384, F32)
        batches = rows.shape[0] // MB
        rate = jax.nn.sigmoid(jnp.dot(rows, rate_weight[layer], preferred_element_type=F32))
        rate = rate * (rate_base[layer] * (1.0 / MB))
        rate = rate.reshape(batches, MB, pairs, 2).transpose(0, 2, 3, 1).reshape(batches, pairs, 1, 128)
        state, mixed = initial[layer], None
        for turn in range(seq_count):
            mixed, state = run_chain(turn, place, qkv, rate, gains[layer], state, mixed)
            if turn < seq_count - 1:
                state = lax.ppermute(state, "seq", [(turn, turn + 1)])
        parts = product(mixed, out_weight, layer, 1024, B16).reshape(lax.axis_size("head"), -1, stream.shape[1])
        parts = lax.all_to_all(parts, "head", 0, 0, tiled=True)
        summed = jnp.sum(parts.astype(F32), axis=0)
        out = (stream + summed).astype(B16)
        stream = out.astype(F32)
    return out


def solution(mesh):
    rows = P(("dp", "seq", "head"), None)
    in_specs = (
        rows,
        P(),
        P(None, None, "head"),
        P(None, None, "head"),
        P(None, "head"),
        P(None, "head", None, None),
        P(None, "head", None, None),
        P(None, "head", None),
        P(None, "head", None),
    )
    return jax.shard_map(body, mesh=mesh, in_specs=in_specs, out_specs=rows, check_vma=False)
```

```python
import functools

import jax
import jax.numpy as jnp
from jax import lax
from jax.experimental import pallas as pl
from jax.experimental.pallas import tpu as pltpu
from jax.sharding import PartitionSpec as P

F32 = jnp.float32
B16 = jnp.bfloat16
MB = 64
GELU_A = 0.7978845608028654
GELU_B = 0.044715
NN = (((1,), (0,)), ((), ()))
NT = (((1,), (1,)), ((), ()))


def dot(left, right, dims=NN):
    return lax.dot_general(left, right, dims, preferred_element_type=F32)


def first_half(shape):
    return lax.broadcasted_iota(jnp.int32, shape, len(shape) - 1) < 64


def spread(x):
    mask = first_half(x.shape)
    zero = jnp.zeros_like(x)
    return jnp.concatenate([jnp.where(mask, x, zero), jnp.where(mask, zero, x)], axis=0)


def flip(x):
    y = spread(x).T
    return y[:64] + y[64:]


def fold(y):
    return jnp.where(first_half((64, 128)), y[:64], y[64:])


def mean0(x):
    return jnp.sum(x, axis=0, keepdims=True) * (1.0 / 64)


def normalise(y):
    centre = y - mean0(y)
    scale = lax.rsqrt(mean0(centre * centre) + 1e-5)
    return centre * scale, scale


def gelu_parts(h):
    square = h * h
    t = jnp.tanh(h * (GELU_A + (GELU_A * GELU_B) * square))
    half = 0.5 * h
    return square, t, half, half + half * t


def chain_steps(pairs, batches, where, qkv, rate, gain, w1, w2, out, rows, target):
    def block(b):
        return pl.ds(pl.multiple_of(where[b + 1] * MB, MB), MB)

    def rates(b, p):
        slot = rate[where[b + 1]]
        return jnp.concatenate([slot[2 * p : 2 * p + 1], slot[2 * p + 1 : 2 * p + 2]], axis=1)

    def tiles(b, p):
        return [qkv[block(b), p * 384 + j * 128 : p * 384 + (j + 1) * 128] for j in range(3)]

    def queries(b, p):
        t0, t1, _ = tiles(b, p)
        return jnp.where(first_half(t0.shape), t0, t1)

    def prepare_keys(b):
        for p in range(pairs):
            t0, t1, t2 = tiles(b, p)
            mask = first_half(t0.shape)
            keys = pltpu.roll(jnp.where(mask, t2, t0), 64, 1)
            values = jnp.where(mask, t1, t2)
            rows[p, 0:128] = spread(keys).astype(B16)
            target[p] = flip(values - keys)

    def prepare_queries(b):
        for p in range(pairs):
            rows[p, 128:256] = spread(queries(b, p)).astype(B16)

    def put(b, p, y):
        result = queries(b, p) + flip(normalise(y)[0] * gain[p])
        out[block(b), p * 128 : (p + 1) * 128] = result.astype(B16)

    prepare_keys(0)
    rows[:, 128:256] = jnp.zeros((pairs, 128, 128), B16)

    def step(b, carry):
        first = [w1[p].astype(B16) for p in range(pairs)]
        second = [w2[p].astype(B16) for p in range(pairs)]
        hidden = [dot(first[p], rows[p], NT) for p in range(pairs)]
        act, slope, act_q = [], [], []
        for p in range(pairs):
            square, t, half, a = gelu_parts(hidden[p][:, :128])
            slope.append(0.5 + 0.5 * t + half * (1.0 - t * t) * (GELU_A + (3 * GELU_A * GELU_B) * square))
            act.append(a.astype(B16))
        for p in range(pairs):
            act_q.append(gelu_parts(hidden[p][:, 128:])[3].astype(B16))
        result, result_q = [], []
        for p in range(pairs):
            turned = second[p].T
            result.append(fold(dot(turned, act[p])))
            result_q.append(fold(dot(turned, act_q[p])))
        cotangent = []
        for p in range(pairs):
            y, scale = normalise(result[p])
            dy = (y * gain[p] - target[p]) * rates(b, p) * gain[p]
            dy = scale * (dy - mean0(dy) - y * mean0(dy * y))
            cotangent.append(spread(dy).astype(B16))
        for p in range(pairs):
            down = (dot(second[p], cotangent[p]) * slope[p]).astype(B16)
            w1[p] = w1[p] - dot(down, rows[p, 0:128])
            w2[p] = w2[p] - dot(act[p], cotangent[p], NT)
        for p in range(pairs):
            put(jnp.maximum(b - 1, 0), p, result_q[p])
        prepare_keys(jnp.minimum(b + 1, batches - 1))
        prepare_queries(b)
        return carry

    lax.fori_loop(0, batches, step, 0)
    for p in range(pairs):
        hidden = dot(w1[p].astype(B16), rows[p, 128:256], NT)
        a = gelu_parts(hidden)[3].astype(B16)
        put(batches - 1, p, fold(dot(w2[p].astype(B16).T, a)))


def chain_kernel(pairs, first_pair, batches, turn, where, qkv_a, qkv_b, rate_a, rate_b, gain, state, *refs):
    out, state_out, qkv_v, rate_v, gain_v, state_v, final, out_v, w1, w2, rows, target, sems = refs[-13:]
    columns = pl.ds(first_pair * 384, pairs * 384)
    near, far = qkv_a.shape[0], qkv_b.shape[0]

    @pl.when(where[0] == turn)
    def _():
        moves = [
            (qkv_a.at[:, columns], qkv_v.at[pl.ds(0, near)]),
            (qkv_b.at[:, columns], qkv_v.at[pl.ds(near, far)]),
            (rate_a, rate_v.at[pl.ds(0, near // MB)]),
            (rate_b, rate_v.at[pl.ds(near // MB, far // MB)]),
            (gain.at[pl.ds(first_pair, pairs)], gain_v),
            (state, state_v),
        ]
        moves = [pltpu.make_async_copy(a, b, sems.at[i]) for i, (a, b) in enumerate(moves)]
        for move in moves:
            move.start()
        for move in moves:
            move.wait()
        w1[...] = state_v[0].astype(F32)
        w2[...] = state_v[1].astype(F32)
        chain_steps(pairs, batches, where, qkv_v, rate_v.at[:, pl.ds(2 * first_pair, 2 * pairs)], gain_v, w1, w2, out_v, rows, target)
        final[0] = w1[...].astype(B16)
        final[1] = w2[...].astype(B16)
        back = [
            pltpu.make_async_copy(final, state_out, sems.at[0]),
            pltpu.make_async_copy(out_v, out.at[:, pl.ds(first_pair * 128, pairs * 128)], sems.at[1]),
        ]
        for move in back:
            move.start()
        for move in back:
            move.wait()


ANYWHERE = pl.BlockSpec(memory_space=pl.ANY)
MOST = 56 << 20


def run_chain(turn, first_pair, where, qkv, rate, gain, state, out):
    tokens = sum(part.shape[0] for part in qkv)
    heads = rate[0].shape[1]
    pairs = state.shape[1]
    batches = tokens // MB
    operands = [where, *qkv, *rate, gain, state] + ([] if out is None else [out])
    return pl.pallas_call(
        functools.partial(chain_kernel, pairs, first_pair, batches, turn),
        out_shape=[
            jax.ShapeDtypeStruct((tokens, heads * 64), B16),
            jax.ShapeDtypeStruct(state.shape, B16),
        ],
        in_specs=[pl.BlockSpec(memory_space=pltpu.SMEM)] + [ANYWHERE] * (len(operands) - 1),
        out_specs=[ANYWHERE, ANYWHERE],
        scratch_shapes=[
            pltpu.VMEM((tokens, pairs * 384), F32),
            pltpu.VMEM((batches, heads, MB), F32),
            pltpu.VMEM((pairs,) + gain.shape[1:], F32),
            pltpu.VMEM(state.shape, state.dtype),
            pltpu.VMEM(state.shape, B16),
            pltpu.VMEM((tokens, pairs * 128), B16),
            pltpu.VMEM(state.shape[1:], F32),
            pltpu.VMEM(state.shape[1:], F32),
            pltpu.VMEM((pairs, 256, 128), B16),
            pltpu.VMEM((pairs, 64, 128), F32),
            pltpu.SemaphoreType.DMA((6,)),
        ],
        input_output_aliases={} if out is None else {7: 0},
        compiler_params=pltpu.CompilerParams(vmem_limit_bytes=MOST),
        cost_estimate=pl.CostEstimate(flops=10**9, bytes_accessed=30 * 10**6, transcendentals=0),
        name=f"chain_{turn}",
    )(*operands)


def project_kernel(count, *refs):
    blocks = refs[:count]
    weight, rate_weight, base, out, rate, rows, sems = refs[count:]

    @pl.when(pl.program_id(0) == 0)
    def _():
        moves = [pltpu.make_async_copy(b, rows.at[pl.ds(i * MB, MB)], sems.at[i]) for i, b in enumerate(blocks)]
        for move in moves:
            move.start()
        for move in moves:
            move.wait()
        gate = dot(rows[...], rate_weight[0]).T
        gate = base[0] * jax.nn.sigmoid(gate)
        for i in range(count):
            rate[i] = gate[:, i * MB : (i + 1) * MB]

    out[...] = dot(rows[...], weight[0])


def project(blocks, layer, qkv_weight, rate_weight, base):
    count = len(blocks)
    depth, columns = qkv_weight.shape[1:]
    heads = rate_weight.shape[2]
    tile = 384
    return pl.pallas_call(
        functools.partial(project_kernel, count),
        grid=(columns // tile,),
        out_shape=[
            jax.ShapeDtypeStruct((count * MB, columns), F32),
            jax.ShapeDtypeStruct((count, heads, MB), F32),
        ],
        in_specs=[ANYWHERE] * count
        + [
            pl.BlockSpec((1, depth, tile), lambda i: (layer, 0, i)),
            pl.BlockSpec((1, depth, heads), lambda i: (layer, 0, 0)),
            pl.BlockSpec((1, heads, 1), lambda i: (layer, 0, 0)),
        ],
        out_specs=[
            pl.BlockSpec((count * MB, tile), lambda i: (0, i)),
            pl.BlockSpec((count, heads, MB), lambda i: (0, 0, 0)),
        ],
        scratch_shapes=[pltpu.VMEM((count * MB, depth), B16), pltpu.SemaphoreType.DMA((count,))],
        compiler_params=pltpu.CompilerParams(vmem_limit_bytes=MOST),
        cost_estimate=pl.CostEstimate(flops=2 * count * MB * depth * columns, bytes_accessed=depth * columns * 2, transcendentals=0),
        name="project",
    )(*blocks, qkv_weight, rate_weight, base)


def unproject_kernel(count, left, right, *outs):
    total = dot(left[...], right[0]).astype(B16)
    for i in range(count):
        outs[i][...] = total[i * MB : (i + 1) * MB]


def unproject(mixed, first, count, layer, out_weight):
    depth, columns = out_weight.shape[1:]
    tile = 1024
    return pl.pallas_call(
        functools.partial(unproject_kernel, count),
        grid=(columns // tile,),
        out_shape=[jax.ShapeDtypeStruct((MB, columns), B16)] * count,
        in_specs=[
            pl.BlockSpec((count * MB, depth), lambda i: (0, 0)),
            pl.BlockSpec((1, depth, tile), lambda i: (layer, 0, i)),
        ],
        out_specs=[pl.BlockSpec((MB, tile), lambda i: (0, i))] * count,
        compiler_params=pltpu.CompilerParams(vmem_limit_bytes=MOST),
        cost_estimate=pl.CostEstimate(flops=2 * count * MB * depth * columns, bytes_accessed=depth * columns * 2, transcendentals=0),
        name="unproject",
    )(mixed[first * MB : (first + count) * MB], out_weight)


NEAR = [(0, 0), (0, 1), (1, 0), (3, 0), (2, 0)]
FAR = [(1, 1), (3, 1), (2, 1)]
SLOTS = NEAR + FAR


def send(block, dx, dz):
    route = [(2 * x + z, 2 * ((x + dx) % 4) + (z ^ dz)) for x in range(4) for z in range(2)]
    return lax.ppermute(block, "head", route)


def fetch(block, dx, dz):
    return send(block, -dx, dz)


def gather_near(own):
    return [own] + [fetch(own, dx, dz) for dx, dz in NEAR[1:]]


def gather_far(near):
    return [fetch(near[1], 1, 0), fetch(near[1], 3, 0), fetch(near[4], 0, 1)]


def add(*blocks):
    return sum(block.astype(F32) for block in blocks)


def body(tokens, norm_gain, qkv_weight, rate_weight, rate_base, fast_first, fast_second, inner_gain, out_weight):
    seq_count = lax.axis_size("seq")
    layers, heads = rate_base.shape
    pairs = heads // 2
    me = lax.axis_index("head")
    batch = jnp.arange(len(SLOTS))
    offset = (batch // 2 - me // 2) % 4 * 2 + (batch + me) % 2
    table = jnp.array([SLOTS.index((dx, dz)) for dx in range(4) for dz in range(2)])
    where = jnp.concatenate([lax.axis_index("seq").reshape(1), table[offset]]).astype(jnp.int32)

    def turned(weights):
        return weights.reshape(layers, pairs, 128, 256).swapaxes(2, 3)

    initial = jnp.stack([turned(fast_first), turned(fast_second)], axis=1)
    gains = jnp.repeat(inner_gain.reshape(layers, pairs, 2, 64).swapaxes(2, 3), MB, axis=3)
    base = (rate_base * (1.0 / MB))[:, :, None]
    stream = tokens.astype(F32)
    for layer in range(layers):
        mean_square = jnp.mean(stream * stream, axis=-1, keepdims=True)
        normed = (stream * lax.rsqrt(mean_square + 1e-06) * norm_gain[layer]).astype(B16)
        near = gather_near(normed)
        far = gather_far(near)
        parts = [project(blocks, layer, qkv_weight, rate_weight, base) for blocks in (near, far)]
        qkv, rate = zip(*parts)
        mixed = None
        states = [initial[layer][:, list(group)] for group in GROUPS]
        for turn in range(seq_count):
            for i, group in enumerate(GROUPS):
                mixed, state = run_chain(turn, group[0], where, qkv, rate, gains[layer], states[i], mixed)
                if turn < seq_count - 1:
                    states[i] = lax.ppermute(state, "seq", [(turn, turn + 1)])
        part_far = unproject(mixed, len(NEAR), len(FAR), layer, out_weight)
        part = unproject(mixed, 0, len(NEAR), layer, out_weight)
        a, b, c = send(part_far[0], 1, 0), send(part_far[1], 3, 0), send(part_far[2], 0, 1)
        side = add(part[1], a, b).astype(B16)
        across = add(part[4], c).astype(B16)
        side, across, left, right = lax.optimization_barrier((side, across, part[2], part[3]))
        sums = [part[0], send(left, 1, 0), send(right, 3, 0), send(across, 2, 0), send(side, 0, 1)]
        out = (stream + add(*sums)).astype(B16)
        stream = out.astype(F32)
    return out


GROUPS = [(0, 1, 2)]


def solution(mesh):
    rows = P(("dp", "seq", "head"), None)
    in_specs = (
        rows,
        P(),
        P(None, None, "head"),
        P(None, None, "head"),
        P(None, "head"),
        P(None, "head", None, None),
        P(None, "head", None, None),
        P(None, "head", None),
        P(None, "head", None),
    )
    return jax.shard_map(body, mesh=mesh, in_specs=in_specs, out_specs=rows, check_vma=False)
```

```python
import functools

import jax
import jax.numpy as jnp
from jax import lax
from jax.experimental import pallas as pl
from jax.experimental.pallas import tpu as pltpu
from jax.sharding import PartitionSpec as P

F32 = jnp.float32
B16 = jnp.bfloat16
MB = 64
GELU_A = 0.7978845608028654
GELU_B = 0.044715
NN = (((1,), (0,)), ((), ()))
NT = (((1,), (1,)), ((), ()))


def dot(left, right, dims=NN):
    return lax.dot_general(left, right, dims, preferred_element_type=F32)


def first_half(shape):
    return lax.broadcasted_iota(jnp.int32, shape, len(shape) - 1) < 64


def spread(x):
    mask = first_half(x.shape)
    zero = jnp.zeros_like(x)
    return jnp.concatenate([jnp.where(mask, x, zero), jnp.where(mask, zero, x)], axis=0)


def flip(x):
    y = spread(x).T
    return y[:64] + y[64:]


def fold(y):
    return jnp.where(first_half((64, 128)), y[:64], y[64:])


def mean0(x):
    return jnp.sum(x, axis=0, keepdims=True) * (1.0 / 64)


def normalise(y):
    centre = y - mean0(y)
    scale = lax.rsqrt(mean0(centre * centre) + 1e-5)
    return centre * scale, scale


def gelu_parts(h):
    square = h * h
    t = jnp.tanh(h * (GELU_A + (GELU_A * GELU_B) * square))
    half = 0.5 * h
    return square, t, half, half + half * t


def chain_steps(pairs, batches, where, qkv, rate, gain, w1, w2, out, rows, target):
    def block(b):
        return pl.ds(pl.multiple_of(where[b + 1] * MB, MB), MB)

    def rates(b, p):
        slot = rate[where[b + 1]]
        return jnp.concatenate([slot[2 * p : 2 * p + 1], slot[2 * p + 1 : 2 * p + 2]], axis=1)

    def tiles(b, p):
        return [qkv[block(b), p * 384 + j * 128 : p * 384 + (j + 1) * 128] for j in range(3)]

    def queries(b, p):
        t0, t1, _ = tiles(b, p)
        return jnp.where(first_half(t0.shape), t0, t1)

    def prepare_keys(b):
        for p in range(pairs):
            t0, t1, t2 = tiles(b, p)
            mask = first_half(t0.shape)
            keys = pltpu.roll(jnp.where(mask, t2, t0), 64, 1)
            values = jnp.where(mask, t1, t2)
            rows[p, 0:128] = spread(keys).astype(B16)
            target[p] = flip(values - keys)

    def prepare_queries(b):
        for p in range(pairs):
            rows[p, 128:256] = spread(queries(b, p)).astype(B16)

    def put(b, p, y):
        result = queries(b, p) + flip(normalise(y)[0] * gain[p])
        out[block(b), p * 128 : (p + 1) * 128] = result.astype(B16)

    prepare_keys(0)
    rows[:, 128:256] = jnp.zeros((pairs, 128, 128), B16)

    def step(b, carry):
        first = [w1[p].astype(B16) for p in range(pairs)]
        second = [w2[p].astype(B16) for p in range(pairs)]
        hidden = [dot(first[p], rows[p], NT) for p in range(pairs)]
        act, slope, act_q = [], [], []
        for p in range(pairs):
            square, t, half, a = gelu_parts(hidden[p][:, :128])
            slope.append(0.5 + 0.5 * t + half * (1.0 - t * t) * (GELU_A + (3 * GELU_A * GELU_B) * square))
            act.append(a.astype(B16))
        for p in range(pairs):
            act_q.append(gelu_parts(hidden[p][:, 128:])[3].astype(B16))
        result, result_q = [], []
        for p in range(pairs):
            turned = second[p].T
            result.append(fold(dot(turned, act[p])))
            result_q.append(fold(dot(turned, act_q[p])))
        cotangent = []
        for p in range(pairs):
            y, scale = normalise(result[p])
            dy = (y * gain[p] - target[p]) * rates(b, p) * gain[p]
            dy = scale * (dy - mean0(dy) - y * mean0(dy * y))
            cotangent.append(spread(dy).astype(B16))
        for p in range(pairs):
            down = (dot(second[p], cotangent[p]) * slope[p]).astype(B16)
            w1[p] = w1[p] - dot(down, rows[p, 0:128])
            w2[p] = w2[p] - dot(act[p], cotangent[p], NT)
        for p in range(pairs):
            put(jnp.maximum(b - 1, 0), p, result_q[p])
        prepare_keys(jnp.minimum(b + 1, batches - 1))
        prepare_queries(b)
        return carry

    lax.fori_loop(0, batches, step, 0)
    for p in range(pairs):
        hidden = dot(w1[p].astype(B16), rows[p, 128:256], NT)
        a = gelu_parts(hidden)[3].astype(B16)
        put(batches - 1, p, fold(dot(w2[p].astype(B16).T, a)))


def chain_kernel(pairs, first_pair, batches, turn, where, qkv_a, qkv_b, rate_a, rate_b, gain, state, *refs):
    out, state_out, qkv_v, rate_v, gain_v, state_v, final, out_v, w1, w2, rows, target, sems = refs[-13:]
    columns = pl.ds(first_pair * 384, pairs * 384)
    near, far = qkv_a.shape[0], qkv_b.shape[0]

    @pl.when(where[0] == turn)
    def _():
        moves = [
            (qkv_a.at[:, columns], qkv_v.at[pl.ds(0, near)]),
            (qkv_b.at[:, columns], qkv_v.at[pl.ds(near, far)]),
            (rate_a, rate_v.at[pl.ds(0, near // MB)]),
            (rate_b, rate_v.at[pl.ds(near // MB, far // MB)]),
            (gain.at[pl.ds(first_pair, pairs)], gain_v),
            (state, state_v),
        ]
        moves = [pltpu.make_async_copy(a, b, sems.at[i]) for i, (a, b) in enumerate(moves)]
        for move in moves:
            move.start()
        for move in moves:
            move.wait()
        w1[...] = state_v[0].astype(F32)
        w2[...] = state_v[1].astype(F32)
        chain_steps(pairs, batches, where, qkv_v, rate_v.at[:, pl.ds(2 * first_pair, 2 * pairs)], gain_v, w1, w2, out_v, rows, target)
        final[0] = w1[...].astype(B16)
        final[1] = w2[...].astype(B16)
        back = [
            pltpu.make_async_copy(final, state_out, sems.at[0]),
            pltpu.make_async_copy(out_v, out.at[:, pl.ds(first_pair * 128, pairs * 128)], sems.at[1]),
        ]
        for move in back:
            move.start()
        for move in back:
            move.wait()


ANYWHERE = pl.BlockSpec(memory_space=pl.ANY)


def run_chain(turn, first_pair, where, qkv, rate, gain, state, out):
    tokens = sum(part.shape[0] for part in qkv)
    heads = rate[0].shape[1]
    pairs = state.shape[1]
    batches = tokens // MB
    operands = [where, *qkv, *rate, gain, state] + ([] if out is None else [out])
    return pl.pallas_call(
        functools.partial(chain_kernel, pairs, first_pair, batches, turn),
        out_shape=[
            jax.ShapeDtypeStruct((tokens, heads * 64), B16),
            jax.ShapeDtypeStruct(state.shape, B16),
        ],
        in_specs=[pl.BlockSpec(memory_space=pltpu.SMEM)] + [ANYWHERE] * (len(operands) - 1),
        out_specs=[ANYWHERE, ANYWHERE],
        scratch_shapes=[
            pltpu.VMEM((tokens, pairs * 384), F32),
            pltpu.VMEM((batches, heads, MB), F32),
            pltpu.VMEM((pairs,) + gain.shape[1:], F32),
            pltpu.VMEM(state.shape, state.dtype),
            pltpu.VMEM(state.shape, B16),
            pltpu.VMEM((tokens, pairs * 128), B16),
            pltpu.VMEM(state.shape[1:], F32),
            pltpu.VMEM(state.shape[1:], F32),
            pltpu.VMEM((pairs, 256, 128), B16),
            pltpu.VMEM((pairs, 64, 128), F32),
            pltpu.SemaphoreType.DMA((6,)),
        ],
        input_output_aliases={} if out is None else {7: 0},
        compiler_params=pltpu.CompilerParams(vmem_limit_bytes=16 << 20),
        cost_estimate=pl.CostEstimate(flops=10**9, bytes_accessed=30 * 10**6, transcendentals=0),
        name=f"chain_{turn}",
    )(*operands)


def project_kernel(count, layer, *refs):
    blocks = refs[:count]
    weights, rate_weight, base, out, rate, rows, weight, row_sems, sems = refs[count:]
    chunks = sems.shape[0]
    depth = weight.shape[0] // chunks
    loads = [pltpu.make_async_copy(b, rows.at[pl.ds(i * MB, MB)], row_sems.at[i]) for i, b in enumerate(blocks)]
    moves = []
    for i in range(chunks):
        part = pl.ds(i * depth, depth)
        moves.append(pltpu.make_async_copy(weights.at[layer, part], weight.at[part], sems.at[i]))
    for move in loads + moves:
        move.start()
    for move in loads:
        move.wait()
    gate = base[0] * jax.nn.sigmoid(dot(rows[...], rate_weight[0]).T)
    for i in range(count):
        rate[i] = gate[:, i * MB : (i + 1) * MB]
    for i, move in enumerate(moves):
        move.wait()
        part = slice(i * depth, (i + 1) * depth)
        piece = dot(rows[:, part], weight[part])
        out[...] = piece if i == 0 else out[...] + piece


def project(blocks, layer, qkv_weight, rate_weight, base):
    count = len(blocks)
    depth, columns = qkv_weight.shape[1:]
    heads = rate_weight.shape[2]
    chunks = 4
    return pl.pallas_call(
        functools.partial(project_kernel, count, layer),
        grid=(1,),
        out_shape=[
            jax.ShapeDtypeStruct((count * MB, columns), F32),
            jax.ShapeDtypeStruct((count, heads, MB), F32),
        ],
        in_specs=[ANYWHERE] * (count + 1)
        + [
            pl.BlockSpec((1, depth, heads), lambda i: (layer, 0, 0)),
            pl.BlockSpec((1, heads, 1), lambda i: (layer, 0, 0)),
        ],
        out_specs=[
            pl.BlockSpec((count * MB, columns), lambda i: (0, 0)),
            pl.BlockSpec((count, heads, MB), lambda i: (0, 0, 0)),
        ],
        scratch_shapes=[
            pltpu.VMEM((count * MB, depth), B16),
            pltpu.VMEM((depth, columns), B16),
            pltpu.SemaphoreType.DMA((count,)),
            pltpu.SemaphoreType.DMA((chunks,)),
        ],
        compiler_params=pltpu.CompilerParams(vmem_limit_bytes=51 << 20),
        cost_estimate=pl.CostEstimate(flops=2 * count * MB * depth * columns, bytes_accessed=depth * columns * 2, transcendentals=0),
        name="project",
    )(*blocks, qkv_weight, rate_weight, base)


def unproject_kernel(first, count, layer, left, weights, *refs):
    outs, weight, sems = refs[:count], refs[count], refs[count + 1]
    chunks = sems.shape[0]
    width = weight.shape[1] // chunks
    parts = [pl.ds(i * width, width) for i in range(chunks)]
    moves = [pltpu.make_async_copy(weights.at[layer, :, part], weight.at[:, part], sems.at[i]) for i, part in enumerate(parts)]
    for move in moves:
        move.start()
    rows = left[first * MB : (first + count) * MB]
    for part, move in zip(parts, moves):
        move.wait()
        total = dot(rows, weight[:, part]).astype(B16)
        for i in range(count):
            outs[i][:, part] = total[i * MB : (i + 1) * MB]


def unproject(mixed, first, count, layer, out_weight):
    depth, columns = out_weight.shape[1:]
    whole = pl.BlockSpec(memory_space=pltpu.VMEM)
    return pl.pallas_call(
        functools.partial(unproject_kernel, first, count, layer),
        out_shape=[jax.ShapeDtypeStruct((MB, columns), B16)] * count,
        in_specs=[whole, ANYWHERE],
        out_specs=[whole] * count,
        scratch_shapes=[pltpu.VMEM((depth, columns), B16), pltpu.SemaphoreType.DMA((3,))],
        compiler_params=pltpu.CompilerParams(vmem_limit_bytes=58 << 20),
        cost_estimate=pl.CostEstimate(flops=2 * count * MB * depth * columns, bytes_accessed=depth * columns * 2, transcendentals=0),
        name="unproject",
    )(mixed, out_weight)


NEAR = [(0, 0), (0, 1), (1, 0), (3, 0), (2, 0)]
FAR = [(1, 1), (3, 1), (2, 1)]
SLOTS = NEAR + FAR


def send(block, dx, dz):
    route = [(2 * x + z, 2 * ((x + dx) % 4) + (z ^ dz)) for x in range(4) for z in range(2)]
    return lax.ppermute(block, "head", route)


def fetch(block, dx, dz):
    return send(block, -dx, dz)


def gather_near(own):
    return [own] + [fetch(own, dx, dz) for dx, dz in NEAR[1:]]


def gather_far(near):
    return [fetch(near[1], 1, 0), fetch(near[1], 3, 0), fetch(near[4], 0, 1)]


def add(*blocks):
    return sum(block.astype(F32) for block in blocks)


def body(tokens, norm_gain, qkv_weight, rate_weight, rate_base, fast_first, fast_second, inner_gain, out_weight):
    seq_count = lax.axis_size("seq")
    layers, heads = rate_base.shape
    pairs = heads // 2
    me = lax.axis_index("head")
    batch = jnp.arange(len(SLOTS))
    offset = (batch // 2 - me // 2) % 4 * 2 + (batch + me) % 2
    table = jnp.array([SLOTS.index((dx, dz)) for dx in range(4) for dz in range(2)])
    where = jnp.concatenate([lax.axis_index("seq").reshape(1), table[offset]]).astype(jnp.int32)

    def turned(weights):
        return weights.reshape(layers, pairs, 128, 256).swapaxes(2, 3)

    initial = jnp.stack([turned(fast_first), turned(fast_second)], axis=1)
    gains = jnp.repeat(inner_gain.reshape(layers, pairs, 2, 64).swapaxes(2, 3), MB, axis=3)
    base = (rate_base * (1.0 / MB))[:, :, None]
    stream = tokens.astype(F32)
    for layer in range(layers):
        mean_square = jnp.mean(stream * stream, axis=-1, keepdims=True)
        normed = (stream * lax.rsqrt(mean_square + 1e-06) * norm_gain[layer]).astype(B16)
        near = gather_near(normed)
        far = gather_far(near)
        parts = [project(blocks, layer, qkv_weight, rate_weight, base) for blocks in (near, far)]
        qkv, rate = zip(*parts)
        mixed = None
        states = [initial[layer][:, list(group)] for group in GROUPS]
        for turn in range(seq_count):
            for i, group in enumerate(GROUPS):
                mixed, state = run_chain(turn, group[0], where, qkv, rate, gains[layer], states[i], mixed)
                if turn < seq_count - 1:
                    states[i] = lax.ppermute(state, "seq", [(turn, turn + 1)])
        part_far = unproject(mixed, len(NEAR), len(FAR), layer, out_weight)
        part = unproject(mixed, 0, len(NEAR), layer, out_weight)
        a, b, c = send(part_far[0], 1, 0), send(part_far[1], 3, 0), send(part_far[2], 0, 1)
        side = add(part[1], a, b).astype(B16)
        across = add(part[4], c).astype(B16)
        side, across, left, right = lax.optimization_barrier((side, across, part[2], part[3]))
        sums = [part[0], send(left, 1, 0), send(right, 3, 0), send(across, 2, 0), send(side, 0, 1)]
        out = (stream + add(*sums)).astype(B16)
        stream = out.astype(F32)
    return out


GROUPS = [(0, 1, 2)]


def solution(mesh):
    rows = P(("dp", "seq", "head"), None)
    in_specs = (
        rows,
        P(),
        P(None, None, "head"),
        P(None, None, "head"),
        P(None, "head"),
        P(None, "head", None, None),
        P(None, "head", None, None),
        P(None, "head", None),
        P(None, "head", None),
    )
    return jax.shard_map(body, mesh=mesh, in_specs=in_specs, out_specs=rows, check_vma=False)
```

```python
import functools

import jax
import jax.numpy as jnp
from jax import lax
from jax.experimental import pallas as pl
from jax.experimental.pallas import tpu as pltpu
from jax.sharding import PartitionSpec as P

F32 = jnp.float32
B16 = jnp.bfloat16
MB = 64
GELU_A = 0.7978845608028654
GELU_B = 0.044715
NN = (((1,), (0,)), ((), ()))
NT = (((1,), (1,)), ((), ()))


def dot(left, right, dims=NN):
    return lax.dot_general(left, right, dims, preferred_element_type=F32)


def first_half(shape):
    return lax.broadcasted_iota(jnp.int32, shape, len(shape) - 1) < 64


def spread(x):
    mask = first_half(x.shape)
    zero = jnp.zeros_like(x)
    return jnp.concatenate([jnp.where(mask, x, zero), jnp.where(mask, zero, x)], axis=0)


def flip(x):
    y = spread(x).T
    return y[:64] + y[64:]


def fold(y):
    return jnp.where(first_half((64, 128)), y[:64], y[64:])


def mean0(x):
    return jnp.sum(x, axis=0, keepdims=True) * (1.0 / 64)


def normalise(y):
    centre = y - mean0(y)
    scale = lax.rsqrt(mean0(centre * centre) + 1e-5)
    return centre * scale, scale


def gelu_parts(h):
    square = h * h
    t = jnp.tanh(h * (GELU_A + (GELU_A * GELU_B) * square))
    half = 0.5 * h
    return square, t, half, half + half * t


def chain_steps(batches, slot_of, qkv, rate, gain, w1, w2, out, rows, target):
    def block(b):
        return pl.ds(pl.multiple_of(slot_of(b) * MB, MB), MB)

    def tiles(b):
        return [qkv[block(b), j * 128 : (j + 1) * 128].astype(F32) for j in range(3)]

    def queries(b):
        t0, t1, _ = tiles(b)
        return jnp.where(first_half(t0.shape), t0, t1)

    def prepare_keys(b):
        t0, t1, t2 = tiles(b)
        mask = first_half(t0.shape)
        keys = pltpu.roll(jnp.where(mask, t2, t0), 64, 1)
        values = jnp.where(mask, t1, t2)
        rows[0:128] = spread(keys).astype(B16)
        target[...] = flip(values - keys)

    def prepare_queries(b):
        rows[128:256] = spread(queries(b)).astype(B16)

    def put(b, y):
        out[block(b)] = (queries(b) + flip(normalise(y)[0] * gain[...])).astype(B16)

    prepare_keys(0)
    rows[128:256] = jnp.zeros((128, 128), B16)

    def step(b, carry):
        second = w2[...].astype(B16)
        hidden = dot(w1[...].astype(B16), rows[...], NT)
        square, t, half, a = gelu_parts(hidden[:, :128])
        act = a.astype(B16)
        turned = second.T
        result = fold(dot(turned, act))
        slope = 0.5 + 0.5 * t + half * (1.0 - t * t) * (GELU_A + (3 * GELU_A * GELU_B) * square)
        act_q = gelu_parts(hidden[:, 128:])[3].astype(B16)
        result_q = fold(dot(turned, act_q))
        y, scale = normalise(result)
        gates = rate[slot_of(b)]
        gates = jnp.concatenate([gates[0:1], gates[1:2]], axis=1)
        dy = (y * gain[...] - target[...]) * gates * gain[...]
        dy = scale * (dy - mean0(dy) - y * mean0(dy * y))
        cotangent = spread(dy).astype(B16)
        down = (dot(second, cotangent) * slope).astype(B16)
        w1[...] = w1[...] - dot(down, rows[0:128])
        w2[...] = w2[...] - dot(act, cotangent, NT)
        put(jnp.maximum(b - 1, 0), result_q)
        prepare_keys(jnp.minimum(b + 1, batches - 1))
        prepare_queries(b)
        return carry

    lax.fori_loop(0, batches, step, 0)
    hidden = dot(w1[...].astype(B16), rows[128:256], NT)
    a = gelu_parts(hidden)[3].astype(B16)
    put(batches - 1, fold(dot(w2[...].astype(B16).T, a)))


SLOT_DIGITS = 0x63745210
LAG = 2


def chain_kernel(pairs, batches, layer, turn, where, qkv_a, qkv_b, rate_a, rate_b, gains, first, second, *refs):
    out, state_out, qkv_v, rate_v, gain_v, init_v, state_v, out_v, gain, w1, w2, rows, target, sems = refs[-14:]
    near, far = qkv_a.shape[0], qkv_b.shape[0]
    place, me = where[0], where[1]
    pair = turn - LAG * place

    def slot_of(b):
        digit = 2 * ((b // 2 - me // 2) & 3) + ((b ^ me) & 1)
        return (SLOT_DIGITS >> (4 * digit)) & 7

    def fetch(moves):
        copies = [pltpu.make_async_copy(a, b, sems.at[i]) for i, (a, b) in enumerate(moves)]
        for copy in copies:
            copy.start()
        for copy in copies:
            copy.wait()

    @pl.when((pair >= 0) & (pair < pairs))
    def _():
        columns = pl.ds(pl.multiple_of(pair * 384, 384), 384)
        fetch(
            [
                (qkv_a.at[:, columns], qkv_v.at[pl.ds(0, near)]),
                (qkv_b.at[:, columns], qkv_v.at[pl.ds(near, far)]),
                (rate_a.at[:, pair], rate_v.at[pl.ds(0, near // MB)]),
                (rate_b.at[:, pair], rate_v.at[pl.ds(near // MB, far // MB)]),
                (gains.at[layer, pair], gain_v),
            ]
        )
        if turn < pairs:

            @pl.when(place == 0)
            def _():
                heads = pl.ds(2 * pair, 2)
                fetch([(first.at[layer, heads], init_v.at[0]), (second.at[layer, heads], init_v.at[1])])
                w1[...] = init_v[0].reshape(128, 256).T
                w2[...] = init_v[1].reshape(128, 256).T

        if turn >= LAG:

            @pl.when(place > 0)
            def _():
                fetch([(refs[0], state_v)])
                w1[...] = state_v[0].astype(F32)
                w2[...] = state_v[1].astype(F32)

        row = jnp.concatenate([gain_v[0:1], gain_v[1:2]], axis=1)
        gain[...] = flip(jnp.broadcast_to(row, (64, 128)))
        chain_steps(batches, slot_of, qkv_v, rate_v, gain, w1, w2, out_v, rows, target)
        state_v[0] = w1[...].astype(B16)
        state_v[1] = w2[...].astype(B16)
        place_out = pl.ds(pl.multiple_of(pair * 128, 128), 128)
        fetch([(state_v, state_out), (out_v, out.at[:, place_out])])


ANYWHERE = pl.BlockSpec(memory_space=pl.ANY)


def run_chain(turn, layer, where, qkv, rate, gains, first, second, state, out):
    tokens = sum(part.shape[0] for part in qkv)
    pairs = gains.shape[1]
    batches = tokens // MB
    shape = (2, 256, 128)
    operands = [where, *qkv, *rate, gains, first, second]
    operands += [] if state is None else [state]
    aliases = {}
    if out is not None:
        aliases = {len(operands): 0}
        operands += [out]
    return pl.pallas_call(
        functools.partial(chain_kernel, pairs, batches, layer, turn),
        out_shape=[
            jax.ShapeDtypeStruct((tokens, pairs * 128), B16),
            jax.ShapeDtypeStruct(shape, B16),
        ],
        in_specs=[pl.BlockSpec(memory_space=pltpu.SMEM)] + [ANYWHERE] * (len(operands) - 1),
        out_specs=[ANYWHERE, ANYWHERE],
        scratch_shapes=[
            pltpu.VMEM((tokens, 384), B16),
            pltpu.VMEM((batches, 2, MB), F32),
            pltpu.VMEM((2, MB), F32),
            pltpu.VMEM((2, 2, 64, 256), F32),
            pltpu.VMEM(shape, B16),
            pltpu.VMEM((tokens, 128), B16),
            pltpu.VMEM((64, 128), F32),
            pltpu.VMEM(shape[1:], F32),
            pltpu.VMEM(shape[1:], F32),
            pltpu.VMEM((256, 128), B16),
            pltpu.VMEM((64, 128), F32),
            pltpu.SemaphoreType.DMA((5,)),
        ],
        input_output_aliases=aliases,
        compiler_params=pltpu.CompilerParams(vmem_limit_bytes=16 << 20),
        cost_estimate=pl.CostEstimate(flops=6 * 10**9, bytes_accessed=10**6, transcendentals=0),
        name=f"chain_{turn}",
    )(*operands)


def settle_kernel(stream, gain, *refs):
    *parts, out, normed = refs
    total = stream[...].astype(F32)
    if parts:
        total = total + sum(part[...].astype(F32) for part in parts)
        out[...] = total.astype(B16)
        total = out[...].astype(F32)
    mean_square = jnp.mean(total * total, axis=-1, keepdims=True)
    normed[...] = (total * lax.rsqrt(mean_square + 1e-06) * gain[...]).astype(B16)


def settle(stream, gain, parts):
    whole = pl.BlockSpec(memory_space=pltpu.VMEM)
    return pl.pallas_call(
        settle_kernel,
        out_shape=[jax.ShapeDtypeStruct(stream.shape, B16)] * 2,
        in_specs=[whole] * (2 + len(parts)),
        out_specs=[whole] * 2,
        compiler_params=pltpu.CompilerParams(vmem_limit_bytes=32 << 20),
        name="settle",
    )(stream, gain, *parts)


def project_kernel(count, layer, *refs):
    blocks = refs[:count]
    weights, rate_weight, base, out, rate, rows, weight, total, row_sems, sems = refs[count:]
    chunks = sems.shape[0]
    depth = weight.shape[0] // chunks
    loads = [pltpu.make_async_copy(b, rows.at[pl.ds(i * MB, MB)], row_sems.at[i]) for i, b in enumerate(blocks)]
    moves = []
    for i in range(chunks):
        part = pl.ds(i * depth, depth)
        moves.append(pltpu.make_async_copy(weights.at[layer, part], weight.at[part], sems.at[i]))
    for move in loads + moves:
        move.start()
    for move in loads:
        move.wait()
    gate = base[0] * jax.nn.sigmoid(dot(rows[...], rate_weight[0]).T)
    for i in range(count):
        for p in range(gate.shape[0] // 2):
            rate[i, p] = gate[2 * p : 2 * p + 2, i * MB : (i + 1) * MB]
    for i, move in enumerate(moves):
        move.wait()
        part = slice(i * depth, (i + 1) * depth)
        piece = dot(rows[:, part], weight[part])
        if i == chunks - 1:
            out[...] = (total[...] + piece).astype(B16)
        else:
            total[...] = piece if i == 0 else total[...] + piece


def project(blocks, layer, qkv_weight, rate_weight, base):
    count = len(blocks)
    depth, columns = qkv_weight.shape[1:]
    heads = rate_weight.shape[2]
    chunks = 4
    return pl.pallas_call(
        functools.partial(project_kernel, count, layer),
        grid=(1,),
        out_shape=[
            jax.ShapeDtypeStruct((count * MB, columns), B16),
            jax.ShapeDtypeStruct((count, heads // 2, 2, MB), F32),
        ],
        in_specs=[ANYWHERE] * (count + 1)
        + [
            pl.BlockSpec((1, depth, heads), lambda i: (layer, 0, 0)),
            pl.BlockSpec((1, heads, 1), lambda i: (layer, 0, 0)),
        ],
        out_specs=[
            pl.BlockSpec((count * MB, columns), lambda i: (0, 0)),
            pl.BlockSpec((count, heads // 2, 2, MB), lambda i: (0, 0, 0, 0)),
        ],
        scratch_shapes=[
            pltpu.VMEM((count * MB, depth), B16),
            pltpu.VMEM((depth, columns), B16),
            pltpu.VMEM((count * MB, columns), F32),
            pltpu.SemaphoreType.DMA((count,)),
            pltpu.SemaphoreType.DMA((chunks,)),
        ],
        compiler_params=pltpu.CompilerParams(vmem_limit_bytes=51 << 20),
        cost_estimate=pl.CostEstimate(flops=2 * count * MB * depth * columns, bytes_accessed=depth * columns * 2, transcendentals=0),
        name="project",
    )(*blocks, qkv_weight, rate_weight, base)


def unproject_kernel(first, count, layer, left, weights, *refs):
    outs, weight, sems = refs[:count], refs[count], refs[count + 1]
    chunks = sems.shape[0]
    width = weight.shape[1] // chunks
    parts = [pl.ds(i * width, width) for i in range(chunks)]
    moves = [pltpu.make_async_copy(weights.at[layer, :, part], weight.at[:, part], sems.at[i]) for i, part in enumerate(parts)]
    for move in moves:
        move.start()
    rows = left[first * MB : (first + count) * MB]
    for part, move in zip(parts, moves):
        move.wait()
        total = dot(rows, weight[:, part]).astype(B16)
        for i in range(count):
            outs[i][:, part] = total[i * MB : (i + 1) * MB]


def unproject(mixed, first, count, layer, out_weight):
    depth, columns = out_weight.shape[1:]
    whole = pl.BlockSpec(memory_space=pltpu.VMEM)
    return pl.pallas_call(
        functools.partial(unproject_kernel, first, count, layer),
        out_shape=[jax.ShapeDtypeStruct((MB, columns), B16)] * count,
        in_specs=[whole, ANYWHERE],
        out_specs=[whole] * count,
        scratch_shapes=[pltpu.VMEM((depth, columns), B16), pltpu.SemaphoreType.DMA((3,))],
        compiler_params=pltpu.CompilerParams(vmem_limit_bytes=58 << 20),
        cost_estimate=pl.CostEstimate(flops=2 * count * MB * depth * columns, bytes_accessed=depth * columns * 2, transcendentals=0),
        name="unproject",
    )(mixed, out_weight)


NEAR = [(0, 0), (0, 1), (1, 0), (3, 0), (2, 0)]
FAR = [(1, 1), (3, 1), (2, 1)]
SLOTS = NEAR + FAR


def send(block, dx, dz):
    route = [(2 * x + z, 2 * ((x + dx) % 4) + (z ^ dz)) for x in range(4) for z in range(2)]
    return lax.ppermute(block, "head", route)


def fetch(block, dx, dz):
    return send(block, -dx, dz)


def gather_near(own):
    return [own] + [fetch(own, dx, dz) for dx, dz in NEAR[1:]]


def gather_far(near):
    return [fetch(near[1], 1, 0), fetch(near[1], 3, 0), fetch(near[4], 0, 1)]


def add(*blocks):
    return sum(block.astype(F32) for block in blocks)


def body(tokens, norm_gain, qkv_weight, rate_weight, rate_base, fast_first, fast_second, inner_gain, out_weight):
    seq_count = lax.axis_size("seq")
    layers, heads = rate_base.shape
    pairs = heads // 2
    where = jnp.stack([lax.axis_index("seq"), lax.axis_index("head")]).astype(jnp.int32)
    stream, normed = tokens, settle(tokens, norm_gain[:1], [])[1]
    for layer in range(layers):
        near = gather_near(normed)
        far = gather_far(near)
        if layer == 0:
            rate_weight, rate_base, inner_gain = lax.optimization_barrier((rate_weight, rate_base, inner_gain, near[4]))[:3]
            base = (rate_base * (1.0 / MB))[:, :, None]
            gains = inner_gain.reshape(layers, pairs, 2, 64)
        parts = [project(blocks, layer, qkv_weight, rate_weight, base) for blocks in (near, far)]
        qkv, rate = zip(*parts)
        mixed, sent = None, {}
        for turn in range(LAG * (seq_count - 1) + pairs):
            state = sent.get(turn - LAG)
            mixed, state = run_chain(turn, layer, where, qkv, rate, gains, fast_first, fast_second, state, mixed)
            route = [(row, row + 1) for row in range(seq_count - 1) if 0 <= turn - LAG * row < pairs]
            if route:
                sent[turn] = lax.ppermute(state, "seq", route)
        part_far = unproject(mixed, len(NEAR), len(FAR), layer, out_weight)
        part = unproject(mixed, 0, len(NEAR), layer, out_weight)
        a, b, c = send(part_far[0], 1, 0), send(part_far[1], 3, 0), send(part_far[2], 0, 1)
        side = add(part[1], a, b).astype(B16)
        across = add(part[4], c).astype(B16)
        side, across, left, right = lax.optimization_barrier((side, across, part[2], part[3]))
        sums = [part[0], send(left, 1, 0), send(right, 3, 0), send(across, 2, 0), send(side, 0, 1)]
        following = min(layer + 1, layers - 1)
        stream, normed = settle(stream, norm_gain[following : following + 1], sums)
    return stream


def solution(mesh):
    rows = P(("dp", "seq", "head"), None)
    in_specs = (
        rows,
        P(),
        P(None, None, "head"),
        P(None, None, "head"),
        P(None, "head"),
        P(None, "head", None, None),
        P(None, "head", None, None),
        P(None, "head", None),
        P(None, "head", None),
    )
    return jax.shard_map(body, mesh=mesh, in_specs=in_specs, out_specs=rows, check_vma=False)
```

```python
import functools

import jax
import jax.numpy as jnp
from jax import lax
from jax.experimental import pallas as pl
from jax.experimental.pallas import tpu as pltpu
from jax.sharding import PartitionSpec as P

F32 = jnp.float32
B16 = jnp.bfloat16
MB = 64
GELU_A = 0.7978845608028654
GELU_B = 0.044715
NN = (((1,), (0,)), ((), ()))
NT = (((1,), (1,)), ((), ()))


def dot(left, right, dims=NN):
    return lax.dot_general(left, right, dims, preferred_element_type=F32)


def first_half(shape):
    return lax.broadcasted_iota(jnp.int32, shape, len(shape) - 1) < 64


def spread(x):
    mask = first_half(x.shape)
    zero = jnp.zeros_like(x)
    return jnp.concatenate([jnp.where(mask, x, zero), jnp.where(mask, zero, x)], axis=0)


def flip(x):
    y = spread(x).T
    return y[:64] + y[64:]


def fold(y):
    return jnp.where(first_half((64, 128)), y[:64], y[64:])


def mean0(x):
    return jnp.sum(x, axis=0, keepdims=True) * (1.0 / 64)


def normalise(y):
    centre = y - mean0(y)
    scale = lax.rsqrt(mean0(centre * centre) + 1e-5)
    return centre * scale, scale


def gelu_parts(h):
    square = h * h
    t = jnp.tanh(h * (GELU_A + (GELU_A * GELU_B) * square))
    half = 0.5 * h
    return square, t, half, half + half * t


def chain_steps(pairs, batches, slot_of, qkv, rate, gain, w1, w2, out, rows, target):
    every = range(pairs)

    def block(b):
        return pl.ds(pl.multiple_of(slot_of(b) * MB, MB), MB)

    def tiles(b, p):
        return [qkv[block(b), p * 384 + j * 128 : p * 384 + (j + 1) * 128].astype(F32) for j in range(3)]

    def queries(b, p):
        t0, t1, _ = tiles(b, p)
        return jnp.where(first_half(t0.shape), t0, t1)

    def prepare_keys(b):
        for p in every:
            t0, t1, t2 = tiles(b, p)
            mask = first_half(t0.shape)
            keys = pltpu.roll(jnp.where(mask, t2, t0), 64, 1)
            values = jnp.where(mask, t1, t2)
            rows[p, 0:128] = spread(keys).astype(B16)
            target[p] = flip(values - keys)

    def prepare_queries(b):
        for p in every:
            rows[p, 128:256] = spread(queries(b, p)).astype(B16)

    def put(b, p, y):
        out[block(b), p * 128 : (p + 1) * 128] = (queries(b, p) + flip(normalise(y)[0] * gain[p])).astype(B16)

    def answer(b):
        for p in every:
            hidden = dot(w1[p].astype(B16), rows[p, 128:256], NT)
            act = gelu_parts(hidden)[3].astype(B16)
            put(b, p, fold(dot(w2[p].astype(B16).T, act)))

    for b in range(batches):
        prepare_keys(b)
        if b > 0:
            prepare_queries(b - 1)
        second = [w2[p].astype(B16) for p in every]
        wanted = slice(0, 256 if b > 0 else 128)
        hidden = [dot(w1[p].astype(B16), rows[p, wanted], NT) for p in every]
        parts = [gelu_parts(hidden[p][:, :128]) for p in every]
        act = [part[3].astype(B16) for part in parts]
        turned = [second[p].T for p in every]
        result = [fold(dot(turned[p], act[p])) for p in every]
        slope = [
            0.5 + 0.5 * t + half * (1.0 - t * t) * (GELU_A + (3 * GELU_A * GELU_B) * square) for square, t, half, _ in parts
        ]
        if b > 0:
            act_q = [gelu_parts(hidden[p][:, 128:])[3].astype(B16) for p in every]
            result_q = [fold(dot(turned[p], act_q[p])) for p in every]
        cotangent = []
        gates = rate[slot_of(b)]
        for p in every:
            y, scale = normalise(result[p])
            gate = jnp.concatenate([gates[2 * p : 2 * p + 1], gates[2 * p + 1 : 2 * p + 2]], axis=1)
            dy = (y * gain[p] - target[p]) * gate * gain[p]
            dy = scale * (dy - mean0(dy) - y * mean0(dy * y))
            cotangent.append(spread(dy).astype(B16))
        for p in every:
            down = (dot(second[p], cotangent[p]) * slope[p]).astype(B16)
            w1[p] = w1[p] - dot(down, rows[p, 0:128])
            w2[p] = w2[p] - dot(act[p], cotangent[p], NT)
        if b > 0:
            for p in every:
                put(b - 1, p, result_q[p])
    prepare_queries(batches - 1)
    answer(batches - 1)


SLOT_DIGITS = 0x63745210
GROUPS = [(0, 1), (1, 2)]


def chain_kernel(group, batches, layer, turn, where, qkv_a, qkv_b, rate_a, rate_b, gains, *refs):
    first_pair, pairs = group
    out, state_out, qkv_v, rate_v, start_v, state_v, out_v, gain, w1, w2, rows, target, sems = refs[-13:]
    near, far = qkv_a.shape[0], qkv_b.shape[0]
    me = where[1]

    def slot_of(b):
        digit = 2 * ((b // 2 - me // 2) & 3) + ((b ^ me) & 1)
        return (SLOT_DIGITS >> (4 * digit)) & 7

    def fetch(moves):
        copies = [pltpu.make_async_copy(a, b, sems.at[i]) for i, (a, b) in enumerate(moves)]
        for copy in copies:
            copy.start()
        for copy in copies:
            copy.wait()

    @pl.when(where[0] == turn)
    def _():
        columns = pl.ds(first_pair * 384, pairs * 384)
        heads = pl.ds(2 * first_pair, 2 * pairs)
        moves = [
            (qkv_a.at[:, columns], qkv_v.at[pl.ds(0, near)]),
            (qkv_b.at[:, columns], qkv_v.at[pl.ds(near, far)]),
            (rate_a, rate_v.at[pl.ds(0, near // MB)]),
            (rate_b, rate_v.at[pl.ds(near // MB, far // MB)]),
        ]
        if turn == 0:
            moves += [(refs[0].at[layer, heads], start_v.at[0]), (refs[1].at[layer, heads], start_v.at[1])]
        else:
            moves += [(refs[0], start_v)]
        fetch(moves)
        for p in range(pairs):
            if turn == 0:
                w1[p] = start_v[0, 2 * p : 2 * p + 2].reshape(128, 256).T
                w2[p] = start_v[1, 2 * p : 2 * p + 2].reshape(128, 256).T
            else:
                w1[p] = start_v[0, p].astype(F32)
                w2[p] = start_v[1, p].astype(F32)
            pair = first_pair + p
            row = jnp.concatenate([gains[2 * pair, layer : layer + 1], gains[2 * pair + 1, layer : layer + 1]], axis=1)
            gain[p] = flip(jnp.broadcast_to(row, (64, 128)))
        chain_steps(pairs, batches, slot_of, qkv_v, rate_v.at[:, heads], gain, w1, w2, out_v, rows, target)
        state_v[0] = w1[...].astype(B16)
        state_v[1] = w2[...].astype(B16)
        fetch([(state_v, state_out), (out_v, out.at[:, pl.ds(first_pair * 128, pairs * 128)])])


ANYWHERE = pl.BlockSpec(memory_space=pl.ANY)
WHOLE = pl.BlockSpec(memory_space=pltpu.VMEM)


def run_chain(turn, group, layer, where, qkv, rate, gains, state, out):
    tokens = sum(part.shape[0] for part in qkv)
    heads = rate[0].shape[1]
    pairs = group[1]
    batches = tokens // MB
    shape = (2, pairs, 256, 128)
    start = pltpu.VMEM((2, 2 * pairs, 64, 256), F32) if turn == 0 else pltpu.VMEM(shape, B16)
    operands = [where, *qkv, *rate, gains, *state]
    aliases = {}
    if out is not None:
        aliases = {len(operands): 0}
        operands += [out]
    return pl.pallas_call(
        functools.partial(chain_kernel, group, batches, layer, turn),
        out_shape=[
            jax.ShapeDtypeStruct((tokens, heads * 64), B16),
            jax.ShapeDtypeStruct(shape, B16),
        ],
        in_specs=[pl.BlockSpec(memory_space=pltpu.SMEM)] + [ANYWHERE] * 4 + [WHOLE] + [ANYWHERE] * (len(operands) - 6),
        out_specs=[ANYWHERE, ANYWHERE],
        scratch_shapes=[
            pltpu.VMEM((tokens, pairs * 384), B16),
            pltpu.VMEM((batches, heads, MB), F32),
            start,
            pltpu.VMEM(shape, B16),
            pltpu.VMEM((tokens, pairs * 128), B16),
            pltpu.VMEM((pairs, 64, 128), F32),
            pltpu.VMEM(shape[1:], F32),
            pltpu.VMEM(shape[1:], F32),
            pltpu.VMEM((pairs, 256, 128), B16),
            pltpu.VMEM((pairs, 64, 128), F32),
            pltpu.SemaphoreType.DMA((6,)),
        ],
        input_output_aliases=aliases,
        compiler_params=pltpu.CompilerParams(vmem_limit_bytes=16 << 20),
        cost_estimate=pl.CostEstimate(flops=6 * 10**9, bytes_accessed=10**6, transcendentals=0),
        name=f"chain_{turn}_{group[0]}",
    )(*operands)


def settle_kernel(layer, stream, gain, *refs):
    *parts, out, normed = refs
    total = stream[...].astype(F32)
    if parts:
        total = total + sum(part[...].astype(F32) for part in parts)
        out[...] = total.astype(B16)
        total = out[...].astype(F32)
    mean_square = jnp.mean(total * total, axis=-1, keepdims=True)
    normed[...] = (total * lax.rsqrt(mean_square + 1e-06) * gain[layer : layer + 1]).astype(B16)


def settle(stream, gain, layer, parts):
    return pl.pallas_call(
        functools.partial(settle_kernel, layer),
        out_shape=[jax.ShapeDtypeStruct(stream.shape, B16)] * 2,
        in_specs=[WHOLE] * (2 + len(parts)),
        out_specs=[WHOLE] * 2,
        compiler_params=pltpu.CompilerParams(vmem_limit_bytes=32 << 20),
        name="settle",
    )(stream, gain, *parts)


def project_kernel(count, layer, *refs):
    blocks = refs[:count]
    weights, rate_weight, base, out, rate, rows, sems = refs[count:]
    loads = [pltpu.make_async_copy(b, rows.at[pl.ds(i * MB, MB)], sems.at[i]) for i, b in enumerate(blocks)]
    for load in loads:
        load.start()
    for load in loads:
        load.wait()
    gate = jax.nn.sigmoid(dot(rows[...], rate_weight[:, layer], NT)) * (base[layer : layer + 1] * (1.0 / MB))
    gate = gate.T
    for i in range(count):
        rate[i] = gate[:, i * MB : (i + 1) * MB]
    out[...] = dot(rows[...], weights[layer]).astype(B16)


def project(blocks, layer, qkv_weight, rate_weight, base):
    count = len(blocks)
    depth, columns = qkv_weight.shape[1:]
    heads = rate_weight.shape[0]
    return pl.pallas_call(
        functools.partial(project_kernel, count, layer),
        out_shape=[
            jax.ShapeDtypeStruct((count * MB, columns), B16),
            jax.ShapeDtypeStruct((count, heads, MB), F32),
        ],
        in_specs=[ANYWHERE] * count + [WHOLE] * 3,
        out_specs=[WHOLE] * 2,
        scratch_shapes=[pltpu.VMEM((count * MB, depth), B16), pltpu.SemaphoreType.DMA((count,))],
        compiler_params=pltpu.CompilerParams(vmem_limit_bytes=16 << 20),
        cost_estimate=pl.CostEstimate(flops=2 * count * MB * depth * columns, bytes_accessed=10**6, transcendentals=0),
        name="project",
    )(*blocks, qkv_weight, rate_weight, base)


def unproject_kernel(first, count, layer, left, weights, *outs):
    total = dot(left[first * MB : (first + count) * MB], weights[layer]).astype(B16)
    for i in range(count):
        outs[i][...] = total[i * MB : (i + 1) * MB]


def unproject(mixed, first, count, layer, out_weight):
    depth, columns = out_weight.shape[1:]
    return pl.pallas_call(
        functools.partial(unproject_kernel, first, count, layer),
        out_shape=[jax.ShapeDtypeStruct((MB, columns), B16)] * count,
        in_specs=[WHOLE] * 2,
        out_specs=[WHOLE] * count,
        compiler_params=pltpu.CompilerParams(vmem_limit_bytes=16 << 20),
        cost_estimate=pl.CostEstimate(flops=2 * count * MB * depth * columns, bytes_accessed=10**6, transcendentals=0),
        name="unproject",
    )(mixed, out_weight)


NEAR = [(0, 0), (0, 1), (1, 0), (3, 0), (2, 0)]
FAR = [(1, 1), (3, 1), (2, 1)]
SLOTS = NEAR + FAR


def send(block, dx, dz):
    route = [(2 * x + z, 2 * ((x + dx) % 4) + (z ^ dz)) for x in range(4) for z in range(2)]
    return lax.ppermute(block, "head", route)


def fetch(block, dx, dz):
    return send(block, -dx, dz)


def gather_near(own):
    return [own] + [fetch(own, dx, dz) for dx, dz in NEAR[1:]]


def gather_far(near):
    return [fetch(near[1], 1, 0), fetch(near[1], 3, 0), fetch(near[4], 0, 1)]


def add(*blocks):
    return sum(block.astype(F32) for block in blocks)


def body(tokens, norm_gain, qkv_weight, rate_weight, rate_base, fast_first, fast_second, inner_gain, out_weight):
    seq_count = lax.axis_size("seq")
    layers, heads = rate_base.shape
    rate_weight = rate_weight.transpose(2, 0, 1)
    gains = inner_gain.transpose(1, 0, 2)
    stream, normed = tokens, settle(tokens, norm_gain, 0, [])[1]
    place, me = lax.axis_index("seq"), lax.axis_index("head")
    for layer in range(layers):
        near = gather_near(normed)
        far = gather_far(near)
        if layer == 0:
            place, me = lax.optimization_barrier((place, me, near[4]))[:2]
            where = jnp.stack([place, me]).astype(jnp.int32)
        parts = [project(blocks, layer, qkv_weight, rate_weight, rate_base) for blocks in (near, far)]
        qkv, rate = zip(*parts)
        mixed = None
        states = [(fast_first, fast_second) for _ in GROUPS]
        for turn in range(seq_count):
            for i, group in enumerate(GROUPS):
                mixed, state = run_chain(turn, group, layer, where, qkv, rate, gains, states[i], mixed)
                if turn < seq_count - 1:
                    states[i] = (lax.ppermute(state, "seq", [(turn, turn + 1)]),)
        part_far = unproject(mixed, len(NEAR), len(FAR), layer, out_weight)
        part = unproject(mixed, 0, len(NEAR), layer, out_weight)
        a, b, c = send(part_far[0], 1, 0), send(part_far[1], 3, 0), send(part_far[2], 0, 1)
        side = add(part[1], a, b).astype(B16)
        across = add(part[4], c).astype(B16)
        side, across, left, right = lax.optimization_barrier((side, across, part[2], part[3]))
        sums = [part[0], send(left, 1, 0), send(right, 3, 0), send(across, 2, 0), send(side, 0, 1)]
        stream, normed = settle(stream, norm_gain, min(layer + 1, layers - 1), sums)
    return stream


def solution(mesh):
    rows = P(("dp", "seq", "head"), None)
    in_specs = (
        rows,
        P(),
        P(None, None, "head"),
        P(None, None, "head"),
        P(None, "head"),
        P(None, "head", None, None),
        P(None, "head", None, None),
        P(None, "head", None),
        P(None, "head", None),
    )
    return jax.shard_map(body, mesh=mesh, in_specs=in_specs, out_specs=rows, check_vma=False)
```

```python
import functools

import jax
import jax.numpy as jnp
from jax import lax
from jax.experimental import pallas as pl
from jax.experimental.pallas import tpu as pltpu
from jax.sharding import PartitionSpec as P

F32 = jnp.float32
B16 = jnp.bfloat16
MB = 64
GELU_A = 0.7978845608028654
GELU_B = 0.044715
NN = (((1,), (0,)), ((), ()))
NT = (((1,), (1,)), ((), ()))


def dot(left, right, dims=NN):
    return lax.dot_general(left, right, dims, preferred_element_type=F32)


def first_half(shape):
    return lax.broadcasted_iota(jnp.int32, shape, len(shape) - 1) < 64


def spread(x):
    mask = first_half(x.shape)
    zero = jnp.zeros_like(x)
    return jnp.concatenate([jnp.where(mask, x, zero), jnp.where(mask, zero, x)], axis=0)


def flip(x):
    y = spread(x).T
    return y[:64] + y[64:]


def fold(y):
    return jnp.where(first_half((64, 128)), y[:64], y[64:])


def mean0(x):
    return jnp.sum(x, axis=0, keepdims=True) * (1.0 / 64)


def normalise(y):
    centre = y - mean0(y)
    scale = lax.rsqrt(mean0(centre * centre) + 1e-5)
    return centre * scale, scale


def gelu_parts(h):
    square = h * h
    t = jnp.tanh(h * (GELU_A + (GELU_A * GELU_B) * square))
    half = 0.5 * h
    return square, t, half, half + half * t


def chain_steps(batches, tiles, gates_of, put_out, gain, w1, w2, rows, base, down, mix, target):
    def queries(b):
        t0, t1, _ = tiles(b)
        return jnp.where(first_half(t0.shape), t0, t1)

    def keys_and_target(b):
        t0, t1, t2 = tiles(b)
        mask = first_half(t0.shape)
        keys = pltpu.roll(jnp.where(mask, t2, t0), 64, 1)
        return spread(keys).astype(B16), flip(jnp.where(mask, t1, t2) - keys)

    def put(b, y):
        put_out(b, (queries(b) + flip(normalise(y)[0] * gain)).astype(B16))

    def answer(b, first, turned):
        hidden = dot(first, spread(queries(b)).astype(B16), NT)
        act = gelu_parts(hidden)[3].astype(B16)
        put(b, fold(dot(turned, act)))

    keys, wanted = keys_and_target(0)
    rows[0] = keys
    target[...] = wanted
    base[...] = dot(w1[...].astype(B16), keys, NT)
    for b in range(batches):
        hidden = base[...]
        if b > 0:
            hidden = hidden - dot(down[...], mix[...])
        square, t, half, a = gelu_parts(hidden)
        act = a.astype(B16)
        second = w2[...].astype(B16)
        turned = second.T
        result = fold(dot(turned, act))
        slope = 0.5 + 0.5 * t + half * (1.0 - t * t) * (GELU_A + (3 * GELU_A * GELU_B) * square)
        first = w1[...]
        if b > 0:
            first = first - dot(down[...], rows[(b - 1) % 2])
            w1[...] = first
        first = first.astype(B16)
        if b < batches - 1:
            keys, wanted = keys_and_target(b + 1)
            next_base = dot(first, keys, NT)
            next_mix = dot(rows[b % 2], keys, NT).astype(B16)
        y, scale = normalise(result)
        dy = (y * gain - target[...]) * gates_of(b) * gain
        dy = scale * (dy - mean0(dy) - y * mean0(dy * y))
        cotangent = spread(dy).astype(B16)
        down[...] = (dot(second, cotangent) * slope).astype(B16)
        w2[...] = w2[...] - dot(act, cotangent, NT)
        if b > 0:
            answer(b - 1, first, turned)
        if b < batches - 1:
            rows[(b + 1) % 2] = keys
            target[...] = wanted
            base[...] = next_base
            mix[...] = next_mix
    w1[...] = w1[...] - dot(down[...], rows[(batches - 1) % 2])
    answer(batches - 1, w1[...].astype(B16), w2[...].astype(B16).T)


SLOT_DIGITS = 0x63745210
LAG = 2


def chain_kernel(pairs, batches, layer, turn, where, qkv, rate, gains, first, second, *refs):
    out, state_out, w1, w2, rows, base, down, mix, target = refs[-9:]
    place, me = where[0], where[1]
    pair = turn - LAG * place

    def slot_of(b):
        digit = 2 * ((b // 2 - me // 2) & 3) + ((b ^ me) & 1)
        return (SLOT_DIGITS >> (4 * digit)) & 7

    def block(b):
        return pl.ds(pl.multiple_of(slot_of(b) * MB, MB), MB)

    def lanes(width, j=0):
        return pl.ds(pl.multiple_of(pair * width + j * 128, 128), 128)

    def tiles(b):
        return [qkv[block(b), lanes(384, j)].astype(F32) for j in range(3)]

    def gates_of(b):
        gates = rate[slot_of(b), pair]
        return jnp.concatenate([gates[0:1], gates[1:2]], axis=1)

    def put_out(b, value):
        out[block(b), lanes(128)] = value

    @pl.when((pair >= 0) & (pair < pairs))
    def _():
        if turn < pairs:

            @pl.when(place == 0)
            def _():
                heads = pl.ds(2 * pair, 2)
                w1[...] = first[layer, heads].reshape(128, 256).T
                w2[...] = second[layer, heads].reshape(128, 256).T

        if turn >= LAG:

            @pl.when(place > 0)
            def _():
                w1[...] = refs[0][0].astype(F32)
                w2[...] = refs[0][1].astype(F32)

        row = jnp.concatenate([gains[2 * pair, layer : layer + 1], gains[2 * pair + 1, layer : layer + 1]], axis=1)
        gain = flip(jnp.broadcast_to(row, (64, 128)))
        chain_steps(batches, tiles, gates_of, put_out, gain, w1, w2, rows, base, down, mix, target)
        state_out[0] = w1[...].astype(B16)
        state_out[1] = w2[...].astype(B16)


ANYWHERE = pl.BlockSpec(memory_space=pl.ANY)
WHOLE = pl.BlockSpec(memory_space=pltpu.VMEM)


def run_chain(turn, layer, where, qkv, rate, gains, first, second, state, out):
    tokens = qkv.shape[0]
    pairs = rate.shape[1]
    shape = (2, 256, 128)
    operands = [where, qkv, rate, gains, first, second] + ([] if state is None else [state])
    aliases = {}
    if out is not None:
        aliases = {len(operands): 0}
        operands += [out]
    return pl.pallas_call(
        functools.partial(chain_kernel, pairs, tokens // MB, layer, turn),
        out_shape=[
            jax.ShapeDtypeStruct((tokens, pairs * 128), B16),
            jax.ShapeDtypeStruct(shape, B16),
        ],
        in_specs=[pl.BlockSpec(memory_space=pltpu.SMEM)] + [WHOLE] * (len(operands) - 1),
        out_specs=[WHOLE, WHOLE],
        scratch_shapes=[
            pltpu.VMEM(shape[1:], F32),
            pltpu.VMEM(shape[1:], F32),
            pltpu.VMEM((2, 128, 128), B16),
            pltpu.VMEM((256, 128), F32),
            pltpu.VMEM((256, 128), B16),
            pltpu.VMEM((128, 128), B16),
            pltpu.VMEM((64, 128), F32),
        ],
        input_output_aliases=aliases,
        compiler_params=pltpu.CompilerParams(vmem_limit_bytes=16 << 20),
        cost_estimate=pl.CostEstimate(flops=6 * 10**9, bytes_accessed=10**6, transcendentals=0),
        name=f"chain_{turn}",
    )(*operands)


def hold_kernel(*refs):
    refs[-1][...] = jnp.zeros_like(refs[-1])


def hold(*arrays):
    return pl.pallas_call(
        hold_kernel,
        out_shape=jax.ShapeDtypeStruct((8, 128), F32),
        in_specs=[WHOLE] * len(arrays),
        out_specs=WHOLE,
        compiler_params=pltpu.CompilerParams(vmem_limit_bytes=16 << 20),
        name="hold",
    )(*arrays)


def settle_kernel(layer, stream, gain, *refs):
    *parts, out, normed = refs
    total = stream[...].astype(F32)
    if parts:
        total = total + sum(part[...].astype(F32) for part in parts)
        out[...] = total.astype(B16)
        total = out[...].astype(F32)
    mean_square = jnp.mean(total * total, axis=-1, keepdims=True)
    normed[...] = (total * lax.rsqrt(mean_square + 1e-06) * gain[layer : layer + 1]).astype(B16)


def settle(stream, gain, layer, parts):
    return pl.pallas_call(
        functools.partial(settle_kernel, layer),
        out_shape=[jax.ShapeDtypeStruct(stream.shape, B16)] * 2,
        in_specs=[WHOLE] * (2 + len(parts)),
        out_specs=[WHOLE] * 2,
        compiler_params=pltpu.CompilerParams(vmem_limit_bytes=32 << 20),
        name="settle",
    )(stream, gain, *parts)


def project_kernel(count, first, layer, *refs):
    blocks = refs[:count]
    weights, rate_weight, base = refs[count : count + 3]
    out, rate, rows, sems = refs[-4:]
    loads = [pltpu.make_async_copy(b, rows.at[pl.ds(i * MB, MB)], sems.at[i]) for i, b in enumerate(blocks)]
    for load in loads:
        load.start()
    for load in loads:
        load.wait()
    gate = jax.nn.sigmoid(dot(rows[...], rate_weight[:, layer], NT)) * (base[layer : layer + 1] * (1.0 / MB))
    gate = gate.T
    for i in range(count):
        for p in range(gate.shape[0] // 2):
            rate[first + i, p] = gate[2 * p : 2 * p + 2, i * MB : (i + 1) * MB]
    out[first * MB : (first + count) * MB] = dot(rows[...], weights[layer]).astype(B16)


def project(blocks, first, total, layer, qkv_weight, rate_weight, base, earlier):
    count = len(blocks)
    depth, columns = qkv_weight.shape[1:]
    heads = rate_weight.shape[0]
    operands = [*blocks, qkv_weight, rate_weight, base, *earlier]
    return pl.pallas_call(
        functools.partial(project_kernel, count, first, layer),
        out_shape=[
            jax.ShapeDtypeStruct((total * MB, columns), B16),
            jax.ShapeDtypeStruct((total, heads // 2, 2, MB), F32),
        ],
        in_specs=[ANYWHERE] * count + [WHOLE] * (3 + len(earlier)),
        out_specs=[WHOLE] * 2,
        scratch_shapes=[pltpu.VMEM((count * MB, depth), B16), pltpu.SemaphoreType.DMA((count,))],
        input_output_aliases={count + 3 + i: i for i in range(len(earlier))},
        compiler_params=pltpu.CompilerParams(vmem_limit_bytes=16 << 20),
        cost_estimate=pl.CostEstimate(flops=2 * count * MB * depth * columns, bytes_accessed=10**6, transcendentals=0),
        name="project",
    )(*operands)


def unproject_kernel(first, count, layer, left, weights, *outs):
    total = dot(left[first * MB : (first + count) * MB], weights[layer]).astype(B16)
    for i in range(count):
        outs[i][...] = total[i * MB : (i + 1) * MB]


def unproject(mixed, first, count, layer, out_weight):
    depth, columns = out_weight.shape[1:]
    return pl.pallas_call(
        functools.partial(unproject_kernel, first, count, layer),
        out_shape=[jax.ShapeDtypeStruct((MB, columns), B16)] * count,
        in_specs=[WHOLE] * 2,
        out_specs=[WHOLE] * count,
        compiler_params=pltpu.CompilerParams(vmem_limit_bytes=16 << 20),
        cost_estimate=pl.CostEstimate(flops=2 * count * MB * depth * columns, bytes_accessed=10**6, transcendentals=0),
        name="unproject",
    )(mixed, out_weight)


NEAR = [(0, 0), (0, 1), (1, 0), (3, 0), (2, 0)]
FAR = [(1, 1), (3, 1), (2, 1)]
SLOTS = NEAR + FAR


def send(block, dx, dz):
    route = [(2 * x + z, 2 * ((x + dx) % 4) + (z ^ dz)) for x in range(4) for z in range(2)]
    return lax.ppermute(block, "head", route)


def fetch(block, dx, dz):
    return send(block, -dx, dz)


def gather_near(own):
    return [own] + [fetch(own, dx, dz) for dx, dz in NEAR[1:]]


def gather_far(near):
    return [fetch(near[1], 1, 0), fetch(near[1], 3, 0), fetch(near[4], 0, 1)]


def add(*blocks):
    return sum(block.astype(F32) for block in blocks)


def body(tokens, norm_gain, qkv_weight, rate_weight, rate_base, fast_first, fast_second, inner_gain, out_weight):
    seq_count = lax.axis_size("seq")
    layers, heads = rate_base.shape
    pairs = heads // 2
    rate_weight = rate_weight.transpose(2, 0, 1)
    gains = inner_gain.transpose(1, 0, 2)
    stream, normed = tokens, settle(tokens, norm_gain, 0, [])[1]
    place, me = lax.axis_index("seq"), lax.axis_index("head")
    for layer in range(layers):
        near = gather_near(normed)
        if layer == 0:
            held = hold(normed, qkv_weight, rate_weight, rate_base, out_weight, fast_first, fast_second, gains)
            near[1], near[4], place, me = lax.optimization_barrier((near[1], near[4], place, me, held))[:4]
            where = jnp.stack([place, me]).astype(jnp.int32)
        far = gather_far(near)
        made = ()
        for blocks, first in ((near, 0), (far, len(NEAR))):
            made = project(blocks, first, len(SLOTS), layer, qkv_weight, rate_weight, rate_base, made)
        qkv, rate = made
        mixed, sent = None, {}
        for turn in range(LAG * (seq_count - 1) + pairs):
            state = sent.get(turn - LAG)
            mixed, state = run_chain(turn, layer, where, qkv, rate, gains, fast_first, fast_second, state, mixed)
            route = [(row, row + 1) for row in range(seq_count - 1) if 0 <= turn - LAG * row < pairs]
            if route:
                sent[turn] = lax.ppermute(state, "seq", route)
        part_far = unproject(mixed, len(NEAR), len(FAR), layer, out_weight)
        part = unproject(mixed, 0, len(NEAR), layer, out_weight)
        a, b, c = send(part_far[0], 1, 0), send(part_far[1], 3, 0), send(part_far[2], 0, 1)
        side = add(part[1], a, b).astype(B16)
        across = add(part[4], c).astype(B16)
        side, across, left, right = lax.optimization_barrier((side, across, part[2], part[3]))
        sums = [part[0], send(left, 1, 0), send(right, 3, 0), send(across, 2, 0), send(side, 0, 1)]
        stream, normed = settle(stream, norm_gain, min(layer + 1, layers - 1), sums)
    return stream


def solution(mesh):
    rows = P(("dp", "seq", "head"), None)
    in_specs = (
        rows,
        P(),
        P(None, None, "head"),
        P(None, None, "head"),
        P(None, "head"),
        P(None, "head", None, None),
        P(None, "head", None, None),
        P(None, "head", None),
        P(None, "head", None),
    )
    return jax.shard_map(body, mesh=mesh, in_specs=in_specs, out_specs=rows, check_vma=False)
```

```python
import functools

import jax
import jax.numpy as jnp
from jax import lax
from jax.experimental import pallas as pl
from jax.experimental.pallas import tpu as pltpu
from jax.sharding import PartitionSpec as P

F32 = jnp.float32
B16 = jnp.bfloat16
MB = 64
GELU_A = 0.7978845608028654
GELU_B = 0.044715
NN = (((1,), (0,)), ((), ()))
NT = (((1,), (1,)), ((), ()))


def dot(left, right, dims=NN):
    return lax.dot_general(left, right, dims, preferred_element_type=F32)


def first_half(shape):
    return lax.broadcasted_iota(jnp.int32, shape, len(shape) - 1) < 64


def spread(x):
    mask = first_half(x.shape)
    zero = jnp.zeros_like(x)
    return jnp.concatenate([jnp.where(mask, x, zero), jnp.where(mask, zero, x)], axis=0)


def flip(x):
    y = spread(x).T
    return y[:64] + y[64:]


def fold(y):
    return jnp.where(first_half((64, 128)), y[:64], y[64:])


def mean0(x):
    return jnp.sum(x, axis=0, keepdims=True) * (1.0 / 64)


def normalise(y):
    centre = y - mean0(y)
    scale = lax.rsqrt(mean0(centre * centre) + 1e-5)
    return centre * scale, scale


def gelu_parts(h):
    square = h * h
    t = jnp.tanh(h * (GELU_A + (GELU_A * GELU_B) * square))
    half = 0.5 * h
    return square, t, half, half + half * t


def chain_steps(batches, tiles, gates_of, put_out, gain, w1, w2, rows, base, down, mix, target):
    def queries(b):
        t0, t1, _ = tiles(b)
        return jnp.where(first_half(t0.shape), t0, t1)

    def keys_and_target(b):
        t0, t1, t2 = tiles(b)
        mask = first_half(t0.shape)
        keys = pltpu.roll(jnp.where(mask, t2, t0), 64, 1)
        return spread(keys).astype(B16), flip(jnp.where(mask, t1, t2) - keys)

    def put(b, y):
        put_out(b, (queries(b) + flip(normalise(y)[0] * gain)).astype(B16))

    def answer(b, first, turned):
        hidden = dot(first, spread(queries(b)).astype(B16), NT)
        act = gelu_parts(hidden)[3].astype(B16)
        put(b, fold(dot(turned, act)))

    keys, wanted = keys_and_target(0)
    rows[0] = keys
    rows[1] = jnp.zeros_like(keys)
    target[...] = wanted
    base[...] = dot(w1[...].astype(B16), keys, NT)
    down[...] = jnp.zeros_like(down)
    mix[...] = jnp.zeros_like(mix)

    def step(b, now):
        hidden = base[...] - dot(down[...], mix[...])
        square, t, half, a = gelu_parts(hidden)
        act = a.astype(B16)
        second = w2[...].astype(B16)
        turned = second.T
        result = fold(dot(turned, act))
        slope = 0.5 + 0.5 * t + half * (1.0 - t * t) * (GELU_A + (3 * GELU_A * GELU_B) * square)
        first = w1[...] - dot(down[...], rows[1 - now])
        w1[...] = first
        first = first.astype(B16)
        keys, wanted = keys_and_target(jnp.minimum(b + 1, batches - 1))
        next_base = dot(first, keys, NT)
        next_mix = dot(rows[now], keys, NT).astype(B16)
        y, scale = normalise(result)
        dy = (y * gain - target[...]) * gates_of(b) * gain
        dy = scale * (dy - mean0(dy) - y * mean0(dy * y))
        cotangent = spread(dy).astype(B16)
        down[...] = (dot(second, cotangent) * slope).astype(B16)
        w2[...] = w2[...] - dot(act, cotangent, NT)
        answer(jnp.maximum(b - 1, 0), first, turned)
        rows[1 - now] = keys
        target[...] = wanted
        base[...] = next_base
        mix[...] = next_mix

    def steps(i, carry):
        for now in range(2):
            step(2 * i + now, now)
        return carry

    lax.fori_loop(0, batches // 2, steps, 0)
    w1[...] = w1[...] - dot(down[...], rows[1])
    answer(batches - 1, w1[...].astype(B16), w2[...].astype(B16).T)


SLOT_DIGITS = 0x63745210
LAG = 2


def chain_kernel(pairs, batches, layer, turn, where, qkv, rate, gains, first, second, *refs):
    out, state_out, w1, w2, rows, base, down, mix, target = refs[-9:]
    place, me = where[0], where[1]
    pair = turn - LAG * place

    def slot_of(b):
        digit = 2 * ((b // 2 - me // 2) & 3) + ((b ^ me) & 1)
        return (SLOT_DIGITS >> (4 * digit)) & 7

    def block(b):
        return pl.ds(pl.multiple_of(slot_of(b) * MB, MB), MB)

    def lanes(width, j=0):
        return pl.ds(pl.multiple_of(pair * width + j * 128, 128), 128)

    def tiles(b):
        return [qkv[block(b), lanes(384, j)].astype(F32) for j in range(3)]

    def gates_of(b):
        gates = rate[slot_of(b), pair]
        return jnp.concatenate([gates[0:1], gates[1:2]], axis=1)

    def put_out(b, value):
        out[block(b), lanes(128)] = value

    @pl.when((pair >= 0) & (pair < pairs))
    def _():
        if turn < pairs:

            @pl.when(place == 0)
            def _():
                heads = pl.ds(2 * pair, 2)
                w1[...] = first[layer, heads].reshape(128, 256).T
                w2[...] = second[layer, heads].reshape(128, 256).T

        if turn >= LAG:

            @pl.when(place > 0)
            def _():
                w1[...] = refs[0][0].astype(F32)
                w2[...] = refs[0][1].astype(F32)

        row = jnp.concatenate([gains[2 * pair, layer : layer + 1], gains[2 * pair + 1, layer : layer + 1]], axis=1)
        gain = flip(jnp.broadcast_to(row, (64, 128)))
        chain_steps(batches, tiles, gates_of, put_out, gain, w1, w2, rows, base, down, mix, target)
        state_out[0] = w1[...].astype(B16)
        state_out[1] = w2[...].astype(B16)


ANYWHERE = pl.BlockSpec(memory_space=pl.ANY)
WHOLE = pl.BlockSpec(memory_space=pltpu.VMEM)


def run_chain(turn, layer, where, qkv, rate, gains, first, second, state, out):
    tokens = qkv.shape[0]
    pairs = rate.shape[1]
    shape = (2, 256, 128)
    operands = [where, qkv, rate, gains, first, second] + ([] if state is None else [state])
    aliases = {}
    if out is not None:
        aliases = {len(operands): 0}
        operands += [out]
    return pl.pallas_call(
        functools.partial(chain_kernel, pairs, tokens // MB, layer, turn),
        out_shape=[
            jax.ShapeDtypeStruct((tokens, pairs * 128), B16),
            jax.ShapeDtypeStruct(shape, B16),
        ],
        in_specs=[pl.BlockSpec(memory_space=pltpu.SMEM)] + [WHOLE] * (len(operands) - 1),
        out_specs=[WHOLE, WHOLE],
        scratch_shapes=[
            pltpu.VMEM(shape[1:], F32),
            pltpu.VMEM(shape[1:], F32),
            pltpu.VMEM((2, 128, 128), B16),
            pltpu.VMEM((256, 128), F32),
            pltpu.VMEM((256, 128), B16),
            pltpu.VMEM((128, 128), B16),
            pltpu.VMEM((64, 128), F32),
        ],
        input_output_aliases=aliases,
        compiler_params=pltpu.CompilerParams(vmem_limit_bytes=16 << 20),
        cost_estimate=pl.CostEstimate(flops=6 * 10**9, bytes_accessed=10**6, transcendentals=0),
        name=f"chain_{turn}",
    )(*operands)


def hold_kernel(count, layer, *refs):
    arrays, held, sems = refs[:count], refs[-count - 1 : -1], refs[-1]
    moves = [pltpu.make_async_copy(array.at[layer], copy, sems.at[i]) for i, (array, copy) in enumerate(zip(arrays, held))]
    for move in moves:
        move.start()
    for move in moves:
        move.wait()


def hold(arrays, layer, after):
    count = len(arrays)
    return pl.pallas_call(
        functools.partial(hold_kernel, count, layer),
        out_shape=[jax.ShapeDtypeStruct(array.shape[1:], array.dtype) for array in arrays],
        in_specs=[ANYWHERE] * (count + 1),
        out_specs=[WHOLE] * count,
        scratch_shapes=[pltpu.SemaphoreType.DMA((count,))],
        compiler_params=pltpu.CompilerParams(vmem_limit_bytes=46 << 20),
        name="hold",
    )(*arrays, after)


def settle_kernel(layer, stream, gain, *refs):
    *parts, out, normed = refs
    total = stream[...].astype(F32)
    if parts:
        total = total + sum(part[...].astype(F32) for part in parts)
        out[...] = total.astype(B16)
        total = out[...].astype(F32)
    mean_square = jnp.mean(total * total, axis=-1, keepdims=True)
    normed[...] = (total * lax.rsqrt(mean_square + 1e-06) * gain[layer : layer + 1]).astype(B16)


def settle(stream, gain, layer, parts):
    return pl.pallas_call(
        functools.partial(settle_kernel, layer),
        out_shape=[jax.ShapeDtypeStruct(stream.shape, B16)] * 2,
        in_specs=[WHOLE] * (2 + len(parts)),
        out_specs=[WHOLE] * 2,
        compiler_params=pltpu.CompilerParams(vmem_limit_bytes=32 << 20),
        name="settle",
    )(stream, gain, *parts)


def project_kernel(count, first, layer, *refs):
    blocks = refs[:count]
    weights, rate_weight, base = refs[count : count + 3]
    out, rate, rows, sems = refs[-4:]
    loads = [pltpu.make_async_copy(b, rows.at[pl.ds(i * MB, MB)], sems.at[i]) for i, b in enumerate(blocks)]
    for load in loads:
        load.start()
    for load in loads:
        load.wait()
    gate = jax.nn.sigmoid(dot(rows[...], rate_weight[:, layer], NT)) * (base[layer : layer + 1] * (1.0 / MB))
    gate = gate.T
    for i in range(count):
        for p in range(gate.shape[0] // 2):
            rate[first + i, p] = gate[2 * p : 2 * p + 2, i * MB : (i + 1) * MB]
    tile = 384

    def step(i, carry):
        columns = pl.ds(pl.multiple_of(i * tile, tile), tile)
        out[first * MB : (first + count) * MB, columns] = dot(rows[...], weights[:, columns]).astype(B16)
        return carry

    lax.fori_loop(0, out.shape[1] // tile, step, 0)


def project(blocks, first, total, layer, qkv_weight, rate_weight, base, earlier):
    count = len(blocks)
    depth, columns = qkv_weight.shape
    heads = rate_weight.shape[0]
    operands = [*blocks, qkv_weight, rate_weight, base, *earlier]
    return pl.pallas_call(
        functools.partial(project_kernel, count, first, layer),
        out_shape=[
            jax.ShapeDtypeStruct((total * MB, columns), B16),
            jax.ShapeDtypeStruct((total, heads // 2, 2, MB), F32),
        ],
        in_specs=[ANYWHERE] * count + [WHOLE] * (3 + len(earlier)),
        out_specs=[WHOLE] * 2,
        scratch_shapes=[pltpu.VMEM((count * MB, depth), B16), pltpu.SemaphoreType.DMA((count,))],
        input_output_aliases={count + 3 + i: i for i in range(len(earlier))},
        compiler_params=pltpu.CompilerParams(vmem_limit_bytes=16 << 20),
        cost_estimate=pl.CostEstimate(flops=2 * count * MB * depth * columns, bytes_accessed=10**6, transcendentals=0),
        name="project",
    )(*operands)


def unproject_kernel(first, count, left, weights, *outs):
    total = dot(left[first * MB : (first + count) * MB], weights[...]).astype(B16)
    for i in range(count):
        outs[i][...] = total[i * MB : (i + 1) * MB]


def unproject(mixed, first, count, out_weight):
    depth, columns = out_weight.shape
    return pl.pallas_call(
        functools.partial(unproject_kernel, first, count),
        out_shape=[jax.ShapeDtypeStruct((MB, columns), B16)] * count,
        in_specs=[WHOLE] * 2,
        out_specs=[WHOLE] * count,
        compiler_params=pltpu.CompilerParams(vmem_limit_bytes=16 << 20),
        cost_estimate=pl.CostEstimate(flops=2 * count * MB * depth * columns, bytes_accessed=10**6, transcendentals=0),
        name="unproject",
    )(mixed, out_weight)


NEAR = [(0, 0), (0, 1), (1, 0), (3, 0), (2, 0)]
FAR = [(1, 1), (3, 1), (2, 1)]
SLOTS = NEAR + FAR


def send(block, dx, dz):
    route = [(2 * x + z, 2 * ((x + dx) % 4) + (z ^ dz)) for x in range(4) for z in range(2)]
    return lax.ppermute(block, "head", route)


def fetch(block, dx, dz):
    return send(block, -dx, dz)


def gather_near(own):
    return [own] + [fetch(own, dx, dz) for dx, dz in NEAR[1:]]


def gather_far(near):
    return [fetch(near[1], 1, 0), fetch(near[1], 3, 0), fetch(near[4], 0, 1)]


def add(*blocks):
    return sum(block.astype(F32) for block in blocks)


def body(tokens, norm_gain, qkv_weight, rate_weight, rate_base, fast_first, fast_second, inner_gain, out_weight):
    seq_count = lax.axis_size("seq")
    layers, heads = rate_base.shape
    pairs = heads // 2
    rate_weight = rate_weight.transpose(2, 0, 1)
    gains = inner_gain.transpose(1, 0, 2)
    stream, normed = tokens, settle(tokens, norm_gain, 0, [])[1]
    place, me = lax.axis_index("seq"), lax.axis_index("head")
    for layer in range(layers):
        near = gather_near(normed)
        qkv_held, out_held = hold([qkv_weight, out_weight], layer, normed)
        if layer == 0:
            place, me = lax.optimization_barrier((place, me, near[4]))[:2]
            where = jnp.stack([place, me]).astype(jnp.int32)
        far = gather_far(near)
        made = ()
        for blocks, first in ((near, 0), (far, len(NEAR))):
            made = project(blocks, first, len(SLOTS), layer, qkv_held, rate_weight, rate_base, made)
        qkv, rate = made
        mixed, sent = None, {}
        for turn in range(LAG * (seq_count - 1) + pairs):
            state = sent.get(turn - LAG)
            mixed, state = run_chain(turn, layer, where, qkv, rate, gains, fast_first, fast_second, state, mixed)
            route = [(row, row + 1) for row in range(seq_count - 1) if 0 <= turn - LAG * row < pairs]
            if route:
                sent[turn] = lax.ppermute(state, "seq", route)
        part_far = unproject(mixed, len(NEAR), len(FAR), out_held)
        part = unproject(mixed, 0, len(NEAR), out_held)
        a, b, c = send(part_far[0], 1, 0), send(part_far[1], 3, 0), send(part_far[2], 0, 1)
        side = add(part[1], a, b).astype(B16)
        across = add(part[4], c).astype(B16)
        side, across, left, right = lax.optimization_barrier((side, across, part[2], part[3]))
        sums = [part[0], send(left, 1, 0), send(right, 3, 0), send(across, 2, 0), send(side, 0, 1)]
        stream, normed = settle(stream, norm_gain, min(layer + 1, layers - 1), sums)
    return stream


def solution(mesh):
    rows = P(("dp", "seq", "head"), None)
    in_specs = (
        rows,
        P(),
        P(None, None, "head"),
        P(None, None, "head"),
        P(None, "head"),
        P(None, "head", None, None),
        P(None, "head", None, None),
        P(None, "head", None),
        P(None, "head", None),
    )
    return jax.shard_map(body, mesh=mesh, in_specs=in_specs, out_specs=rows, check_vma=False)
```

```python
import functools

import jax
import jax.numpy as jnp
import numpy as np
from jax import lax
from jax.experimental import pallas as pl
from jax.experimental.pallas import tpu as pltpu
from jax.sharding import PartitionSpec as P

F32 = jnp.float32
B16 = jnp.bfloat16
MB = 64
GELU_A = 0.7978845608028654
GELU_B = 0.044715
NN = (((1,), (0,)), ((), ()))
NT = (((1,), (1,)), ((), ()))


def dot(left, right, dims=NN):
    return lax.dot_general(left, right, dims, preferred_element_type=F32)


def first_half(shape):
    return lax.broadcasted_iota(jnp.int32, shape, len(shape) - 1) < 64


def spread(x):
    mask = first_half(x.shape)
    zero = jnp.zeros_like(x)
    return jnp.concatenate([jnp.where(mask, x, zero), jnp.where(mask, zero, x)], axis=0)


def flip(x):
    y = spread(x).T
    return y[:64] + y[64:]


def fold(y):
    return jnp.where(first_half((64, 128)), y[:64], y[64:])


def mean0(x):
    return jnp.sum(x, axis=0, keepdims=True) * (1.0 / 64)


def normalise(y):
    centre = y - mean0(y)
    scale = lax.rsqrt(mean0(centre * centre) + 1e-5)
    return centre * scale, scale


def gelu_parts(h):
    square = h * h
    t = jnp.tanh(h * (GELU_A + (GELU_A * GELU_B) * square))
    half = 0.5 * h
    return square, t, half, half + half * t


def chain_steps(pairs, batches, block, qkv, gates_of, gain, w1, w2, out, rows, target):
    every = range(pairs)

    def tiles(b, p):
        return [qkv[block(b), p * 384 + j * 128 : p * 384 + (j + 1) * 128].astype(F32) for j in range(3)]

    def queries(b, p):
        t0, t1, _ = tiles(b, p)
        return jnp.where(first_half(t0.shape), t0, t1)

    def prepare_keys(b):
        for p in every:
            t0, t1, t2 = tiles(b, p)
            mask = first_half(t0.shape)
            keys = pltpu.roll(jnp.where(mask, t2, t0), 64, 1)
            values = jnp.where(mask, t1, t2)
            rows[p, 0:128] = spread(keys).astype(B16)
            target[p] = flip(values - keys)

    def prepare_queries(b):
        for p in every:
            rows[p, 128:256] = spread(queries(b, p)).astype(B16)

    def put(b, p, y):
        out[block(b), p * 128 : (p + 1) * 128] = (queries(b, p) + flip(normalise(y)[0] * gain[p])).astype(B16)

    prepare_keys(0)
    rows[:, 128:256] = jnp.zeros((pairs, 128, 128), B16)

    def step(b):
        second = [w2[p].astype(B16) for p in every]
        hidden = [dot(w1[p].astype(B16), rows[p], NT) for p in every]
        parts = [gelu_parts(hidden[p][:, :128]) for p in every]
        act = [part[3].astype(B16) for part in parts]
        turned = [second[p].T for p in every]
        result = [fold(dot(turned[p], act[p])) for p in every]
        slope = [
            0.5 + 0.5 * t + half * (1.0 - t * t) * (GELU_A + (3 * GELU_A * GELU_B) * square) for square, t, half, _ in parts
        ]
        act_q = [gelu_parts(hidden[p][:, 128:])[3].astype(B16) for p in every]
        result_q = [fold(dot(turned[p], act_q[p])) for p in every]
        cotangent = []
        for p in every:
            y, scale = normalise(result[p])
            dy = (y * gain[p] - target[p]) * gates_of(b, p) * gain[p]
            dy = scale * (dy - mean0(dy) - y * mean0(dy * y))
            cotangent.append(spread(dy).astype(B16))
        for p in every:
            down = (dot(second[p], cotangent[p]) * slope[p]).astype(B16)
            w1[p] = w1[p] - dot(down, rows[p, 0:128])
            w2[p] = w2[p] - dot(act[p], cotangent[p], NT)
        for p in every:
            put(jnp.maximum(b - 1, 0), p, result_q[p])
        prepare_keys(jnp.minimum(b + 1, batches - 1))
        prepare_queries(b)

    def steps(i, carry):
        for j in range(UNROLL):
            step(UNROLL * i + j)
        return carry

    lax.fori_loop(0, batches // UNROLL, steps, 0)
    for p in every:
        hidden = dot(w1[p].astype(B16), rows[p, 128:256], NT)
        act = gelu_parts(hidden)[3].astype(B16)
        put(batches - 1, p, fold(dot(w2[p].astype(B16).T, act)))


UNROLL = 2


def chain_kernel(layer, turn, where, qkv, rate, gains, *refs):
    out, state_out, gain, w1, w2, rows, target = refs[-7:]
    pairs = rate.shape[1]

    @pl.when(where[0] == turn)
    def _():
        for p in range(pairs):
            if turn == 0:
                heads = slice(2 * p, 2 * p + 2)
                w1[p] = refs[0][layer, heads].reshape(128, 256).T
                w2[p] = refs[1][layer, heads].reshape(128, 256).T
            else:
                w1[p] = refs[0][0, p].astype(F32)
                w2[p] = refs[0][1, p].astype(F32)
            row = jnp.concatenate([gains[2 * p, layer : layer + 1], gains[2 * p + 1, layer : layer + 1]], axis=1)
            gain[p] = flip(jnp.broadcast_to(row, (64, 128)))

        def block(b):
            return pl.ds(pl.multiple_of(where[b + 1] * MB, MB), MB)

        def gates_of(b, p):
            gates = rate[where[b + 1], p]
            return jnp.concatenate([gates[0:1], gates[1:2]], axis=1)

        chain_steps(pairs, qkv.shape[0] // MB, block, qkv, gates_of, gain, w1, w2, out, rows, target)
        state_out[0] = w1[...].astype(B16)
        state_out[1] = w2[...].astype(B16)


ANYWHERE = pl.BlockSpec(memory_space=pl.ANY)
WHOLE = pl.BlockSpec(memory_space=pltpu.VMEM)


def run_chain(turn, layer, where, qkv, rate, gains, state, out):
    tokens = qkv.shape[0]
    pairs = rate.shape[1]
    shape = (2, pairs, 256, 128)
    operands = [where, qkv, rate, gains, *state]
    aliases = {}
    if out is not None:
        aliases = {len(operands): 0}
        operands += [out]
    return pl.pallas_call(
        functools.partial(chain_kernel, layer, turn),
        out_shape=[
            jax.ShapeDtypeStruct((tokens, pairs * 128), B16),
            jax.ShapeDtypeStruct(shape, B16),
        ],
        in_specs=[pl.BlockSpec(memory_space=pltpu.SMEM)] + [WHOLE] * (len(operands) - 1),
        out_specs=[WHOLE, WHOLE],
        scratch_shapes=[
            pltpu.VMEM((pairs, 64, 128), F32),
            pltpu.VMEM(shape[1:], F32),
            pltpu.VMEM(shape[1:], F32),
            pltpu.VMEM((pairs, 256, 128), B16),
            pltpu.VMEM((pairs, 64, 128), F32),
        ],
        input_output_aliases=aliases,
        compiler_params=pltpu.CompilerParams(vmem_limit_bytes=16 << 20),
        cost_estimate=pl.CostEstimate(flops=6 * 10**9, bytes_accessed=10**6, transcendentals=0),
        name=f"chain_{turn}",
    )(*operands)


def settle_kernel(layer, stream, gain, *refs):
    *parts, out, normed = refs
    total = stream[...].astype(F32)
    if parts:
        total = total + sum(part[...].astype(F32) for part in parts)
        out[...] = total.astype(B16)
        total = out[...].astype(F32)
    mean_square = jnp.mean(total * total, axis=-1, keepdims=True)
    normed[...] = (total * lax.rsqrt(mean_square + 1e-06) * gain[layer : layer + 1]).astype(B16)


def settle(stream, gain, layer, parts):
    return pl.pallas_call(
        functools.partial(settle_kernel, layer),
        out_shape=[jax.ShapeDtypeStruct(stream.shape, B16)] * 2,
        in_specs=[WHOLE] * (2 + len(parts)),
        out_specs=[WHOLE] * 2,
        compiler_params=pltpu.CompilerParams(vmem_limit_bytes=8 << 20),
        cost_estimate=pl.CostEstimate(flops=0 if parts else 2 * 10**10, bytes_accessed=10**6, transcendentals=0),
        name="settle",
    )(stream, gain, *parts)


def project_kernel(count, first, layer, *refs):
    blocks = refs[:count]
    weights, rate_weight, base = refs[count : count + 3]
    out, rate, rows, sems = refs[-4:]
    loads = [pltpu.make_async_copy(b, rows.at[pl.ds(i * MB, MB)], sems.at[i]) for i, b in enumerate(blocks)]
    for load in loads:
        load.start()
    for load in loads:
        load.wait()
    gate = jax.nn.sigmoid(dot(rows[...], rate_weight[:, layer], NT)) * (base[layer : layer + 1] * (1.0 / MB))
    gate = gate.T
    for i in range(count):
        for p in range(gate.shape[0] // 2):
            rate[first + i, p] = gate[2 * p : 2 * p + 2, i * MB : (i + 1) * MB]
    out[first * MB : (first + count) * MB] = dot(rows[...], weights[layer]).astype(B16)


def project(blocks, first, total, layer, qkv_weight, rate_weight, base, earlier):
    count = len(blocks)
    depth, columns = qkv_weight.shape[1:]
    heads = rate_weight.shape[0]
    operands = [*blocks, qkv_weight, rate_weight, base, *earlier]
    return pl.pallas_call(
        functools.partial(project_kernel, count, first, layer),
        out_shape=[
            jax.ShapeDtypeStruct((total * MB, columns), B16),
            jax.ShapeDtypeStruct((total, heads // 2, 2, MB), F32),
        ],
        in_specs=[ANYWHERE] * count + [WHOLE] * (3 + len(earlier)),
        out_specs=[WHOLE] * 2,
        scratch_shapes=[pltpu.VMEM((count * MB, depth), B16), pltpu.SemaphoreType.DMA((count,))],
        input_output_aliases={count + 3 + i: i for i in range(len(earlier))},
        compiler_params=pltpu.CompilerParams(vmem_limit_bytes=16 << 20),
        cost_estimate=pl.CostEstimate(flops=2 * count * MB * depth * columns, bytes_accessed=10**6, transcendentals=0),
        name="project",
    )(*operands)


def unproject_kernel(first, count, layer, left, weights, *outs):
    total = dot(left[first * MB : (first + count) * MB], weights[layer]).astype(B16)
    for i in range(count):
        outs[i][...] = total[i * MB : (i + 1) * MB]


def unproject(mixed, first, count, layer, out_weight):
    depth, columns = out_weight.shape[1:]
    return pl.pallas_call(
        functools.partial(unproject_kernel, first, count, layer),
        out_shape=[jax.ShapeDtypeStruct((MB, columns), B16)] * count,
        in_specs=[WHOLE] * 2,
        out_specs=[WHOLE] * count,
        compiler_params=pltpu.CompilerParams(vmem_limit_bytes=16 << 20),
        cost_estimate=pl.CostEstimate(flops=2 * count * MB * depth * columns, bytes_accessed=10**6, transcendentals=0),
        name="unproject",
    )(mixed, out_weight)


NEAR = [(0, 0), (0, 1), (1, 0), (3, 0), (2, 0)]
FAR = [(1, 1), (3, 1), (2, 1)]
SLOTS = NEAR + FAR
SLOT_OF = np.array(
    [[SLOTS.index(((b // 2 - me // 2) % 4, (b + me) % 2)) for b in range(8)] for me in range(8)], dtype=np.int32
)


def send(block, dx, dz):
    route = [(2 * x + z, 2 * ((x + dx) % 4) + (z ^ dz)) for x in range(4) for z in range(2)]
    return lax.ppermute(block, "head", route)


def fetch(block, dx, dz):
    return send(block, -dx, dz)


def gather_near(own):
    return [own] + [fetch(own, dx, dz) for dx, dz in NEAR[1:]]


def gather_far(near):
    return [fetch(near[1], 1, 0), fetch(near[1], 3, 0), fetch(near[4], 0, 1)]


def add(*blocks):
    return sum(block.astype(F32) for block in blocks)


def body(tokens, norm_gain, qkv_weight, rate_weight, rate_base, fast_first, fast_second, inner_gain, out_weight):
    seq_count = lax.axis_size("seq")
    layers, heads = rate_base.shape
    rate_weight = rate_weight.transpose(2, 0, 1)
    gains = inner_gain.transpose(1, 0, 2)
    stream, normed = tokens, settle(tokens, norm_gain, 0, [])[1]
    place, me = lax.axis_index("seq"), lax.axis_index("head")
    for layer in range(layers):
        near = gather_near(normed)
        if layer == 0:
            place, me = lax.optimization_barrier((place, me, near[4]))[:2]
            slots = lax.dynamic_slice(jnp.asarray(SLOT_OF), (me, 0), (1, len(SLOTS)))[0]
            where = jnp.concatenate([place.reshape(1), slots]).astype(jnp.int32)
        far = gather_far(near)
        made = ()
        for blocks, first in ((near, 0), (far, len(NEAR))):
            made = project(blocks, first, len(SLOTS), layer, qkv_weight, rate_weight, rate_base, made)
        qkv, rate = made
        mixed, state = None, (fast_first, fast_second)
        for turn in range(seq_count):
            mixed, state = run_chain(turn, layer, where, qkv, rate, gains, state, mixed)
            if turn < seq_count - 1:
                state = (lax.ppermute(state, "seq", [(turn, turn + 1)]),)
        part_far = unproject(mixed, len(NEAR), len(FAR), layer, out_weight)
        part = unproject(mixed, 0, len(NEAR), layer, out_weight)
        a, b, c = send(part_far[0], 1, 0), send(part_far[1], 3, 0), send(part_far[2], 0, 1)
        side = add(part[1], a, b).astype(B16)
        across = add(part[4], c).astype(B16)
        side, across, left, right = lax.optimization_barrier((side, across, part[2], part[3]))
        sums = [part[0], send(left, 1, 0), send(right, 3, 0), send(across, 2, 0), send(side, 0, 1)]
        stream, normed = settle(stream, norm_gain, min(layer + 1, layers - 1), sums)
    return stream


def solution(mesh):
    rows = P(("dp", "seq", "head"), None)
    in_specs = (
        rows,
        P(),
        P(None, None, "head"),
        P(None, None, "head"),
        P(None, "head"),
        P(None, "head", None, None),
        P(None, "head", None, None),
        P(None, "head", None),
        P(None, "head", None),
    )
    return jax.shard_map(body, mesh=mesh, in_specs=in_specs, out_specs=rows, check_vma=False)
```

```python
import functools

import jax
import jax.numpy as jnp
import numpy as np
from jax import lax
from jax.experimental import pallas as pl
from jax.experimental.pallas import tpu as pltpu
from jax.sharding import PartitionSpec as P

F32 = jnp.float32
B16 = jnp.bfloat16
MB = 64
GELU_A = 0.7978845608028654
GELU_B = 0.044715
NN = (((1,), (0,)), ((), ()))
NT = (((1,), (1,)), ((), ()))


def dot(left, right, dims=NN):
    return lax.dot_general(left, right, dims, preferred_element_type=F32)


def first_half(shape):
    return lax.broadcasted_iota(jnp.int32, shape, len(shape) - 1) < 64


def spread(x):
    mask = first_half(x.shape)
    zero = jnp.zeros_like(x)
    return jnp.concatenate([jnp.where(mask, x, zero), jnp.where(mask, zero, x)], axis=0)


def flip(x):
    y = spread(x).T
    return y[:64] + y[64:]


def fold(y):
    return jnp.where(first_half((64, 128)), y[:64], y[64:])


def mean0(x):
    return jnp.sum(x, axis=0, keepdims=True) * (1.0 / 64)


def normalise(y):
    centre = y - mean0(y)
    scale = lax.rsqrt(mean0(centre * centre) + 1e-5)
    return centre * scale, scale


def gelu_parts(h):
    square = h * h
    t = jnp.tanh(h * (GELU_A + (GELU_A * GELU_B) * square))
    half = 0.5 * h
    return square, t, half, half + half * t


def chain_steps(pairs, batches, block, qkv, gates_of, gain, w1, w2, out, rows, target):
    every = range(pairs)

    def tiles(b, p):
        return [qkv[block(b), p * 384 + j * 128 : p * 384 + (j + 1) * 128].astype(F32) for j in range(3)]

    def queries(b, p):
        t0, t1, _ = tiles(b, p)
        return jnp.where(first_half(t0.shape), t0, t1)

    def keys_and_target(b, p):
        t0, t1, t2 = tiles(b, p)
        mask = first_half(t0.shape)
        keys = pltpu.roll(jnp.where(mask, t2, t0), 64, 1)
        values = jnp.where(mask, t1, t2)
        return spread(keys).astype(B16), flip(values - keys)

    def spread_queries(b, p):
        return spread(queries(b, p)).astype(B16)

    def put(b, p, y):
        out[block(b), p * 128 : (p + 1) * 128] = (queries(b, p) + flip(normalise(y)[0] * gain[p])).astype(B16)

    for p in every:
        rows[p, 0:128], target[p] = keys_and_target(0, p)
    rows[:, 128:256] = jnp.zeros((pairs, 128, 128), B16)

    def step(b):
        first = [w1[p].astype(B16) for p in every]
        second = [w2[p].astype(B16) for p in every]
        hidden = [dot(first[p], rows[p], NT) for p in every]
        turned = [second[p].T for p in every]
        parts = [gelu_parts(hidden[p][:, :128]) for p in every]
        act = [part[3].astype(B16) for part in parts]
        result = [dot(turned[p], act[p]) for p in every]
        slope = [
            0.5 + 0.5 * t + half * (1.0 - t * t) * (GELU_A + (3 * GELU_A * GELU_B) * square) for square, t, half, _ in parts
        ]
        act_q = [gelu_parts(hidden[p][:, 128:])[3].astype(B16) for p in every]
        result_q = [dot(turned[p], act_q[p]) for p in every]
        normal = [normalise(fold(result[p])) for p in every]
        cotangent = []
        for p in every:
            y, scale = normal[p]
            dy = (y * gain[p] - target[p]) * gates_of(b, p) * gain[p]
            dy = scale * (dy - mean0(dy) - y * mean0(dy * y))
            cotangent.append(spread(dy).astype(B16))
        back = [dot(second[p], cotangent[p]) for p in every]
        step2 = [dot(act[p], cotangent[p], NT) for p in every]
        down = [(back[p] * slope[p]).astype(B16) for p in every]
        step1 = [dot(down[p], rows[p, 0:128]) for p in every]
        for p in every:
            w2[p] = w2[p] - step2[p]
        following = [keys_and_target(jnp.minimum(b + 1, batches - 1), p) for p in every]
        asked = [spread_queries(b, p) for p in every]
        for p in every:
            put(jnp.maximum(b - 1, 0), p, fold(result_q[p]))
        for p in every:
            w1[p] = w1[p] - step1[p]
        for p in every:
            rows[p, 0:128], target[p] = following[p]
            rows[p, 128:256] = asked[p]

    def steps(i, carry):
        for j in range(UNROLL):
            step(UNROLL * i + j)
        return carry

    lax.fori_loop(0, batches // UNROLL, steps, 0)
    hidden = [dot(w1[p].astype(B16), rows[p, 128:256], NT) for p in every]
    turned = [w2[p].astype(B16).T for p in every]
    act = [gelu_parts(hidden[p])[3].astype(B16) for p in every]
    result = [dot(turned[p], act[p]) for p in every]
    for p in every:
        put(batches - 1, p, fold(result[p]))


UNROLL = 2


def chain_kernel(layer, turn, where, qkv, rate, gains, *refs):
    out, state_out, gain, w1, w2, rows, target = refs[-7:]
    pairs = rate.shape[1]

    @pl.when(where[0] == turn)
    def _():
        for p in range(pairs):
            if turn == 0:
                heads = slice(2 * p, 2 * p + 2)
                w1[p] = refs[0][layer, heads].reshape(128, 256).T
                w2[p] = refs[1][layer, heads].reshape(128, 256).T
            else:
                w1[p] = refs[0][0, p].astype(F32)
                w2[p] = refs[0][1, p].astype(F32)
            row = jnp.concatenate([gains[2 * p, layer : layer + 1], gains[2 * p + 1, layer : layer + 1]], axis=1)
            gain[p] = flip(jnp.broadcast_to(row, (64, 128)))

        def block(b):
            return pl.ds(pl.multiple_of(where[b + 1] * MB, MB), MB)

        def gates_of(b, p):
            gates = rate[where[b + 1], p]
            return jnp.concatenate([gates[0:1], gates[1:2]], axis=1)

        chain_steps(pairs, qkv.shape[0] // MB, block, qkv, gates_of, gain, w1, w2, out, rows, target)
        state_out[0] = w1[...].astype(B16)
        state_out[1] = w2[...].astype(B16)


ANYWHERE = pl.BlockSpec(memory_space=pl.ANY)
WHOLE = pl.BlockSpec(memory_space=pltpu.VMEM)


def run_chain(turn, layer, where, qkv, rate, gains, state, out):
    tokens = qkv.shape[0]
    pairs = rate.shape[1]
    shape = (2, pairs, 256, 128)
    operands = [where, qkv, rate, gains, *state]
    aliases = {}
    if out is not None:
        aliases = {len(operands): 0}
        operands += [out]
    return pl.pallas_call(
        functools.partial(chain_kernel, layer, turn),
        out_shape=[
            jax.ShapeDtypeStruct((tokens, pairs * 128), B16),
            jax.ShapeDtypeStruct(shape, B16),
        ],
        in_specs=[pl.BlockSpec(memory_space=pltpu.SMEM)] + [WHOLE] * (len(operands) - 1),
        out_specs=[WHOLE, WHOLE],
        scratch_shapes=[
            pltpu.VMEM((pairs, 64, 128), F32),
            pltpu.VMEM(shape[1:], F32),
            pltpu.VMEM(shape[1:], F32),
            pltpu.VMEM((pairs, 256, 128), B16),
            pltpu.VMEM((pairs, 64, 128), F32),
        ],
        input_output_aliases=aliases,
        compiler_params=pltpu.CompilerParams(vmem_limit_bytes=16 << 20),
        cost_estimate=pl.CostEstimate(flops=6 * 10**9, bytes_accessed=10**6, transcendentals=0),
        name=f"chain_{turn}",
    )(*operands)


def settle_kernel(layer, stream, gain, *refs):
    *parts, out, normed = refs
    total = stream[...].astype(F32)
    if parts:
        total = total + sum(part[...].astype(F32) for part in parts)
        out[...] = total.astype(B16)
        total = out[...].astype(F32)
    mean_square = jnp.mean(total * total, axis=-1, keepdims=True)
    normed[...] = (total * lax.rsqrt(mean_square + 1e-06) * gain[layer : layer + 1]).astype(B16)


def settle(stream, gain, layer, parts):
    return pl.pallas_call(
        functools.partial(settle_kernel, layer),
        out_shape=[jax.ShapeDtypeStruct(stream.shape, B16)] * 2,
        in_specs=[WHOLE] * (2 + len(parts)),
        out_specs=[WHOLE] * 2,
        compiler_params=pltpu.CompilerParams(vmem_limit_bytes=8 << 20),
        cost_estimate=pl.CostEstimate(flops=0 if parts else 2 * 10**10, bytes_accessed=10**6, transcendentals=0),
        name="settle",
    )(stream, gain, *parts)


def project_kernel(count, first, layer, *refs):
    blocks = refs[:count]
    weights, rate_weight, base = refs[count : count + 3]
    out, rate, rows, sems = refs[-4:]
    loads = [pltpu.make_async_copy(b, rows.at[pl.ds(i * MB, MB)], sems.at[i]) for i, b in enumerate(blocks)]
    for load in loads:
        load.start()
    for load in loads:
        load.wait()
    gate = jax.nn.sigmoid(dot(rows[...], rate_weight[:, layer], NT)) * (base[layer : layer + 1] * (1.0 / MB))
    gate = gate.T
    for i in range(count):
        for p in range(gate.shape[0] // 2):
            rate[first + i, p] = gate[2 * p : 2 * p + 2, i * MB : (i + 1) * MB]
    out[first * MB : (first + count) * MB] = dot(rows[...], weights[layer]).astype(B16)


def project(blocks, first, total, layer, qkv_weight, rate_weight, base, earlier):
    count = len(blocks)
    depth, columns = qkv_weight.shape[1:]
    heads = rate_weight.shape[0]
    operands = [*blocks, qkv_weight, rate_weight, base, *earlier]
    return pl.pallas_call(
        functools.partial(project_kernel, count, first, layer),
        out_shape=[
            jax.ShapeDtypeStruct((total * MB, columns), B16),
            jax.ShapeDtypeStruct((total, heads // 2, 2, MB), F32),
        ],
        in_specs=[ANYWHERE] * count + [WHOLE] * (3 + len(earlier)),
        out_specs=[WHOLE] * 2,
        scratch_shapes=[pltpu.VMEM((count * MB, depth), B16), pltpu.SemaphoreType.DMA((count,))],
        input_output_aliases={count + 3 + i: i for i in range(len(earlier))},
        compiler_params=pltpu.CompilerParams(vmem_limit_bytes=16 << 20),
        cost_estimate=pl.CostEstimate(flops=2 * count * MB * depth * columns, bytes_accessed=10**6, transcendentals=0),
        name="project",
    )(*operands)


def unproject_kernel(first, count, layer, left, weights, *outs):
    total = dot(left[first * MB : (first + count) * MB], weights[layer]).astype(B16)
    for i in range(count):
        outs[i][...] = total[i * MB : (i + 1) * MB]


def unproject(mixed, first, count, layer, out_weight):
    depth, columns = out_weight.shape[1:]
    return pl.pallas_call(
        functools.partial(unproject_kernel, first, count, layer),
        out_shape=[jax.ShapeDtypeStruct((MB, columns), B16)] * count,
        in_specs=[WHOLE] * 2,
        out_specs=[WHOLE] * count,
        compiler_params=pltpu.CompilerParams(vmem_limit_bytes=16 << 20),
        cost_estimate=pl.CostEstimate(flops=2 * count * MB * depth * columns, bytes_accessed=10**6, transcendentals=0),
        name="unproject",
    )(mixed, out_weight)


NEAR = [(0, 0), (0, 1), (1, 0), (3, 0), (2, 0)]
FAR = [(1, 1), (3, 1), (2, 1)]
SLOTS = NEAR + FAR
SLOT_OF = np.array(
    [[SLOTS.index(((b // 2 - me // 2) % 4, (b + me) % 2)) for b in range(8)] for me in range(8)], dtype=np.int32
)


def send(block, dx, dz):
    route = [(2 * x + z, 2 * ((x + dx) % 4) + (z ^ dz)) for x in range(4) for z in range(2)]
    return lax.ppermute(block, "head", route)


def fetch(block, dx, dz):
    return send(block, -dx, dz)


def gather_near(own):
    return [own] + [fetch(own, dx, dz) for dx, dz in NEAR[1:]]


def gather_far(near):
    return [fetch(near[1], 1, 0), fetch(near[1], 3, 0), fetch(near[4], 0, 1)]


def add(*blocks):
    return sum(block.astype(F32) for block in blocks)


def body(tokens, norm_gain, qkv_weight, rate_weight, rate_base, fast_first, fast_second, inner_gain, out_weight):
    seq_count = lax.axis_size("seq")
    layers, heads = rate_base.shape
    rate_weight = rate_weight.transpose(2, 0, 1)
    gains = inner_gain.transpose(1, 0, 2)
    stream, normed = tokens, settle(tokens, norm_gain, 0, [])[1]
    place, me = lax.axis_index("seq"), lax.axis_index("head")
    for layer in range(layers):
        near = gather_near(normed)
        if layer == 0:
            place, me = lax.optimization_barrier((place, me, near[4]))[:2]
            slots = lax.dynamic_slice(jnp.asarray(SLOT_OF), (me, 0), (1, len(SLOTS)))[0]
            where = jnp.concatenate([place.reshape(1), slots]).astype(jnp.int32)
        far = gather_far(near)
        made = ()
        for blocks, first in ((near, 0), (far, len(NEAR))):
            made = project(blocks, first, len(SLOTS), layer, qkv_weight, rate_weight, rate_base, made)
        qkv, rate = made
        mixed, state = None, (fast_first, fast_second)
        for turn in range(seq_count):
            mixed, state = run_chain(turn, layer, where, qkv, rate, gains, state, mixed)
            if turn < seq_count - 1:
                state = (lax.ppermute(state, "seq", [(turn, turn + 1)]),)
        part_far = unproject(mixed, len(NEAR), len(FAR), layer, out_weight)
        part = unproject(mixed, 0, len(NEAR), layer, out_weight)
        a, b, c = send(part_far[0], 1, 0), send(part_far[1], 3, 0), send(part_far[2], 0, 1)
        side = add(part[1], a, b).astype(B16)
        across = add(part[4], c).astype(B16)
        sums = [part[0], send(part[2], 1, 0), send(part[3], 3, 0), send(across, 2, 0), send(side, 0, 1)]
        stream, normed = settle(stream, norm_gain, min(layer + 1, layers - 1), sums)
    return stream


def solution(mesh):
    rows = P(("dp", "seq", "head"), None)
    in_specs = (
        rows,
        P(),
        P(None, None, "head"),
        P(None, None, "head"),
        P(None, "head"),
        P(None, "head", None, None),
        P(None, "head", None, None),
        P(None, "head", None),
        P(None, "head", None),
    )
    return jax.shard_map(body, mesh=mesh, in_specs=in_specs, out_specs=rows, check_vma=False)
```

```python
import functools

import jax
import jax.numpy as jnp
from jax import lax
from jax.experimental import pallas as pl
from jax.experimental.pallas import tpu as pltpu
from jax.sharding import PartitionSpec as P

F32 = jnp.float32
B16 = jnp.bfloat16
MB = 64
GELU_A = 0.7978845608028654
GELU_B = 0.044715
NN = (((1,), (0,)), ((), ()))
NT = (((1,), (1,)), ((), ()))


def dot(left, right, dims=NN):
    return lax.dot_general(left, right, dims, preferred_element_type=F32)


def first_half(shape):
    return lax.broadcasted_iota(jnp.int32, shape, len(shape) - 1) < 64


def spread(x):
    mask = first_half(x.shape)
    zero = jnp.zeros_like(x)
    return jnp.concatenate([jnp.where(mask, x, zero), jnp.where(mask, zero, x)], axis=0)


def flip(x):
    y = spread(x).T
    return y[:64] + y[64:]


def fold(y):
    return jnp.where(first_half((64, 128)), y[:64], y[64:])


def mean0(x):
    return jnp.sum(x, axis=0, keepdims=True) * (1.0 / 64)


def normalise(y):
    centre = y - mean0(y)
    scale = lax.rsqrt(mean0(centre * centre) + 1e-5)
    return centre * scale, scale


def gelu_parts(h):
    square = h * h
    t = jnp.tanh(h * (GELU_A + (GELU_A * GELU_B) * square))
    half = 0.5 * h
    return square, t, half, half + half * t


def chain_steps(pairs, batches, block, qkv, gates_of, gain, w1, w2, out, rows, target):
    every = range(pairs)

    def tiles(b, p):
        return [qkv[block(b), p * 384 + j * 128 : p * 384 + (j + 1) * 128].astype(F32) for j in range(3)]

    def queries(b, p):
        t0, t1, _ = tiles(b, p)
        return jnp.where(first_half(t0.shape), t0, t1)

    def keys_and_target(b, p):
        t0, t1, t2 = tiles(b, p)
        mask = first_half(t0.shape)
        keys = pltpu.roll(jnp.where(mask, t2, t0), 64, 1)
        values = jnp.where(mask, t1, t2)
        return spread(keys).astype(B16), flip(values - keys)

    def spread_queries(b, p):
        return spread(queries(b, p)).astype(B16)

    def put(b, p, y):
        out[block(b), p * 128 : (p + 1) * 128] = (queries(b, p) + flip(normalise(y)[0] * gain[p])).astype(B16)

    for p in every:
        rows[p, 0:128], target[p] = keys_and_target(0, p)
    rows[:, 128:256] = jnp.zeros((pairs, 128, 128), B16)

    def step(b):
        first = [w1[p].astype(B16) for p in every]
        second = [w2[p].astype(B16) for p in every]
        hidden = [dot(first[p], rows[p], NT) for p in every]
        turned = [second[p].T for p in every]
        parts = [gelu_parts(hidden[p][:, :128]) for p in every]
        act = [part[3].astype(B16) for part in parts]
        result = [dot(turned[p], act[p]) for p in every]
        slope = [
            0.5 + 0.5 * t + half * (1.0 - t * t) * (GELU_A + (3 * GELU_A * GELU_B) * square) for square, t, half, _ in parts
        ]
        act_q = [gelu_parts(hidden[p][:, 128:])[3].astype(B16) for p in every]
        result_q = [dot(turned[p], act_q[p]) for p in every]
        normal = [normalise(fold(result[p])) for p in every]
        cotangent = []
        for p in every:
            y, scale = normal[p]
            dy = (y * gain[p] - target[p]) * gates_of(b, p) * gain[p]
            dy = scale * (dy - mean0(dy) - y * mean0(dy * y))
            cotangent.append(spread(dy).astype(B16))
        back = [dot(second[p], cotangent[p]) for p in every]
        step2 = [dot(act[p], cotangent[p], NT) for p in every]
        down = [(back[p] * slope[p]).astype(B16) for p in every]
        step1 = [dot(down[p], rows[p, 0:128]) for p in every]
        for p in every:
            w2[p] = w2[p] - step2[p]
        following = [keys_and_target(jnp.minimum(b + 1, batches - 1), p) for p in every]
        asked = [spread_queries(b, p) for p in every]
        for p in every:
            put(jnp.maximum(b - 1, 0), p, fold(result_q[p]))
        for p in every:
            w1[p] = w1[p] - step1[p]
        for p in every:
            rows[p, 0:128], target[p] = following[p]
            rows[p, 128:256] = asked[p]

    def steps(i, carry):
        for j in range(UNROLL):
            step(UNROLL * i + j)
        return carry

    lax.fori_loop(0, batches // UNROLL, steps, 0)
    hidden = [dot(w1[p].astype(B16), rows[p, 128:256], NT) for p in every]
    turned = [w2[p].astype(B16).T for p in every]
    act = [gelu_parts(hidden[p])[3].astype(B16) for p in every]
    result = [dot(turned[p], act[p]) for p in every]
    for p in every:
        put(batches - 1, p, fold(result[p]))


UNROLL = 2
SLOT_DIGITS = 0x63745210
GROUPS = [(0, 1), (1, 2)]


def chain_kernel(layer, turn, group, qkv, rate, gains, *refs):
    out, state_out, gain, w1, w2, rows, target = refs[-7:]
    first_pair, pairs = group
    me = lax.axis_index("head")

    def slot_of(b):
        digit = 2 * ((b // 2 - me // 2) & 3) + ((b ^ me) & 1)
        return (SLOT_DIGITS >> (4 * digit)) & 7

    @pl.when(lax.axis_index("seq") == turn)
    def _():
        for p in range(pairs):
            if turn == 0:
                heads = slice(2 * (first_pair + p), 2 * (first_pair + p + 1))
                w1[p] = refs[0][layer, heads].reshape(128, 256).T
                w2[p] = refs[1][layer, heads].reshape(128, 256).T
            else:
                w1[p] = refs[0][0, p].astype(F32)
                w2[p] = refs[0][1, p].astype(F32)
            pair = first_pair + p
            row = jnp.concatenate([gains[2 * pair, layer : layer + 1], gains[2 * pair + 1, layer : layer + 1]], axis=1)
            gain[p] = flip(jnp.broadcast_to(row, (64, 128)))

        def block(b):
            return pl.ds(pl.multiple_of(slot_of(b) * MB, MB), MB)

        def gates_of(b, p):
            gates = rate[slot_of(b), first_pair + p]
            return jnp.concatenate([gates[0:1], gates[1:2]], axis=1)

        mine = qkv.at[:, pl.ds(384 * first_pair, 384 * pairs)]
        result = out.at[:, pl.ds(128 * first_pair, 128 * pairs)]
        chain_steps(pairs, qkv.shape[0] // MB, block, mine, gates_of, gain, w1, w2, result, rows, target)
        state_out[0] = w1[...].astype(B16)
        state_out[1] = w2[...].astype(B16)


ANYWHERE = pl.BlockSpec(memory_space=pl.ANY)
WHOLE = pl.BlockSpec(memory_space=pltpu.VMEM)


def run_chain(turn, layer, group, qkv, rate, gains, state, out):
    tokens = qkv.shape[0]
    pairs = group[1]
    shape = (2, pairs, 256, 128)
    operands = [qkv, rate, gains, *state]
    aliases = {}
    if out is not None:
        aliases = {len(operands): 0}
        operands += [out]
    return pl.pallas_call(
        functools.partial(chain_kernel, layer, turn, group),
        out_shape=[
            jax.ShapeDtypeStruct((tokens, rate.shape[1] * 128), B16),
            jax.ShapeDtypeStruct(shape, B16),
        ],
        in_specs=[WHOLE] * len(operands),
        out_specs=[WHOLE, WHOLE],
        scratch_shapes=[
            pltpu.VMEM((pairs, 64, 128), F32),
            pltpu.VMEM(shape[1:], F32),
            pltpu.VMEM(shape[1:], F32),
            pltpu.VMEM((pairs, 256, 128), B16),
            pltpu.VMEM((pairs, 64, 128), F32),
        ],
        input_output_aliases=aliases,
        compiler_params=pltpu.CompilerParams(vmem_limit_bytes=16 << 20),
        cost_estimate=pl.CostEstimate(flops=6 * 10**9, bytes_accessed=10**6, transcendentals=0),
        name=f"chain_{turn}_{group[0]}",
    )(*operands)


def settle_kernel(layer, stream, gain, *refs):
    *parts, out, normed = refs
    total = stream[...].astype(F32)
    if parts:
        total = total + sum(part[...].astype(F32) for part in parts)
        out[...] = total.astype(B16)
        total = out[...].astype(F32)
    mean_square = jnp.mean(total * total, axis=-1, keepdims=True)
    normed[...] = (total * lax.rsqrt(mean_square + 1e-06) * gain[layer : layer + 1]).astype(B16)


def settle(stream, gain, layer, parts):
    return pl.pallas_call(
        functools.partial(settle_kernel, layer),
        out_shape=[jax.ShapeDtypeStruct(stream.shape, B16)] * 2,
        in_specs=[WHOLE] * (2 + len(parts)),
        out_specs=[WHOLE] * 2,
        compiler_params=pltpu.CompilerParams(vmem_limit_bytes=8 << 20),
        cost_estimate=pl.CostEstimate(flops=0 if parts else 2 * 10**10, bytes_accessed=10**6, transcendentals=0),
        name="settle",
    )(stream, gain, *parts)


def project_kernel(count, first, layer, *refs):
    blocks = refs[:count]
    weights, rate_weight, base = refs[count : count + 3]
    out, rate, rows, sems = refs[-4:]
    loads = [pltpu.make_async_copy(b, rows.at[pl.ds(i * MB, MB)], sems.at[i]) for i, b in enumerate(blocks)]
    for load in loads:
        load.start()
    for load in loads:
        load.wait()
    gate = jax.nn.sigmoid(dot(rows[...], rate_weight[:, layer], NT)) * (base[layer : layer + 1] * (1.0 / MB))
    gate = gate.T
    for i in range(count):
        for p in range(gate.shape[0] // 2):
            rate[first + i, p] = gate[2 * p : 2 * p + 2, i * MB : (i + 1) * MB]
    out[first * MB : (first + count) * MB] = dot(rows[...], weights[layer]).astype(B16)


def project(blocks, first, total, layer, qkv_weight, rate_weight, base, earlier):
    count = len(blocks)
    depth, columns = qkv_weight.shape[1:]
    heads = rate_weight.shape[0]
    operands = [*blocks, qkv_weight, rate_weight, base, *earlier]
    return pl.pallas_call(
        functools.partial(project_kernel, count, first, layer),
        out_shape=[
            jax.ShapeDtypeStruct((total * MB, columns), B16),
            jax.ShapeDtypeStruct((total, heads // 2, 2, MB), F32),
        ],
        in_specs=[ANYWHERE] * count + [WHOLE] * (3 + len(earlier)),
        out_specs=[WHOLE] * 2,
        scratch_shapes=[pltpu.VMEM((count * MB, depth), B16), pltpu.SemaphoreType.DMA((count,))],
        input_output_aliases={count + 3 + i: i for i in range(len(earlier))},
        compiler_params=pltpu.CompilerParams(vmem_limit_bytes=16 << 20),
        cost_estimate=pl.CostEstimate(flops=2 * count * MB * depth * columns, bytes_accessed=10**6, transcendentals=0),
        name="project",
    )(*operands)


def unproject_kernel(first, count, layer, left, weights, *outs):
    total = dot(left[first * MB : (first + count) * MB], weights[layer]).astype(B16)
    for i in range(count):
        outs[i][...] = total[i * MB : (i + 1) * MB]


def unproject(mixed, first, count, layer, out_weight):
    depth, columns = out_weight.shape[1:]
    return pl.pallas_call(
        functools.partial(unproject_kernel, first, count, layer),
        out_shape=[jax.ShapeDtypeStruct((MB, columns), B16)] * count,
        in_specs=[WHOLE] * 2,
        out_specs=[WHOLE] * count,
        compiler_params=pltpu.CompilerParams(vmem_limit_bytes=16 << 20),
        cost_estimate=pl.CostEstimate(flops=2 * count * MB * depth * columns, bytes_accessed=10**6, transcendentals=0),
        name="unproject",
    )(mixed, out_weight)


NEAR = [(0, 0), (0, 1), (1, 0), (3, 0), (2, 0)]
FAR = [(1, 1), (3, 1), (2, 1)]
SLOTS = NEAR + FAR

def send(block, dx, dz):
    route = [(2 * x + z, 2 * ((x + dx) % 4) + (z ^ dz)) for x in range(4) for z in range(2)]
    return lax.ppermute(block, "head", route)


def fetch(block, dx, dz):
    return send(block, -dx, dz)


def gather_near(own):
    return [own] + [fetch(own, dx, dz) for dx, dz in NEAR[1:]]


def gather_far(near):
    return [fetch(near[1], 1, 0), fetch(near[1], 3, 0), fetch(near[4], 0, 1)]


def add(*blocks):
    return sum(block.astype(F32) for block in blocks)


def body(tokens, norm_gain, qkv_weight, rate_weight, rate_base, fast_first, fast_second, inner_gain, out_weight):
    seq_count = lax.axis_size("seq")
    layers, heads = rate_base.shape
    rate_weight = rate_weight.transpose(2, 0, 1)
    gains = inner_gain.transpose(1, 0, 2)
    stream, normed = tokens, settle(tokens, norm_gain, 0, [])[1]
    for layer in range(layers):
        near = gather_near(normed)
        far = gather_far(near)
        made = ()
        for blocks, first in ((near, 0), (far, len(NEAR))):
            made = project(blocks, first, len(SLOTS), layer, qkv_weight, rate_weight, rate_base, made)
        qkv, rate = made
        mixed, states = None, [(fast_first, fast_second)] * len(GROUPS)
        for turn in range(seq_count):
            for i, group in enumerate(GROUPS):
                mixed, state = run_chain(turn, layer, group, qkv, rate, gains, states[i], mixed)
                if turn < seq_count - 1:
                    states[i] = (lax.ppermute(state, "seq", [(turn, turn + 1)]),)
        part_far = unproject(mixed, len(NEAR), len(FAR), layer, out_weight)
        part = unproject(mixed, 0, len(NEAR), layer, out_weight)
        a, b, c = send(part_far[0], 1, 0), send(part_far[1], 3, 0), send(part_far[2], 0, 1)
        side = add(part[1], a, b).astype(B16)
        across = add(part[4], c).astype(B16)
        left, right = part[2], part[3]
        if layer == layers - 1:
            side, across, left, right = lax.optimization_barrier((side, across, left, right))
        sums = [part[0], send(left, 1, 0), send(right, 3, 0), send(across, 2, 0), send(side, 0, 1)]
        stream, normed = settle(stream, norm_gain, min(layer + 1, layers - 1), sums)
    return stream


def solution(mesh):
    rows = P(("dp", "seq", "head"), None)
    in_specs = (
        rows,
        P(),
        P(None, None, "head"),
        P(None, None, "head"),
        P(None, "head"),
        P(None, "head", None, None),
        P(None, "head", None, None),
        P(None, "head", None),
        P(None, "head", None),
    )
    return jax.shard_map(body, mesh=mesh, in_specs=in_specs, out_specs=rows, check_vma=False)
```

```python
import functools

import jax
import jax.numpy as jnp
from jax import lax
from jax.experimental import pallas as pl
from jax.experimental.pallas import tpu as pltpu
from jax.sharding import PartitionSpec as P

F32 = jnp.float32
B16 = jnp.bfloat16
MB = 64
GELU_A = 0.7978845608028654
GELU_B = 0.044715
NN = (((1,), (0,)), ((), ()))
NT = (((1,), (1,)), ((), ()))


def dot(left, right, dims=NN):
    return lax.dot_general(left, right, dims, preferred_element_type=F32)


def first_half(shape):
    return lax.broadcasted_iota(jnp.int32, shape, len(shape) - 1) < 64


def spread(x):
    mask = first_half(x.shape)
    zero = jnp.zeros_like(x)
    return jnp.concatenate([jnp.where(mask, x, zero), jnp.where(mask, zero, x)], axis=0)


def flip(x):
    y = spread(x).T
    return y[:64] + y[64:]


def fold(y):
    return jnp.where(first_half((64, 128)), y[:64], y[64:])


def mean0(x):
    return jnp.sum(x, axis=0, keepdims=True) * (1.0 / 64)


def normalise(y):
    centre = y - mean0(y)
    scale = lax.rsqrt(mean0(centre * centre) + 1e-5)
    return centre * scale, scale


def gelu_parts(h):
    square = h * h
    t = jnp.tanh(h * (GELU_A + (GELU_A * GELU_B) * square))
    half = 0.5 * h
    return square, t, half, half + half * t


def chain_steps(pairs, batches, block, qkv, gates_of, gain, w1, w2, out, rows, target):
    every = range(pairs)

    def tiles(b, p):
        return [qkv[block(b), p * 384 + j * 128 : p * 384 + (j + 1) * 128].astype(F32) for j in range(3)]

    def queries(b, p):
        t0, t1, _ = tiles(b, p)
        return jnp.where(first_half(t0.shape), t0, t1)

    def keys_and_target(b, p):
        t0, t1, t2 = tiles(b, p)
        mask = first_half(t0.shape)
        keys = pltpu.roll(jnp.where(mask, t2, t0), 64, 1)
        values = jnp.where(mask, t1, t2)
        return spread(keys).astype(B16), flip(values - keys)

    def spread_queries(b, p):
        return spread(queries(b, p)).astype(B16)

    def put(b, p, y):
        out[block(b), p * 128 : (p + 1) * 128] = (queries(b, p) + flip(normalise(y)[0] * gain[p])).astype(B16)

    for p in every:
        rows[p, 0:128], target[p] = keys_and_target(0, p)
    rows[:, 128:256] = jnp.zeros((pairs, 128, 128), B16)

    def step(b):
        first = [w1[p].astype(B16) for p in every]
        second = [w2[p].astype(B16) for p in every]
        hidden = [dot(first[p], rows[p], NT) for p in every]
        turned = [second[p].T for p in every]
        parts = [gelu_parts(hidden[p][:, :128]) for p in every]
        act = [part[3].astype(B16) for part in parts]
        result = [dot(turned[p], act[p]) for p in every]
        slope = [
            0.5 + 0.5 * t + half * (1.0 - t * t) * (GELU_A + (3 * GELU_A * GELU_B) * square) for square, t, half, _ in parts
        ]
        act_q = [gelu_parts(hidden[p][:, 128:])[3].astype(B16) for p in every]
        result_q = [dot(turned[p], act_q[p]) for p in every]
        normal = [normalise(fold(result[p])) for p in every]
        cotangent = []
        for p in every:
            y, scale = normal[p]
            dy = (y * gain[p] - target[p]) * gates_of(b, p) * gain[p]
            dy = scale * (dy - mean0(dy) - y * mean0(dy * y))
            cotangent.append(spread(dy).astype(B16))
        back = [dot(second[p], cotangent[p]) for p in every]
        step2 = [dot(act[p], cotangent[p], NT) for p in every]
        down = [(back[p] * slope[p]).astype(B16) for p in every]
        step1 = [dot(down[p], rows[p, 0:128]) for p in every]
        for p in every:
            w2[p] = w2[p] - step2[p]
        following = [keys_and_target(jnp.minimum(b + 1, batches - 1), p) for p in every]
        asked = [spread_queries(b, p) for p in every]
        for p in every:
            put(jnp.maximum(b - 1, 0), p, fold(result_q[p]))
        for p in every:
            w1[p] = w1[p] - step1[p]
        for p in every:
            rows[p, 0:128], target[p] = following[p]
            rows[p, 128:256] = asked[p]

    def steps(i, carry):
        for j in range(UNROLL):
            step(UNROLL * i + j)
        return carry

    lax.fori_loop(0, batches // UNROLL, steps, 0)
    hidden = [dot(w1[p].astype(B16), rows[p, 128:256], NT) for p in every]
    turned = [w2[p].astype(B16).T for p in every]
    act = [gelu_parts(hidden[p])[3].astype(B16) for p in every]
    result = [dot(turned[p], act[p]) for p in every]
    for p in every:
        put(batches - 1, p, fold(result[p]))


UNROLL = 2
SLOT_DIGITS = 0x63745210
GROUPS = [(0, 1), (1, 2)]


def chain_kernel(layer, turn, group, outputs, qkv, rate, gains, *refs):
    *state_out, gain, w1, w2, rows, target = refs[len(refs) - 5 - outputs + 1 :]
    out = refs[len(refs) - 5 - outputs]
    first_pair, pairs = group
    me = lax.axis_index("head")

    def slot_of(b):
        digit = 2 * ((b // 2 - me // 2) & 3) + ((b ^ me) & 1)
        return (SLOT_DIGITS >> (4 * digit)) & 7

    @pl.when(lax.axis_index("seq") == turn)
    def _():
        for p in range(pairs):
            if turn == 0:
                heads = slice(2 * (first_pair + p), 2 * (first_pair + p + 1))
                w1[p] = refs[0][layer, heads].reshape(128, 256).T
                w2[p] = refs[1][layer, heads].reshape(128, 256).T
            else:
                w1[p] = refs[0][0, p].astype(F32)
                w2[p] = refs[0][1, p].astype(F32)
            pair = first_pair + p
            row = jnp.concatenate([gains[2 * pair, layer : layer + 1], gains[2 * pair + 1, layer : layer + 1]], axis=1)
            gain[p] = flip(jnp.broadcast_to(row, (64, 128)))

        def block(b):
            return pl.ds(pl.multiple_of(slot_of(b) * MB, MB), MB)

        def gates_of(b, p):
            gates = rate[slot_of(b), first_pair + p]
            return jnp.concatenate([gates[0:1], gates[1:2]], axis=1)

        mine = qkv.at[:, pl.ds(384 * first_pair, 384 * pairs)]
        result = out.at[:, pl.ds(128 * first_pair, 128 * pairs)]
        chain_steps(pairs, qkv.shape[0] // MB, block, mine, gates_of, gain, w1, w2, result, rows, target)
        for state in state_out:
            state[0] = w1[...].astype(B16)
            state[1] = w2[...].astype(B16)


ANYWHERE = pl.BlockSpec(memory_space=pl.ANY)
WHOLE = pl.BlockSpec(memory_space=pltpu.VMEM)


def run_chain(turn, last, layer, group, qkv, rate, gains, state, out):
    tokens = qkv.shape[0]
    pairs = group[1]
    shape = (2, pairs, 256, 128)
    operands = [qkv, rate, gains, *state]
    aliases = {}
    if out is not None:
        aliases = {len(operands): 0}
        operands += [out]
    out_shape = [jax.ShapeDtypeStruct((tokens, rate.shape[1] * 128), B16)]
    out_shape += [] if last else [jax.ShapeDtypeStruct(shape, B16)]
    return pl.pallas_call(
        functools.partial(chain_kernel, layer, turn, group, len(out_shape)),
        out_shape=out_shape,
        in_specs=[WHOLE] * len(operands),
        out_specs=[WHOLE] * len(out_shape),
        scratch_shapes=[
            pltpu.VMEM((pairs, 64, 128), F32),
            pltpu.VMEM(shape[1:], F32),
            pltpu.VMEM(shape[1:], F32),
            pltpu.VMEM((pairs, 256, 128), B16),
            pltpu.VMEM((pairs, 64, 128), F32),
        ],
        input_output_aliases=aliases,
        compiler_params=pltpu.CompilerParams(vmem_limit_bytes=16 << 20),
        cost_estimate=pl.CostEstimate(flops=6 * 10**9, bytes_accessed=10**6, transcendentals=0),
        name=f"chain_{turn}_{group[0]}",
    )(*operands)


def settle_kernel(layer, stream, gain, *refs):
    *parts, out, normed = refs
    total = stream[...].astype(F32)
    if parts:
        total = total + sum(part[...].astype(F32) for part in parts)
        out[...] = total.astype(B16)
        total = out[...].astype(F32)
    mean_square = jnp.mean(total * total, axis=-1, keepdims=True)
    normed[...] = (total * lax.rsqrt(mean_square + 1e-06) * gain[layer : layer + 1]).astype(B16)


def settle(stream, gain, layer, parts):
    whole = [WHOLE] * (2 + len(parts))
    if not parts:
        whole = [pl.BlockSpec(array.shape, lambda i: (0, 0)) for array in (stream, gain)]
    return pl.pallas_call(
        functools.partial(settle_kernel, layer),
        grid=() if parts else (1,),
        out_shape=[jax.ShapeDtypeStruct(stream.shape, B16)] * 2,
        in_specs=whole,
        out_specs=[WHOLE] * 2,
        compiler_params=pltpu.CompilerParams(vmem_limit_bytes=8 << 20),
        cost_estimate=pl.CostEstimate(flops=0 if parts else 2 * 10**10, bytes_accessed=10**6, transcendentals=0),
        name="settle",
    )(stream, gain, *parts)


def project_kernel(count, first, layer, *refs):
    blocks = refs[:count]
    weights, rate_weight, base = refs[count : count + 3]
    out, rate, rows, sems = refs[-4:]
    loads = [pltpu.make_async_copy(b, rows.at[pl.ds(i * MB, MB)], sems.at[i]) for i, b in enumerate(blocks)]
    for load in loads:
        load.start()
    for load in loads:
        load.wait()
    gate = jax.nn.sigmoid(dot(rows[...], rate_weight[:, layer], NT)) * (base[layer : layer + 1] * (1.0 / MB))
    gate = gate.T
    for i in range(count):
        for p in range(gate.shape[0] // 2):
            rate[first + i, p] = gate[2 * p : 2 * p + 2, i * MB : (i + 1) * MB]
    out[first * MB : (first + count) * MB] = dot(rows[...], weights[layer]).astype(B16)


def project(blocks, first, total, layer, qkv_weight, rate_weight, base, earlier):
    count = len(blocks)
    depth, columns = qkv_weight.shape[1:]
    heads = rate_weight.shape[0]
    operands = [*blocks, qkv_weight, rate_weight, base, *earlier]
    return pl.pallas_call(
        functools.partial(project_kernel, count, first, layer),
        out_shape=[
            jax.ShapeDtypeStruct((total * MB, columns), B16),
            jax.ShapeDtypeStruct((total, heads // 2, 2, MB), F32),
        ],
        in_specs=[ANYWHERE] * count + [WHOLE] * (3 + len(earlier)),
        out_specs=[WHOLE] * 2,
        scratch_shapes=[pltpu.VMEM((count * MB, depth), B16), pltpu.SemaphoreType.DMA((count,))],
        input_output_aliases={count + 3 + i: i for i in range(len(earlier))},
        compiler_params=pltpu.CompilerParams(vmem_limit_bytes=16 << 20),
        cost_estimate=pl.CostEstimate(flops=2 * count * MB * depth * columns, bytes_accessed=10**6, transcendentals=0),
        name="project",
    )(*operands)


def unproject_kernel(first, count, layer, left, weights, *outs):
    total = dot(left[first * MB : (first + count) * MB], weights[layer]).astype(B16)
    for i in range(count):
        outs[i][...] = total[i * MB : (i + 1) * MB]


def unproject(mixed, first, count, layer, out_weight):
    depth, columns = out_weight.shape[1:]
    return pl.pallas_call(
        functools.partial(unproject_kernel, first, count, layer),
        out_shape=[jax.ShapeDtypeStruct((MB, columns), B16)] * count,
        in_specs=[WHOLE] * 2,
        out_specs=[WHOLE] * count,
        compiler_params=pltpu.CompilerParams(vmem_limit_bytes=16 << 20),
        cost_estimate=pl.CostEstimate(flops=2 * count * MB * depth * columns, bytes_accessed=10**6, transcendentals=0),
        name="unproject",
    )(mixed, out_weight)


NEAR = [(0, 0), (0, 1), (1, 0), (3, 0), (2, 0)]
FAR = [(1, 1), (3, 1), (2, 1)]
SLOTS = NEAR + FAR

def send(block, dx, dz):
    route = [(2 * x + z, 2 * ((x + dx) % 4) + (z ^ dz)) for x in range(4) for z in range(2)]
    return lax.ppermute(block, "head", route)


def fetch(block, dx, dz):
    return send(block, -dx, dz)


def gather_near(own):
    return [own] + [fetch(own, dx, dz) for dx, dz in NEAR[1:]]


def gather_far(near):
    return [fetch(near[1], 1, 0), fetch(near[1], 3, 0), fetch(near[4], 0, 1)]


def hand_over(states, turn):
    return [lax.ppermute(state, "seq", [(turn, turn + 1)]) for state in states]


def add(*blocks):
    return sum(block.astype(F32) for block in blocks)


def body(tokens, norm_gain, qkv_weight, rate_weight, rate_base, fast_first, fast_second, inner_gain, out_weight):
    seq_count = lax.axis_size("seq")
    layers, heads = rate_base.shape
    rate_weight = rate_weight.transpose(2, 0, 1)
    gains = inner_gain.transpose(1, 0, 2)
    stream, normed = tokens, settle(tokens, norm_gain, 0, [])[1]
    for layer in range(layers):
        near = gather_near(normed)
        far = gather_far(near)
        made = ()
        for blocks, first in ((near, 0), (far, len(NEAR))):
            made = project(blocks, first, len(SLOTS), layer, qkv_weight, rate_weight, rate_base, made)
        qkv, rate = made
        mixed, states = None, [(fast_first, fast_second)] * len(GROUPS)
        for turn in range(seq_count):
            last = turn == seq_count - 1
            for i, group in enumerate(GROUPS):
                mixed, *states[i] = run_chain(turn, last, layer, group, qkv, rate, gains, states[i], mixed)
                if not last and not (layer and turn == 0):
                    states[i] = hand_over(states[i], turn)
            if layer and turn == 0:
                states = [hand_over([state], turn) for state in lax.optimization_barrier([state for (state,) in states])]
        part_far = unproject(mixed, len(NEAR), len(FAR), layer, out_weight)
        part = unproject(mixed, 0, len(NEAR), layer, out_weight)
        a, b, c = send(part_far[0], 1, 0), send(part_far[1], 3, 0), send(part_far[2], 0, 1)
        side = add(part[1], a, b).astype(B16)
        across = add(part[4], c).astype(B16)
        left, right = part[2], part[3]
        if layer == layers - 1:
            side, across, left, right = lax.optimization_barrier((side, across, left, right))
        sums = [part[0], send(left, 1, 0), send(right, 3, 0), send(across, 2, 0), send(side, 0, 1)]
        stream, normed = settle(stream, norm_gain, min(layer + 1, layers - 1), sums)
    return stream


def solution(mesh):
    rows = P(("dp", "seq", "head"), None)
    in_specs = (
        rows,
        P(),
        P(None, None, "head"),
        P(None, None, "head"),
        P(None, "head"),
        P(None, "head", None, None),
        P(None, "head", None, None),
        P(None, "head", None),
        P(None, "head", None),
    )
    return jax.shard_map(body, mesh=mesh, in_specs=in_specs, out_specs=rows, check_vma=False)
```

```python
import functools

import jax
import jax.numpy as jnp
from jax import lax
from jax.experimental import pallas as pl
from jax.experimental.pallas import tpu as pltpu
from jax.sharding import PartitionSpec as P

F32 = jnp.float32
B16 = jnp.bfloat16
MB = 64
GELU_A = 0.7978845608028654
GELU_B = 0.044715
NN = (((1,), (0,)), ((), ()))
NT = (((1,), (1,)), ((), ()))


def dot(left, right, dims=NN):
    return lax.dot_general(left, right, dims, preferred_element_type=F32)


def first_half(shape):
    return lax.broadcasted_iota(jnp.int32, shape, len(shape) - 1) < 64


def spread(x):
    mask = first_half(x.shape)
    zero = jnp.zeros_like(x)
    return jnp.concatenate([jnp.where(mask, x, zero), jnp.where(mask, zero, x)], axis=0)


def flip(x):
    y = spread(x).T
    return y[:64] + y[64:]


def fold(y):
    return jnp.where(first_half((64, 128)), y[:64], y[64:])


def mean0(x):
    return jnp.sum(x, axis=0, keepdims=True) * (1.0 / 64)


def normalise(y):
    centre = y - mean0(y)
    scale = lax.rsqrt(mean0(centre * centre) + 1e-5)
    return centre * scale, scale


def gelu(h):
    h = h.astype(B16)
    a, b, half = B16(GELU_A), B16(GELU_A * GELU_B), B16(0.5) * h
    square = h * h
    t = jnp.tanh(h * (a + b * square))
    slope = B16(0.5) + B16(0.5) * t + half * (B16(1.0) - t * t) * (a + B16(3 * GELU_A * GELU_B) * square)
    return half + half * t, slope


def chain_steps(pairs, batches, block, qkv, gates_of, gain, w1, w2, out, rows, target):
    every = range(pairs)

    def tiles(b, p):
        return [qkv[block(b), p * 384 + j * 128 : p * 384 + (j + 1) * 128].astype(F32) for j in range(3)]

    def queries(b, p):
        t0, t1, _ = tiles(b, p)
        return jnp.where(first_half(t0.shape), t0, t1)

    def keys_and_target(b, p):
        t0, t1, t2 = tiles(b, p)
        mask = first_half(t0.shape)
        keys = pltpu.roll(jnp.where(mask, t2, t0), 64, 1)
        values = jnp.where(mask, t1, t2)
        return spread(keys).astype(B16), flip(values - keys)

    def spread_queries(b, p):
        return spread(queries(b, p)).astype(B16)

    def put(b, p, y):
        out[block(b), p * 128 : (p + 1) * 128] = (queries(b, p) + flip(normalise(y)[0] * gain[p])).astype(B16)

    for p in every:
        rows[p, 0:128], target[p] = keys_and_target(0, p)
    rows[:, 128:256] = jnp.zeros((pairs, 128, 128), B16)

    def step(b):
        first = [w1[p].astype(B16) for p in every]
        second = [w2[p].astype(B16) for p in every]
        hidden = [dot(first[p], rows[p], NT) for p in every]
        turned = [second[p].T for p in every]
        act, slope = zip(*[gelu(hidden[p][:, :128]) for p in every])
        result = [dot(turned[p], act[p]) for p in every]
        act_q = [gelu(hidden[p][:, 128:])[0] for p in every]
        result_q = [dot(turned[p], act_q[p]) for p in every]
        normal = [normalise(fold(result[p])) for p in every]
        cotangent = []
        for p in every:
            y, scale = normal[p]
            dy = (y * gain[p] - target[p]) * gates_of(b, p) * gain[p]
            dy = scale * (dy - mean0(dy) - y * mean0(dy * y))
            cotangent.append(spread(dy).astype(B16))
        back = [dot(second[p], cotangent[p]) for p in every]
        step2 = [dot(act[p], cotangent[p], NT) for p in every]
        down = [back[p].astype(B16) * slope[p] for p in every]
        step1 = [dot(down[p], rows[p, 0:128]) for p in every]
        for p in every:
            w2[p] = w2[p] - step2[p]
        following = [keys_and_target(jnp.minimum(b + 1, batches - 1), p) for p in every]
        asked = [spread_queries(b, p) for p in every]
        for p in every:
            put(jnp.maximum(b - 1, 0), p, fold(result_q[p]))
        for p in every:
            w1[p] = w1[p] - step1[p]
        for p in every:
            rows[p, 0:128], target[p] = following[p]
            rows[p, 128:256] = asked[p]

    def steps(i, carry):
        for j in range(UNROLL):
            step(UNROLL * i + j)
        return carry

    lax.fori_loop(0, batches // UNROLL, steps, 0)
    hidden = [dot(w1[p].astype(B16), rows[p, 128:256], NT) for p in every]
    turned = [w2[p].astype(B16).T for p in every]
    act = [gelu(hidden[p])[0] for p in every]
    result = [dot(turned[p], act[p]) for p in every]
    for p in every:
        put(batches - 1, p, fold(result[p]))


UNROLL = 2
SLOT_DIGITS = 0x62745130
GROUPS = [(0, 1), (1, 2)]


def chain_kernel(layer, turn, group, outputs, qkv, rate, gains, *refs):
    *state_out, gain, w1, w2, rows, target = refs[len(refs) - 5 - outputs + 1 :]
    out = refs[len(refs) - 5 - outputs]
    first_pair, pairs = group
    me = lax.axis_index("head")

    def slot_of(b):
        digit = 2 * ((b // 2 - me // 2) & 3) + ((b ^ me) & 1)
        return (SLOT_DIGITS >> (4 * digit)) & 7

    @pl.when(lax.axis_index("seq") == turn)
    def _():
        for p in range(pairs):
            if turn == 0:
                heads = slice(2 * (first_pair + p), 2 * (first_pair + p + 1))
                w1[p] = refs[0][layer, heads].reshape(128, 256).T
                w2[p] = refs[1][layer, heads].reshape(128, 256).T
            else:
                w1[p] = refs[0][0, p].astype(F32)
                w2[p] = refs[0][1, p].astype(F32)
            pair = first_pair + p
            row = jnp.concatenate([gains[2 * pair, layer : layer + 1], gains[2 * pair + 1, layer : layer + 1]], axis=1)
            gain[p] = flip(jnp.broadcast_to(row, (64, 128)))

        def block(b):
            return pl.ds(pl.multiple_of(slot_of(b) * MB, MB), MB)

        def gates_of(b, p):
            gates = rate[slot_of(b), first_pair + p]
            return jnp.concatenate([gates[0:1], gates[1:2]], axis=1)

        mine = qkv.at[:, pl.ds(384 * first_pair, 384 * pairs)]
        result = out.at[:, pl.ds(128 * first_pair, 128 * pairs)]
        chain_steps(pairs, qkv.shape[0] // MB, block, mine, gates_of, gain, w1, w2, result, rows, target)
        for state in state_out:
            state[0] = w1[...].astype(B16)
            state[1] = w2[...].astype(B16)


ANYWHERE = pl.BlockSpec(memory_space=pl.ANY)
WHOLE = pl.BlockSpec(memory_space=pltpu.VMEM)


def run_chain(turn, last, layer, group, qkv, rate, gains, state, out):
    tokens = qkv.shape[0]
    pairs = group[1]
    shape = (2, pairs, 256, 128)
    operands = [qkv, rate, gains, *state]
    aliases = {}
    if out is not None:
        aliases = {len(operands): 0}
        operands += [out]
    out_shape = [jax.ShapeDtypeStruct((tokens, rate.shape[1] * 128), B16)]
    out_shape += [] if last else [jax.ShapeDtypeStruct(shape, B16)]
    return pl.pallas_call(
        functools.partial(chain_kernel, layer, turn, group, len(out_shape)),
        out_shape=out_shape,
        in_specs=[WHOLE] * len(operands),
        out_specs=[WHOLE] * len(out_shape),
        scratch_shapes=[
            pltpu.VMEM((pairs, 64, 128), F32),
            pltpu.VMEM(shape[1:], F32),
            pltpu.VMEM(shape[1:], F32),
            pltpu.VMEM((pairs, 256, 128), B16),
            pltpu.VMEM((pairs, 64, 128), F32),
        ],
        input_output_aliases=aliases,
        compiler_params=pltpu.CompilerParams(vmem_limit_bytes=16 << 20),
        cost_estimate=pl.CostEstimate(flops=6 * 10**9, bytes_accessed=10**6, transcendentals=0),
        name=f"chain_{turn}_{group[0]}",
    )(*operands)


def settle_kernel(layer, stream, gain, *refs):
    *parts, out, normed = refs
    total = stream[...].astype(F32)
    if parts:
        total = total + sum(part[...].astype(F32) for part in parts)
        out[...] = total.astype(B16)
        total = out[...].astype(F32)
    mean_square = jnp.mean(total * total, axis=-1, keepdims=True)
    normed[...] = (total * lax.rsqrt(mean_square + 1e-06) * gain[layer : layer + 1]).astype(B16)


def settle(stream, gain, layer, parts):
    whole = [WHOLE] * (2 + len(parts))
    if not parts:
        whole = [pl.BlockSpec(array.shape, lambda i: (0, 0)) for array in (stream, gain)]
    return pl.pallas_call(
        functools.partial(settle_kernel, layer),
        grid=() if parts else (1,),
        out_shape=[jax.ShapeDtypeStruct(stream.shape, B16)] * 2,
        in_specs=whole,
        out_specs=[WHOLE] * 2,
        compiler_params=pltpu.CompilerParams(vmem_limit_bytes=8 << 20),
        cost_estimate=pl.CostEstimate(flops=0 if parts else 2 * 10**10, bytes_accessed=10**6, transcendentals=0),
        name="settle",
    )(stream, gain, *parts)


def project_kernel(count, first, layer, *refs):
    blocks = refs[:count]
    weights, rate_weight, base = refs[count : count + 3]
    out, rate, rows, sems = refs[-4:]
    loads = [pltpu.make_async_copy(b, rows.at[pl.ds(i * MB, MB)], sems.at[i]) for i, b in enumerate(blocks)]
    for load in loads:
        load.start()
    for load in loads:
        load.wait()
    gate = jax.nn.sigmoid(dot(rows[...], rate_weight[:, layer], NT)) * (base[layer : layer + 1] * (1.0 / MB))
    gate = gate.T
    for i in range(count):
        for p in range(gate.shape[0] // 2):
            rate[first + i, p] = gate[2 * p : 2 * p + 2, i * MB : (i + 1) * MB]
    out[first * MB : (first + count) * MB] = dot(rows[...], weights[layer]).astype(B16)


def project(blocks, first, total, layer, qkv_weight, rate_weight, base, earlier):
    count = len(blocks)
    depth, columns = qkv_weight.shape[1:]
    heads = rate_weight.shape[0]
    operands = [*blocks, qkv_weight, rate_weight, base, *earlier]
    return pl.pallas_call(
        functools.partial(project_kernel, count, first, layer),
        out_shape=[
            jax.ShapeDtypeStruct((total * MB, columns), B16),
            jax.ShapeDtypeStruct((total, heads // 2, 2, MB), F32),
        ],
        in_specs=[ANYWHERE] * count + [WHOLE] * (3 + len(earlier)),
        out_specs=[WHOLE] * 2,
        scratch_shapes=[pltpu.VMEM((count * MB, depth), B16), pltpu.SemaphoreType.DMA((count,))],
        input_output_aliases={count + 3 + i: i for i in range(len(earlier))},
        compiler_params=pltpu.CompilerParams(vmem_limit_bytes=16 << 20),
        cost_estimate=pl.CostEstimate(flops=2 * count * MB * depth * columns, bytes_accessed=10**6, transcendentals=0),
        name="project",
    )(*operands)


def unproject_kernel(first, count, layer, left, weights, *refs):
    extras, outs = refs[:-count], refs[-count:]
    total = dot(left[first * MB : (first + count) * MB], weights[layer])
    for extra in extras:
        total = total + extra[...].astype(F32)
    for i in range(count):
        outs[i][...] = total[i * MB : (i + 1) * MB].astype(B16)


def unproject(mixed, first, count, layer, out_weight, extras=()):
    depth, columns = out_weight.shape[1:]
    return pl.pallas_call(
        functools.partial(unproject_kernel, first, count, layer),
        out_shape=[jax.ShapeDtypeStruct((MB, columns), B16)] * count,
        in_specs=[WHOLE] * (2 + len(extras)),
        out_specs=[WHOLE] * count,
        compiler_params=pltpu.CompilerParams(vmem_limit_bytes=16 << 20),
        cost_estimate=pl.CostEstimate(flops=2 * count * MB * depth * columns, bytes_accessed=10**6, transcendentals=0),
        name="unproject",
    )(mixed, out_weight, *extras)


NEAR = [(0, 0), (1, 0), (3, 0), (0, 1), (2, 0)]
FAR = [(1, 1), (3, 1), (2, 1)]
SLOTS = NEAR + FAR

def send(block, dx, dz):
    route = [(2 * x + z, 2 * ((x + dx) % 4) + (z ^ dz)) for x in range(4) for z in range(2)]
    return lax.ppermute(block, "head", route)


def fetch(block, dx, dz):
    return send(block, -dx, dz)


def gather_near(own):
    return [own] + [fetch(own, dx, dz) for dx, dz in NEAR[1:]]


def gather_far(near):
    return [fetch(near[3], 1, 0), fetch(near[3], 3, 0), fetch(near[4], 0, 1)]


def hand_over(states, turn):
    return [lax.ppermute(state, "seq", [(turn, turn + 1)]) for state in states]


def body(tokens, norm_gain, qkv_weight, rate_weight, rate_base, fast_first, fast_second, inner_gain, out_weight):
    seq_count = lax.axis_size("seq")
    layers, heads = rate_base.shape
    rate_weight = rate_weight.transpose(2, 0, 1)
    gains = inner_gain.transpose(1, 0, 2)
    stream, normed = tokens, settle(tokens, norm_gain, 0, [])[1]
    for layer in range(layers):
        near = gather_near(normed)
        far = gather_far(near)
        made = ()
        for blocks, first in ((near, 0), (far, len(NEAR))):
            made = project(blocks, first, len(SLOTS), layer, qkv_weight, rate_weight, rate_base, made)
        qkv, rate = made
        mixed, states = None, [(fast_first, fast_second)] * len(GROUPS)
        for turn in range(seq_count):
            last = turn == seq_count - 1
            for i, group in enumerate(GROUPS):
                mixed, *states[i] = run_chain(turn, last, layer, group, qkv, rate, gains, states[i], mixed)
                if not last and not (layer and turn == 0):
                    states[i] = hand_over(states[i], turn)
            if layer and turn == 0:
                states = [hand_over([state], turn) for state in lax.optimization_barrier([state for (state,) in states])]
        part_far = unproject(mixed, len(NEAR), len(FAR), layer, out_weight)
        own, left, right = unproject(mixed, 0, 3, layer, out_weight)
        a, b, c = send(part_far[0], 1, 0), send(part_far[1], 3, 0), send(part_far[2], 0, 1)
        (across,) = unproject(mixed, 4, 1, layer, out_weight, [c])
        (side,) = unproject(mixed, 3, 1, layer, out_weight, [a, b])
        if layer == layers - 1:
            side, across, left, right = lax.optimization_barrier((side, across, left, right))
        sums = [own, send(left, 1, 0), send(right, 3, 0), send(across, 2, 0), send(side, 0, 1)]
        stream, normed = settle(stream, norm_gain, min(layer + 1, layers - 1), sums)
    return stream


def solution(mesh):
    rows = P(("dp", "seq", "head"), None)
    in_specs = (
        rows,
        P(),
        P(None, None, "head"),
        P(None, None, "head"),
        P(None, "head"),
        P(None, "head", None, None),
        P(None, "head", None, None),
        P(None, "head", None),
        P(None, "head", None),
    )
    return jax.shard_map(body, mesh=mesh, in_specs=in_specs, out_specs=rows, check_vma=False)
```

```python
import functools

import jax
import jax.numpy as jnp
from jax import lax
from jax.experimental import pallas as pl
from jax.experimental.pallas import tpu as pltpu
from jax.sharding import PartitionSpec as P

F32 = jnp.float32
B16 = jnp.bfloat16
MB = 64
GELU_A = 0.7978845608028654
GELU_B = 0.044715
NN = (((1,), (0,)), ((), ()))
NT = (((1,), (1,)), ((), ()))


def dot(left, right, dims=NN):
    return lax.dot_general(left, right, dims, preferred_element_type=F32)


def first_half(shape):
    return lax.broadcasted_iota(jnp.int32, shape, len(shape) - 1) < 64


def spread(x):
    mask = first_half(x.shape)
    zero = jnp.zeros_like(x)
    return jnp.concatenate([jnp.where(mask, x, zero), jnp.where(mask, zero, x)], axis=0)


def flip(x):
    y = spread(x).T
    return y[:64] + y[64:]


def fold(y):
    return jnp.where(first_half((64, 128)), y[:64], y[64:])


def mean0(x):
    return jnp.sum(x, axis=0, keepdims=True) * (1.0 / 64)


def normalise(y):
    centre = y - mean0(y)
    scale = lax.rsqrt(mean0(centre * centre) + 1e-5)
    return centre * scale, scale


def gelu(h):
    h = h.astype(B16)
    a, b, half = B16(GELU_A), B16(GELU_A * GELU_B), B16(0.5) * h
    square = h * h
    t = jnp.tanh(h * (a + b * square))
    slope = B16(0.5) + B16(0.5) * t + half * (B16(1.0) - t * t) * (a + B16(3 * GELU_A * GELU_B) * square)
    return half + half * t, slope


def chain_steps(pairs, batches, block, qkv, gates_of, gain, w1, w2, out, rows, target):
    every = range(pairs)

    def tiles(b, p):
        return [qkv[block(b), p * 384 + j * 128 : p * 384 + (j + 1) * 128].astype(F32) for j in range(3)]

    def queries(b, p):
        t0, t1, _ = tiles(b, p)
        return jnp.where(first_half(t0.shape), t0, t1)

    def keys_and_target(b, p):
        t0, t1, t2 = tiles(b, p)
        mask = first_half(t0.shape)
        keys = pltpu.roll(jnp.where(mask, t2, t0), 64, 1)
        values = jnp.where(mask, t1, t2)
        return spread(keys).astype(B16), flip(values - keys)

    def spread_queries(b, p):
        return spread(queries(b, p)).astype(B16)

    def put(b, p, y):
        out[block(b), p * 128 : (p + 1) * 128] = (queries(b, p) + flip(normalise(y)[0] * gain[p])).astype(B16)

    for p in every:
        rows[p, 0:128], target[p] = keys_and_target(0, p)
    rows[:, 128:256] = jnp.zeros((pairs, 128, 128), B16)

    def step(b):
        first = [w1[p].astype(B16) for p in every]
        second = [w2[p].astype(B16) for p in every]
        hidden = [dot(first[p], rows[p], NT) for p in every]
        turned = [second[p].T for p in every]
        act, slope = zip(*[gelu(hidden[p][:, :128]) for p in every])
        result = [dot(turned[p], act[p]) for p in every]
        act_q = [gelu(hidden[p][:, 128:])[0] for p in every]
        result_q = [dot(turned[p], act_q[p]) for p in every]
        normal = [normalise(fold(result[p])) for p in every]
        cotangent = []
        for p in every:
            y, scale = normal[p]
            dy = (y * gain[p] - target[p]) * gates_of(b, p) * gain[p]
            dy = scale * (dy - mean0(dy) - y * mean0(dy * y))
            cotangent.append(spread(dy).astype(B16))
        back = [dot(second[p], cotangent[p]) for p in every]
        step2 = [dot(act[p], cotangent[p], NT) for p in every]
        down = [back[p].astype(B16) * slope[p] for p in every]
        step1 = [dot(down[p], rows[p, 0:128]) for p in every]
        for p in every:
            w2[p] = w2[p] - step2[p]
        following = [keys_and_target(jnp.minimum(b + 1, batches - 1), p) for p in every]
        asked = [spread_queries(b, p) for p in every]
        for p in every:
            put(jnp.maximum(b - 1, 0), p, fold(result_q[p]))
        for p in every:
            w1[p] = w1[p] - step1[p]
        for p in every:
            rows[p, 0:128], target[p] = following[p]
            rows[p, 128:256] = asked[p]

    def steps(i, carry):
        for j in range(UNROLL):
            step(UNROLL * i + j)
        return carry

    lax.fori_loop(0, batches // UNROLL, steps, 0)
    hidden = [dot(w1[p].astype(B16), rows[p, 128:256], NT) for p in every]
    turned = [w2[p].astype(B16).T for p in every]
    act = [gelu(hidden[p])[0] for p in every]
    result = [dot(turned[p], act[p]) for p in every]
    for p in every:
        put(batches - 1, p, fold(result[p]))


UNROLL = 2
SLOT_DIGITS = 0x62745130
GROUPS = [[(0, 3)], [(0, 1), (1, 2)]]


def chain_kernel(layer, turn, group, outputs, qkv, rate, gains, *refs):
    *state_out, gain, w1, w2, rows, target = refs[len(refs) - 5 - outputs + 1 :]
    out = refs[len(refs) - 5 - outputs]
    first_pair, pairs = group
    me = lax.axis_index("head")

    def slot_of(b):
        digit = 2 * ((b // 2 - me // 2) & 3) + ((b ^ me) & 1)
        return (SLOT_DIGITS >> (4 * digit)) & 7

    @pl.when(lax.axis_index("seq") == turn)
    def _():
        for p in range(pairs):
            if turn == 0:
                heads = slice(2 * (first_pair + p), 2 * (first_pair + p + 1))
                w1[p] = refs[0][layer, heads].reshape(128, 256).T
                w2[p] = refs[1][layer, heads].reshape(128, 256).T
            else:
                w1[p] = refs[0][0, p].astype(F32)
                w2[p] = refs[0][1, p].astype(F32)
            pair = first_pair + p
            row = jnp.concatenate([gains[2 * pair, layer : layer + 1], gains[2 * pair + 1, layer : layer + 1]], axis=1)
            gain[p] = flip(jnp.broadcast_to(row, (64, 128)))

        def block(b):
            return pl.ds(pl.multiple_of(slot_of(b) * MB, MB), MB)

        def gates_of(b, p):
            gates = rate[slot_of(b), first_pair + p]
            return jnp.concatenate([gates[0:1], gates[1:2]], axis=1)

        mine = qkv.at[:, pl.ds(384 * first_pair, 384 * pairs)]
        result = out.at[:, pl.ds(128 * first_pair, 128 * pairs)]
        chain_steps(pairs, qkv.shape[0] // MB, block, mine, gates_of, gain, w1, w2, result, rows, target)
        for state in state_out:
            state[0] = w1[...].astype(B16)
            state[1] = w2[...].astype(B16)


ANYWHERE = pl.BlockSpec(memory_space=pl.ANY)
WHOLE = pl.BlockSpec(memory_space=pltpu.VMEM)


def run_chain(turn, last, layer, group, qkv, rate, gains, state, out):
    tokens = qkv.shape[0]
    pairs = group[1]
    shape = (2, pairs, 256, 128)
    operands = [qkv, rate, gains, *state]
    aliases = {}
    if out is not None:
        aliases = {len(operands): 0}
        operands += [out]
    out_shape = [jax.ShapeDtypeStruct((tokens, rate.shape[1] * 128), B16)]
    out_shape += [] if last else [jax.ShapeDtypeStruct(shape, B16)]
    return pl.pallas_call(
        functools.partial(chain_kernel, layer, turn, group, len(out_shape)),
        out_shape=out_shape,
        in_specs=[WHOLE] * len(operands),
        out_specs=[WHOLE] * len(out_shape),
        scratch_shapes=[
            pltpu.VMEM((pairs, 64, 128), F32),
            pltpu.VMEM(shape[1:], F32),
            pltpu.VMEM(shape[1:], F32),
            pltpu.VMEM((pairs, 256, 128), B16),
            pltpu.VMEM((pairs, 64, 128), F32),
        ],
        input_output_aliases=aliases,
        compiler_params=pltpu.CompilerParams(vmem_limit_bytes=16 << 20),
        cost_estimate=pl.CostEstimate(flops=10**7, bytes_accessed=10**4, transcendentals=0),
        name=f"chain_{turn}_{group[0]}",
    )(*operands)


def settle_kernel(layer, stream, gain, *refs):
    *parts, out, normed = refs
    total = stream[...].astype(F32)
    if parts:
        total = total + sum(part[...].astype(F32) for part in parts)
        out[...] = total.astype(B16)
        total = out[...].astype(F32)
    mean_square = jnp.mean(total * total, axis=-1, keepdims=True)
    normed[...] = (total * lax.rsqrt(mean_square + 1e-06) * gain[layer : layer + 1]).astype(B16)


def settle(stream, gain, layer, parts):
    whole = [WHOLE] * (2 + len(parts))
    if not parts:
        whole = [pl.BlockSpec(array.shape, lambda i: (0, 0)) for array in (stream, gain)]
    return pl.pallas_call(
        functools.partial(settle_kernel, layer),
        grid=() if parts else (1,),
        out_shape=[jax.ShapeDtypeStruct(stream.shape, B16)] * 2,
        in_specs=whole,
        out_specs=[WHOLE] * 2,
        compiler_params=pltpu.CompilerParams(vmem_limit_bytes=8 << 20),
        cost_estimate=pl.CostEstimate(flops=0 if parts else 2 * 10**10, bytes_accessed=10**6, transcendentals=0),
        name="settle",
    )(stream, gain, *parts)


def project_kernel(count, first, layer, *refs):
    blocks = refs[:count]
    weights, rate_weight, base = refs[count : count + 3]
    out, rate, rows, sems = refs[-4:]
    loads = [pltpu.make_async_copy(b, rows.at[pl.ds(i * MB, MB)], sems.at[i]) for i, b in enumerate(blocks)]
    for load in loads:
        load.start()
    for load in loads:
        load.wait()
    gate = jax.nn.sigmoid(dot(rows[...], rate_weight[:, layer], NT)) * (base[layer : layer + 1] * (1.0 / MB))
    gate = gate.T
    for i in range(count):
        for p in range(gate.shape[0] // 2):
            rate[first + i, p] = gate[2 * p : 2 * p + 2, i * MB : (i + 1) * MB]
    out[first * MB : (first + count) * MB] = dot(rows[...], weights[layer]).astype(B16)


def project(blocks, first, total, layer, qkv_weight, rate_weight, base, earlier):
    count = len(blocks)
    depth, columns = qkv_weight.shape[1:]
    heads = rate_weight.shape[0]
    operands = [*blocks, qkv_weight, rate_weight, base, *earlier]
    return pl.pallas_call(
        functools.partial(project_kernel, count, first, layer),
        out_shape=[
            jax.ShapeDtypeStruct((total * MB, columns), B16),
            jax.ShapeDtypeStruct((total, heads // 2, 2, MB), F32),
        ],
        in_specs=[ANYWHERE] * count + [WHOLE] * (3 + len(earlier)),
        out_specs=[WHOLE] * 2,
        scratch_shapes=[pltpu.VMEM((count * MB, depth), B16), pltpu.SemaphoreType.DMA((count,))],
        input_output_aliases={count + 3 + i: i for i in range(len(earlier))},
        compiler_params=pltpu.CompilerParams(vmem_limit_bytes=16 << 20),
        cost_estimate=pl.CostEstimate(flops=2 * count * MB * depth * columns, bytes_accessed=10**6, transcendentals=0),
        name="project",
    )(*operands)


def unproject_kernel(first, count, layer, left, weights, *refs):
    extras, outs = refs[:-count], refs[-count:]
    total = dot(left[first * MB : (first + count) * MB], weights[layer])
    for extra in extras:
        total = total + extra[...].astype(F32)
    for i in range(count):
        outs[i][...] = total[i * MB : (i + 1) * MB].astype(B16)


def unproject(mixed, first, count, layer, out_weight, extras=()):
    depth, columns = out_weight.shape[1:]
    return pl.pallas_call(
        functools.partial(unproject_kernel, first, count, layer),
        out_shape=[jax.ShapeDtypeStruct((MB, columns), B16)] * count,
        in_specs=[WHOLE] * (2 + len(extras)),
        out_specs=[WHOLE] * count,
        compiler_params=pltpu.CompilerParams(vmem_limit_bytes=16 << 20),
        cost_estimate=pl.CostEstimate(flops=2 * count * MB * depth * columns, bytes_accessed=10**6, transcendentals=0),
        name="unproject",
    )(mixed, out_weight, *extras)


NEAR = [(0, 0), (1, 0), (3, 0), (0, 1), (2, 0)]
FAR = [(1, 1), (3, 1), (2, 1)]
SLOTS = NEAR + FAR

def send(block, dx, dz):
    route = [(2 * x + z, 2 * ((x + dx) % 4) + (z ^ dz)) for x in range(4) for z in range(2)]
    return lax.ppermute(block, "head", route)


def fetch(block, dx, dz):
    return send(block, -dx, dz)


def gather_near(own):
    return [own] + [fetch(own, dx, dz) for dx, dz in NEAR[1:]]


def gather_far(near):
    return [fetch(near[3], 1, 0), fetch(near[3], 3, 0), fetch(near[4], 0, 1)]


def hand_over(states, turn):
    return [lax.ppermute(state, "seq", [(turn, turn + 1)]) for state in states]


def body(tokens, norm_gain, qkv_weight, rate_weight, rate_base, fast_first, fast_second, inner_gain, out_weight):
    seq_count = lax.axis_size("seq")
    layers, heads = rate_base.shape
    rate_weight = rate_weight.transpose(2, 0, 1)
    gains = inner_gain.transpose(1, 0, 2)
    stream, normed = tokens, settle(tokens, norm_gain, 0, [])[1]
    for layer in range(layers):
        near = gather_near(normed)
        far = gather_far(near)
        made = ()
        for blocks, first in ((near, 0), (far, len(NEAR))):
            made = project(blocks, first, len(SLOTS), layer, qkv_weight, rate_weight, rate_base, made)
        qkv, rate = made
        groups = GROUPS[layer]
        mixed, states = None, [(fast_first, fast_second)] * len(groups)
        for turn in range(seq_count):
            last = turn == seq_count - 1
            for i, group in enumerate(groups):
                mixed, *states[i] = run_chain(turn, last, layer, group, qkv, rate, gains, states[i], mixed)
                if not last and not (layer and turn == 0):
                    states[i] = hand_over(states[i], turn)
            if layer and turn == 0:
                states = [hand_over([state], turn) for state in lax.optimization_barrier([state for (state,) in states])]
        part_far = unproject(mixed, len(NEAR), len(FAR), layer, out_weight)
        own, left, right = unproject(mixed, 0, 3, layer, out_weight)
        a, b, c = send(part_far[0], 1, 0), send(part_far[1], 3, 0), send(part_far[2], 0, 1)
        (across,) = unproject(mixed, 4, 1, layer, out_weight, [c])
        (side,) = unproject(mixed, 3, 1, layer, out_weight, [a, b])
        if layer == layers - 1:
            side, across, left, right = lax.optimization_barrier((side, across, left, right))
        sums = [own, send(left, 1, 0), send(right, 3, 0), send(across, 2, 0), send(side, 0, 1)]
        stream, normed = settle(stream, norm_gain, min(layer + 1, layers - 1), sums)
    return stream


def solution(mesh):
    rows = P(("dp", "seq", "head"), None)
    in_specs = (
        rows,
        P(),
        P(None, None, "head"),
        P(None, None, "head"),
        P(None, "head"),
        P(None, "head", None, None),
        P(None, "head", None, None),
        P(None, "head", None),
        P(None, "head", None),
    )
    return jax.shard_map(body, mesh=mesh, in_specs=in_specs, out_specs=rows, check_vma=False)
```

```python
import functools

import jax
import jax.numpy as jnp
from jax import lax
from jax.experimental import pallas as pl
from jax.experimental.pallas import tpu as pltpu
from jax.sharding import PartitionSpec as P

F32 = jnp.float32
B16 = jnp.bfloat16
MB = 64
GELU_A = 0.7978845608028654
GELU_B = 0.044715
NN = (((1,), (0,)), ((), ()))
NT = (((1,), (1,)), ((), ()))


def dot(left, right, dims=NN):
    return lax.dot_general(left, right, dims, preferred_element_type=F32)


def first_half(shape):
    return lax.broadcasted_iota(jnp.int32, shape, len(shape) - 1) < 64


def spread(x):
    mask = first_half(x.shape)
    zero = jnp.zeros_like(x)
    return jnp.concatenate([jnp.where(mask, x, zero), jnp.where(mask, zero, x)], axis=0)


def flip(x):
    y = spread(x).T
    return y[:64] + y[64:]


def fold(y):
    return jnp.where(first_half((64, 128)), y[:64], y[64:])


def mean0(x):
    return jnp.sum(x, axis=0, keepdims=True) * (1.0 / 64)


def normalise(y):
    centre = y - mean0(y)
    scale = lax.rsqrt(mean0(centre * centre) + 1e-5)
    return centre * scale, scale


def gelu(h):
    h = h.astype(B16)
    a, b, half = B16(GELU_A), B16(GELU_A * GELU_B), B16(0.5) * h
    square = h * h
    t = jnp.tanh(h * (a + b * square))
    slope = B16(0.5) + B16(0.5) * t + half * (B16(1.0) - t * t) * (a + B16(3 * GELU_A * GELU_B) * square)
    return half + half * t, slope


def chain_steps(pairs, batches, block, qkv, gates_of, gain, w1, w2, out, rows, target):
    every = range(pairs)

    def tiles(b, p):
        return [qkv[block(b), p * 384 + j * 128 : p * 384 + (j + 1) * 128].astype(F32) for j in range(3)]

    def queries(b, p):
        t0, t1, _ = tiles(b, p)
        return jnp.where(first_half(t0.shape), t0, t1)

    def keys_and_target(b, p):
        t0, t1, t2 = tiles(b, p)
        mask = first_half(t0.shape)
        keys = pltpu.roll(jnp.where(mask, t2, t0), 64, 1)
        values = jnp.where(mask, t1, t2)
        return spread(keys).astype(B16), flip(values - keys)

    def spread_queries(b, p):
        return spread(queries(b, p)).astype(B16)

    def put(b, p, y):
        out[block(b), p * 128 : (p + 1) * 128] = (queries(b, p) + flip(normalise(y)[0] * gain[p])).astype(B16)

    for p in every:
        rows[p, 0:128], target[p] = keys_and_target(0, p)
    rows[:, 128:256] = jnp.zeros((pairs, 128, 128), B16)

    def step(b):
        first = [w1[p].astype(B16) for p in every]
        second = [w2[p].astype(B16) for p in every]
        hidden = [dot(first[p], rows[p], NT) for p in every]
        turned = [second[p].T for p in every]
        act, slope = zip(*[gelu(hidden[p][:, :128]) for p in every])
        result = [dot(turned[p], act[p]) for p in every]
        act_q = [gelu(hidden[p][:, 128:])[0] for p in every]
        result_q = [dot(turned[p], act_q[p]) for p in every]
        normal = [normalise(fold(result[p])) for p in every]
        cotangent = []
        for p in every:
            y, scale = normal[p]
            dy = (y * gain[p] - target[p]) * gates_of(b, p) * gain[p]
            dy = scale * (dy - mean0(dy) - y * mean0(dy * y))
            cotangent.append(spread(dy).astype(B16))
        back = [dot(second[p], cotangent[p]) for p in every]
        step2 = [dot(act[p], cotangent[p], NT) for p in every]
        down = [back[p].astype(B16) * slope[p] for p in every]
        step1 = [dot(down[p], rows[p, 0:128]) for p in every]
        for p in every:
            w2[p] = w2[p] - step2[p]
        following = [keys_and_target(jnp.minimum(b + 1, batches - 1), p) for p in every]
        asked = [spread_queries(b, p) for p in every]
        for p in every:
            put(jnp.maximum(b - 1, 0), p, fold(result_q[p]))
        for p in every:
            w1[p] = w1[p] - step1[p]
        for p in every:
            rows[p, 0:128], target[p] = following[p]
            rows[p, 128:256] = asked[p]

    def steps(i, carry):
        for j in range(UNROLL):
            step(UNROLL * i + j)
        return carry

    lax.fori_loop(0, batches // UNROLL, steps, 0)
    hidden = [dot(w1[p].astype(B16), rows[p, 128:256], NT) for p in every]
    turned = [w2[p].astype(B16).T for p in every]
    act = [gelu(hidden[p])[0] for p in every]
    result = [dot(turned[p], act[p]) for p in every]
    for p in every:
        put(batches - 1, p, fold(result[p]))


UNROLL = 2
SLOT_DIGITS = 0x62745130
GROUPS = [[(0, 3)], [(0, 1), (1, 2)]]


def chain_kernel(layer, turn, group, outputs, qkv, rate, gains, *refs):
    *state_out, gain, w1, w2, rows, target = refs[len(refs) - 5 - outputs + 1 :]
    out = refs[len(refs) - 5 - outputs]
    first_pair, pairs = group
    me = lax.axis_index("head")

    def slot_of(b):
        digit = 2 * ((b // 2 - me // 2) & 3) + ((b ^ me) & 1)
        return (SLOT_DIGITS >> (4 * digit)) & 7

    @pl.when(lax.axis_index("seq") == turn)
    def _():
        for p in range(pairs):
            if turn == 0:
                heads = slice(2 * (first_pair + p), 2 * (first_pair + p + 1))
                w1[p] = refs[0][layer, heads].reshape(128, 256).T
                w2[p] = refs[1][layer, heads].reshape(128, 256).T
            else:
                w1[p] = refs[0][0, p].astype(F32)
                w2[p] = refs[0][1, p].astype(F32)
            pair = first_pair + p
            row = jnp.concatenate([gains[2 * pair, layer : layer + 1], gains[2 * pair + 1, layer : layer + 1]], axis=1)
            gain[p] = flip(jnp.broadcast_to(row, (64, 128)))

        def block(b):
            return pl.ds(pl.multiple_of(slot_of(b) * MB, MB), MB)

        def gates_of(b, p):
            gates = rate[slot_of(b), first_pair + p]
            return jnp.concatenate([gates[0:1], gates[1:2]], axis=1)

        mine = qkv.at[:, pl.ds(384 * first_pair, 384 * pairs)]
        result = out.at[:, pl.ds(128 * first_pair, 128 * pairs)]
        chain_steps(pairs, qkv.shape[0] // MB, block, mine, gates_of, gain, w1, w2, result, rows, target)
        for state in state_out:
            state[0] = w1[...].astype(B16)
            state[1] = w2[...].astype(B16)


ANYWHERE = pl.BlockSpec(memory_space=pl.ANY)
WHOLE = pl.BlockSpec(memory_space=pltpu.VMEM)


def run_chain(turn, last, layer, group, qkv, rate, gains, state, out):
    tokens = qkv.shape[0]
    pairs = group[1]
    shape = (2, pairs, 256, 128)
    operands = [qkv, rate, gains, *state]
    aliases = {}
    if out is not None:
        aliases = {len(operands): 0}
        operands += [out]
    out_shape = [jax.ShapeDtypeStruct((tokens, rate.shape[1] * 128), B16)]
    out_shape += [] if last else [jax.ShapeDtypeStruct(shape, B16)]
    return pl.pallas_call(
        functools.partial(chain_kernel, layer, turn, group, len(out_shape)),
        out_shape=out_shape,
        in_specs=[WHOLE] * len(operands),
        out_specs=[WHOLE] * len(out_shape),
        scratch_shapes=[
            pltpu.VMEM((pairs, 64, 128), F32),
            pltpu.VMEM(shape[1:], F32),
            pltpu.VMEM(shape[1:], F32),
            pltpu.VMEM((pairs, 256, 128), B16),
            pltpu.VMEM((pairs, 64, 128), F32),
        ],
        input_output_aliases=aliases,
        compiler_params=pltpu.CompilerParams(vmem_limit_bytes=16 << 20),
        cost_estimate=pl.CostEstimate(flops=6 * 10**9 if layer else 10**7, bytes_accessed=10**4, transcendentals=0),
        name=f"chain_{turn}_{group[0]}",
    )(*operands)


def settle_kernel(layer, stream, gain, *refs):
    *parts, out, normed = refs
    total = stream[...].astype(F32)
    if parts:
        total = total + sum(part[...].astype(F32) for part in parts)
        out[...] = total.astype(B16)
        total = out[...].astype(F32)
    mean_square = jnp.mean(total * total, axis=-1, keepdims=True)
    normed[...] = (total * lax.rsqrt(mean_square + 1e-06) * gain[layer : layer + 1]).astype(B16)


def settle(stream, gain, layer, parts):
    whole = [WHOLE] * (2 + len(parts))
    if not parts:
        whole = [pl.BlockSpec(array.shape, lambda i: (0, 0)) for array in (stream, gain)]
    return pl.pallas_call(
        functools.partial(settle_kernel, layer),
        grid=() if parts else (1,),
        out_shape=[jax.ShapeDtypeStruct(stream.shape, B16)] * 2,
        in_specs=whole,
        out_specs=[WHOLE] * 2,
        compiler_params=pltpu.CompilerParams(vmem_limit_bytes=8 << 20),
        cost_estimate=pl.CostEstimate(flops=0 if parts else 2 * 10**10, bytes_accessed=10**6, transcendentals=0),
        name="settle",
    )(stream, gain, *parts)


def project_kernel(count, first, layer, *refs):
    blocks = refs[:count]
    weights, rate_weight, base = refs[count : count + 3]
    out, rate, rows, sems = refs[-4:]
    loads = [pltpu.make_async_copy(b, rows.at[pl.ds(i * MB, MB)], sems.at[i]) for i, b in enumerate(blocks)]
    for load in loads:
        load.start()
    for load in loads:
        load.wait()
    gate = jax.nn.sigmoid(dot(rows[...], rate_weight[:, layer], NT)) * (base[layer : layer + 1] * (1.0 / MB))
    gate = gate.T
    for i in range(count):
        for p in range(gate.shape[0] // 2):
            rate[first + i, p] = gate[2 * p : 2 * p + 2, i * MB : (i + 1) * MB]
    out[first * MB : (first + count) * MB] = dot(rows[...], weights[layer]).astype(B16)


def project(blocks, first, total, layer, qkv_weight, rate_weight, base, earlier):
    count = len(blocks)
    depth, columns = qkv_weight.shape[1:]
    heads = rate_weight.shape[0]
    operands = [*blocks, qkv_weight, rate_weight, base, *earlier]
    return pl.pallas_call(
        functools.partial(project_kernel, count, first, layer),
        out_shape=[
            jax.ShapeDtypeStruct((total * MB, columns), B16),
            jax.ShapeDtypeStruct((total, heads // 2, 2, MB), F32),
        ],
        in_specs=[ANYWHERE] * count + [WHOLE] * (3 + len(earlier)),
        out_specs=[WHOLE] * 2,
        scratch_shapes=[pltpu.VMEM((count * MB, depth), B16), pltpu.SemaphoreType.DMA((count,))],
        input_output_aliases={count + 3 + i: i for i in range(len(earlier))},
        compiler_params=pltpu.CompilerParams(vmem_limit_bytes=16 << 20),
        cost_estimate=pl.CostEstimate(flops=2 * count * MB * depth * columns, bytes_accessed=10**6, transcendentals=0),
        name="project",
    )(*operands)


def unproject_kernel(first, count, layer, left, weights, *refs):
    extras, outs = refs[:-count], refs[-count:]
    total = dot(left[first * MB : (first + count) * MB], weights[layer])
    for extra in extras:
        total = total + extra[...].astype(F32)
    for i in range(count):
        outs[i][...] = total[i * MB : (i + 1) * MB].astype(B16)


def unproject(mixed, first, count, layer, out_weight, extras=()):
    depth, columns = out_weight.shape[1:]
    return pl.pallas_call(
        functools.partial(unproject_kernel, first, count, layer),
        out_shape=[jax.ShapeDtypeStruct((MB, columns), B16)] * count,
        in_specs=[WHOLE] * (2 + len(extras)),
        out_specs=[WHOLE] * count,
        compiler_params=pltpu.CompilerParams(vmem_limit_bytes=16 << 20),
        cost_estimate=pl.CostEstimate(flops=2 * count * MB * depth * columns, bytes_accessed=10**6, transcendentals=0),
        name="unproject",
    )(mixed, out_weight, *extras)


NEAR = [(0, 0), (1, 0), (3, 0), (0, 1), (2, 0)]
FAR = [(1, 1), (3, 1), (2, 1)]
SLOTS = NEAR + FAR

def send(block, dx, dz):
    route = [(2 * x + z, 2 * ((x + dx) % 4) + (z ^ dz)) for x in range(4) for z in range(2)]
    return lax.ppermute(block, "head", route)


def fetch(block, dx, dz):
    return send(block, -dx, dz)


def gather_near(own):
    return [own] + [fetch(own, dx, dz) for dx, dz in NEAR[1:]]


def gather_far(near):
    return [fetch(near[3], 1, 0), fetch(near[3], 3, 0), fetch(near[4], 0, 1)]


def hand_over(states, turn):
    return [lax.ppermute(state, "seq", [(turn, turn + 1)]) for state in states]


def body(tokens, norm_gain, qkv_weight, rate_weight, rate_base, fast_first, fast_second, inner_gain, out_weight):
    seq_count = lax.axis_size("seq")
    layers, heads = rate_base.shape
    rate_weight = rate_weight.transpose(2, 0, 1)
    gains = inner_gain.transpose(1, 0, 2)
    stream, normed = tokens, settle(tokens, norm_gain, 0, [])[1]
    for layer in range(layers):
        near = gather_near(normed)
        far = gather_far(near)
        made = ()
        for blocks, first in ((near, 0), (far, len(NEAR))):
            made = project(blocks, first, len(SLOTS), layer, qkv_weight, rate_weight, rate_base, made)
        qkv, rate = made
        groups = GROUPS[layer]
        mixed, states = None, [(fast_first, fast_second)] * len(groups)
        for turn in range(seq_count):
            last = turn == seq_count - 1
            for i, group in enumerate(groups):
                mixed, *states[i] = run_chain(turn, last, layer, group, qkv, rate, gains, states[i], mixed)
                if not last and not (layer and turn == 0):
                    states[i] = hand_over(states[i], turn)
            if layer and turn == 0:
                states = [hand_over([state], turn) for state in lax.optimization_barrier([state for (state,) in states])]
        part_far = unproject(mixed, len(NEAR), len(FAR), layer, out_weight)
        own, left, right = unproject(mixed, 0, 3, layer, out_weight)
        a, b, c = send(part_far[0], 1, 0), send(part_far[1], 3, 0), send(part_far[2], 0, 1)
        (across,) = unproject(mixed, 4, 1, layer, out_weight, [c])
        (side,) = unproject(mixed, 3, 1, layer, out_weight, [a, b])
        if layer == layers - 1:
            side, across, left, right = lax.optimization_barrier((side, across, left, right))
        sums = [own, send(left, 1, 0), send(right, 3, 0), send(across, 2, 0), send(side, 0, 1)]
        stream, normed = settle(stream, norm_gain, min(layer + 1, layers - 1), sums)
    return stream


def solution(mesh):
    rows = P(("dp", "seq", "head"), None)
    in_specs = (
        rows,
        P(),
        P(None, None, "head"),
        P(None, None, "head"),
        P(None, "head"),
        P(None, "head", None, None),
        P(None, "head", None, None),
        P(None, "head", None),
        P(None, "head", None),
    )
    return jax.shard_map(body, mesh=mesh, in_specs=in_specs, out_specs=rows, check_vma=False)
```

```python
import functools

import jax
import jax.numpy as jnp
from jax import lax
from jax.experimental import pallas as pl
from jax.experimental.pallas import tpu as pltpu
from jax.sharding import PartitionSpec as P

F32 = jnp.float32
B16 = jnp.bfloat16
MB = 64
GELU_A = 0.7978845608028654
GELU_B = 0.044715
NN = (((1,), (0,)), ((), ()))
NT = (((1,), (1,)), ((), ()))


def dot(left, right, dims=NN):
    return lax.dot_general(left, right, dims, preferred_element_type=F32)


def first_half(shape):
    return lax.broadcasted_iota(jnp.int32, shape, len(shape) - 1) < 64


def spread(x):
    mask = first_half(x.shape)
    zero = jnp.zeros_like(x)
    return jnp.concatenate([jnp.where(mask, x, zero), jnp.where(mask, zero, x)], axis=0)


def flip(x):
    y = spread(x).T
    return y[:64] + y[64:]


def fold(y):
    return jnp.where(first_half((64, 128)), y[:64], y[64:])


def mean0(x):
    return jnp.sum(x, axis=0, keepdims=True) * (1.0 / 64)


def normalise(y):
    centre = y - mean0(y)
    scale = lax.rsqrt(mean0(centre * centre) + 1e-5)
    return centre * scale, scale


def gelu(h):
    h = h.astype(B16)
    a, b, half = B16(GELU_A), B16(GELU_A * GELU_B), B16(0.5) * h
    square = h * h
    t = jnp.tanh(h * (a + b * square))
    slope = B16(0.5) + B16(0.5) * t + half * (B16(1.0) - t * t) * (a + B16(3 * GELU_A * GELU_B) * square)
    return half + half * t, slope


def chain_steps(pairs, batches, block, qkv, gates_of, gain, w1, w2, out, rows, target):
    every = range(pairs)

    def tiles(b, p):
        return [qkv[block(b), p * 384 + j * 128 : p * 384 + (j + 1) * 128].astype(F32) for j in range(3)]

    def queries(b, p):
        t0, t1, _ = tiles(b, p)
        return jnp.where(first_half(t0.shape), t0, t1)

    def keys_and_target(b, p):
        t0, t1, t2 = tiles(b, p)
        mask = first_half(t0.shape)
        keys = pltpu.roll(jnp.where(mask, t2, t0), 64, 1)
        values = jnp.where(mask, t1, t2)
        return spread(keys).astype(B16), flip(values - keys)

    def spread_queries(b, p):
        return spread(queries(b, p)).astype(B16)

    def put(b, p, y):
        out[block(b), p * 128 : (p + 1) * 128] = (queries(b, p) + flip(normalise(y)[0] * gain[p])).astype(B16)

    for p in every:
        rows[p, 0:128], target[p] = keys_and_target(0, p)
    rows[:, 128:256] = jnp.zeros((pairs, 128, 128), B16)

    def step(b):
        first = [w1[p].astype(B16) for p in every]
        second = [w2[p].astype(B16) for p in every]
        hidden = [dot(first[p], rows[p], NT) for p in every]
        turned = [second[p].T for p in every]
        act, slope = zip(*[gelu(hidden[p][:, :128]) for p in every])
        result = [dot(turned[p], act[p]) for p in every]
        act_q = [gelu(hidden[p][:, 128:])[0] for p in every]
        result_q = [dot(turned[p], act_q[p]) for p in every]
        normal = [normalise(fold(result[p])) for p in every]
        cotangent = []
        for p in every:
            y, scale = normal[p]
            dy = (y * gain[p] - target[p]) * gates_of(b, p) * gain[p]
            dy = scale * (dy - mean0(dy) - y * mean0(dy * y))
            cotangent.append(spread(dy).astype(B16))
        back = [dot(second[p], cotangent[p]) for p in every]
        step2 = [dot(act[p], cotangent[p], NT) for p in every]
        down = [back[p].astype(B16) * slope[p] for p in every]
        step1 = [dot(down[p], rows[p, 0:128]) for p in every]
        for p in every:
            w2[p] = w2[p] - step2[p]
        following = [keys_and_target(jnp.minimum(b + 1, batches - 1), p) for p in every]
        asked = [spread_queries(b, p) for p in every]
        for p in every:
            put(jnp.maximum(b - 1, 0), p, fold(result_q[p]))
        for p in every:
            w1[p] = w1[p] - step1[p]
        for p in every:
            rows[p, 0:128], target[p] = following[p]
            rows[p, 128:256] = asked[p]

    def steps(i, carry):
        for j in range(UNROLL):
            step(UNROLL * i + j)
        return carry

    lax.fori_loop(0, batches // UNROLL, steps, 0)
    hidden = [dot(w1[p].astype(B16), rows[p, 128:256], NT) for p in every]
    turned = [w2[p].astype(B16).T for p in every]
    act = [gelu(hidden[p])[0] for p in every]
    result = [dot(turned[p], act[p]) for p in every]
    for p in every:
        put(batches - 1, p, fold(result[p]))


UNROLL = 2
SLOT_DIGITS = 0x62745130
GROUPS = [(0, 1), (1, 2)]


def chain_kernel(layer, turn, group, outputs, qkv, rate, gains, *refs):
    *state_out, gain, w1, w2, rows, target = refs[len(refs) - 5 - outputs + 1 :]
    out = refs[len(refs) - 5 - outputs]
    first_pair, pairs = group
    me = lax.axis_index("head")

    def slot_of(b):
        digit = 2 * ((b // 2 - me // 2) & 3) + ((b ^ me) & 1)
        return (SLOT_DIGITS >> (4 * digit)) & 7

    @pl.when(lax.axis_index("seq") == turn)
    def _():
        for p in range(pairs):
            if turn == 0:
                heads = slice(2 * (first_pair + p), 2 * (first_pair + p + 1))
                w1[p] = refs[0][layer, heads].reshape(128, 256).T
                w2[p] = refs[1][layer, heads].reshape(128, 256).T
            else:
                w1[p] = refs[0][0, p].astype(F32)
                w2[p] = refs[0][1, p].astype(F32)
            pair = first_pair + p
            row = jnp.concatenate([gains[2 * pair, layer : layer + 1], gains[2 * pair + 1, layer : layer + 1]], axis=1)
            gain[p] = flip(jnp.broadcast_to(row, (64, 128)))

        def block(b):
            return pl.ds(pl.multiple_of(slot_of(b) * MB, MB), MB)

        def gates_of(b, p):
            gates = rate[slot_of(b), first_pair + p]
            return jnp.concatenate([gates[0:1], gates[1:2]], axis=1)

        mine = qkv.at[:, pl.ds(384 * first_pair, 384 * pairs)]
        result = out.at[:, pl.ds(128 * first_pair, 128 * pairs)]
        chain_steps(pairs, qkv.shape[0] // MB, block, mine, gates_of, gain, w1, w2, result, rows, target)
        for state in state_out:
            state[0] = w1[...].astype(B16)
            state[1] = w2[...].astype(B16)


ANYWHERE = pl.BlockSpec(memory_space=pl.ANY)
WHOLE = pl.BlockSpec(memory_space=pltpu.VMEM)


def run_chain(turn, last, layer, group, qkv, rate, gains, state, out):
    tokens = qkv.shape[0]
    pairs = group[1]
    shape = (2, pairs, 256, 128)
    operands = [qkv, rate, gains, *state]
    aliases = {}
    if out is not None:
        aliases = {len(operands): 0}
        operands += [out]
    cost = 10**7 if layer == 0 and last else 6 * 10**9
    out_shape = [jax.ShapeDtypeStruct((tokens, rate.shape[1] * 128), B16)]
    out_shape += [] if last else [jax.ShapeDtypeStruct(shape, B16)]
    return pl.pallas_call(
        functools.partial(chain_kernel, layer, turn, group, len(out_shape)),
        out_shape=out_shape,
        in_specs=[WHOLE] * len(operands),
        out_specs=[WHOLE] * len(out_shape),
        scratch_shapes=[
            pltpu.VMEM((pairs, 64, 128), F32),
            pltpu.VMEM(shape[1:], F32),
            pltpu.VMEM(shape[1:], F32),
            pltpu.VMEM((pairs, 256, 128), B16),
            pltpu.VMEM((pairs, 64, 128), F32),
        ],
        input_output_aliases=aliases,
        compiler_params=pltpu.CompilerParams(vmem_limit_bytes=16 << 20),
        cost_estimate=pl.CostEstimate(flops=cost, bytes_accessed=10**4, transcendentals=0),
        name=f"chain_{turn}_{group[0]}",
    )(*operands)


def settle_kernel(layer, stream, gain, *refs):
    *parts, out, normed = refs
    total = stream[...].astype(F32)
    if parts:
        total = total + sum(part[...].astype(F32) for part in parts)
        out[...] = total.astype(B16)
        total = out[...].astype(F32)
    mean_square = jnp.mean(total * total, axis=-1, keepdims=True)
    normed[...] = (total * lax.rsqrt(mean_square + 1e-06) * gain[layer : layer + 1]).astype(B16)


def settle(stream, gain, layer, parts):
    whole = [WHOLE] * (2 + len(parts))
    if not parts:
        whole = [pl.BlockSpec(array.shape, lambda i: (0, 0)) for array in (stream, gain)]
    return pl.pallas_call(
        functools.partial(settle_kernel, layer),
        grid=() if parts else (1,),
        out_shape=[jax.ShapeDtypeStruct(stream.shape, B16)] * 2,
        in_specs=whole,
        out_specs=[WHOLE] * 2,
        compiler_params=pltpu.CompilerParams(vmem_limit_bytes=8 << 20),
        cost_estimate=pl.CostEstimate(flops=0 if parts else 2 * 10**10, bytes_accessed=10**6, transcendentals=0),
        name="settle",
    )(stream, gain, *parts)


def project_kernel(count, first, layer, *refs):
    blocks = refs[:count]
    weights, rate_weight, base = refs[count : count + 3]
    out, rate, rows, sems = refs[-4:]
    loads = [pltpu.make_async_copy(b, rows.at[pl.ds(i * MB, MB)], sems.at[i]) for i, b in enumerate(blocks)]
    for load in loads:
        load.start()
    for load in loads:
        load.wait()
    gate = jax.nn.sigmoid(dot(rows[...], rate_weight[:, layer], NT)) * (base[layer : layer + 1] * (1.0 / MB))
    gate = gate.T
    for i in range(count):
        for p in range(gate.shape[0] // 2):
            rate[first + i, p] = gate[2 * p : 2 * p + 2, i * MB : (i + 1) * MB]
    out[first * MB : (first + count) * MB] = dot(rows[...], weights[layer]).astype(B16)


def project(blocks, first, total, layer, qkv_weight, rate_weight, base, earlier):
    count = len(blocks)
    depth, columns = qkv_weight.shape[1:]
    heads = rate_weight.shape[0]
    operands = [*blocks, qkv_weight, rate_weight, base, *earlier]
    return pl.pallas_call(
        functools.partial(project_kernel, count, first, layer),
        out_shape=[
            jax.ShapeDtypeStruct((total * MB, columns), B16),
            jax.ShapeDtypeStruct((total, heads // 2, 2, MB), F32),
        ],
        in_specs=[ANYWHERE] * count + [WHOLE] * (3 + len(earlier)),
        out_specs=[WHOLE] * 2,
        scratch_shapes=[pltpu.VMEM((count * MB, depth), B16), pltpu.SemaphoreType.DMA((count,))],
        input_output_aliases={count + 3 + i: i for i in range(len(earlier))},
        compiler_params=pltpu.CompilerParams(vmem_limit_bytes=16 << 20),
        cost_estimate=pl.CostEstimate(flops=2 * count * MB * depth * columns, bytes_accessed=10**6, transcendentals=0),
        name="project",
    )(*operands)


def unproject_kernel(first, count, layer, left, weights, *refs):
    extras, outs = refs[:-count], refs[-count:]
    total = dot(left[first * MB : (first + count) * MB], weights[layer])
    for extra in extras:
        total = total + extra[...].astype(F32)
    for i in range(count):
        outs[i][...] = total[i * MB : (i + 1) * MB].astype(B16)


def unproject(mixed, first, count, layer, out_weight, extras=()):
    depth, columns = out_weight.shape[1:]
    return pl.pallas_call(
        functools.partial(unproject_kernel, first, count, layer),
        out_shape=[jax.ShapeDtypeStruct((MB, columns), B16)] * count,
        in_specs=[WHOLE] * (2 + len(extras)),
        out_specs=[WHOLE] * count,
        compiler_params=pltpu.CompilerParams(vmem_limit_bytes=16 << 20),
        cost_estimate=pl.CostEstimate(flops=2 * count * MB * depth * columns, bytes_accessed=10**6, transcendentals=0),
        name="unproject",
    )(mixed, out_weight, *extras)


NEAR = [(0, 0), (1, 0), (3, 0), (0, 1), (2, 0)]
FAR = [(1, 1), (3, 1), (2, 1)]
SLOTS = NEAR + FAR

def send(block, dx, dz):
    route = [(2 * x + z, 2 * ((x + dx) % 4) + (z ^ dz)) for x in range(4) for z in range(2)]
    return lax.ppermute(block, "head", route)


def fetch(block, dx, dz):
    return send(block, -dx, dz)


def gather_near(own):
    return [own] + [fetch(own, dx, dz) for dx, dz in NEAR[1:]]


def gather_far(near):
    return [fetch(near[3], 1, 0), fetch(near[3], 3, 0), fetch(near[4], 0, 1)]


def hand_over(states, turn):
    return [lax.ppermute(state, "seq", [(turn, turn + 1)]) for state in states]


def body(tokens, norm_gain, qkv_weight, rate_weight, rate_base, fast_first, fast_second, inner_gain, out_weight):
    seq_count = lax.axis_size("seq")
    layers, heads = rate_base.shape
    rate_weight = rate_weight.transpose(2, 0, 1)
    gains = inner_gain.transpose(1, 0, 2)
    stream, normed = tokens, settle(tokens, norm_gain, 0, [])[1]
    for layer in range(layers):
        near = gather_near(normed)
        far = gather_far(near)
        made = ()
        for blocks, first in ((near, 0), (far, len(NEAR))):
            made = project(blocks, first, len(SLOTS), layer, qkv_weight, rate_weight, rate_base, made)
        qkv, rate = made
        mixed, states = None, [(fast_first, fast_second)] * len(GROUPS)
        for turn in range(seq_count):
            last = turn == seq_count - 1
            for i, group in enumerate(GROUPS):
                mixed, *states[i] = run_chain(turn, last, layer, group, qkv, rate, gains, states[i], mixed)
                if not last and not (layer and turn == 0):
                    states[i] = hand_over(states[i], turn)
            if layer and turn == 0:
                states = [hand_over([state], turn) for state in lax.optimization_barrier([state for (state,) in states])]
        part_far = unproject(mixed, len(NEAR), len(FAR), layer, out_weight)
        own, left, right = unproject(mixed, 0, 3, layer, out_weight)
        a, b, c = send(part_far[0], 1, 0), send(part_far[1], 3, 0), send(part_far[2], 0, 1)
        (across,) = unproject(mixed, 4, 1, layer, out_weight, [c])
        (side,) = unproject(mixed, 3, 1, layer, out_weight, [a, b])
        if layer == layers - 1:
            side, across, left, right = lax.optimization_barrier((side, across, left, right))
        sums = [own, send(left, 1, 0), send(right, 3, 0), send(across, 2, 0), send(side, 0, 1)]
        stream, normed = settle(stream, norm_gain, min(layer + 1, layers - 1), sums)
    return stream


def solution(mesh):
    rows = P(("dp", "seq", "head"), None)
    in_specs = (
        rows,
        P(),
        P(None, None, "head"),
        P(None, None, "head"),
        P(None, "head"),
        P(None, "head", None, None),
        P(None, "head", None, None),
        P(None, "head", None),
        P(None, "head", None),
    )
    return jax.shard_map(body, mesh=mesh, in_specs=in_specs, out_specs=rows, check_vma=False)
```

```python
import functools

import jax
import jax.numpy as jnp
from jax import lax
from jax.experimental import pallas as pl
from jax.experimental.pallas import tpu as pltpu
from jax.sharding import PartitionSpec as P

F32 = jnp.float32
B16 = jnp.bfloat16
MB = 64
GELU_A = 0.7978845608028654
GELU_B = 0.044715
NN = (((1,), (0,)), ((), ()))
NT = (((1,), (1,)), ((), ()))


def dot(left, right, dims=NN):
    return lax.dot_general(left, right, dims, preferred_element_type=F32)


def first_half(shape):
    return lax.broadcasted_iota(jnp.int32, shape, len(shape) - 1) < 64


def spread(x):
    mask = first_half(x.shape)
    zero = jnp.zeros_like(x)
    return jnp.concatenate([jnp.where(mask, x, zero), jnp.where(mask, zero, x)], axis=0)


def flip(x):
    y = spread(x).T
    return y[:64] + y[64:]


def fold(y):
    return jnp.where(first_half((64, 128)), y[:64], y[64:])


def mean0(x):
    return jnp.sum(x, axis=0, keepdims=True) * (1.0 / 64)


def normalise(y):
    centre = y - mean0(y)
    scale = lax.rsqrt(mean0(centre * centre) + 1e-5)
    return centre * scale, scale


def gelu(h):
    h = h.astype(B16)
    a, b, half = B16(GELU_A), B16(GELU_A * GELU_B), B16(0.5) * h
    square = h * h
    t = jnp.tanh(h * (a + b * square))
    slope = B16(0.5) + B16(0.5) * t + half * (B16(1.0) - t * t) * (a + B16(3 * GELU_A * GELU_B) * square)
    return half + half * t, slope


def chain_steps(pairs, batches, block, qkv, gates_of, gain, w1, w2, out, rows, target):
    every = range(pairs)

    def tiles(b, p):
        return [qkv[block(b), p * 384 + j * 128 : p * 384 + (j + 1) * 128].astype(F32) for j in range(3)]

    def queries(b, p):
        t0, t1, _ = tiles(b, p)
        return jnp.where(first_half(t0.shape), t0, t1)

    def keys_and_target(b, p):
        t0, t1, t2 = tiles(b, p)
        mask = first_half(t0.shape)
        keys = pltpu.roll(jnp.where(mask, t2, t0), 64, 1)
        values = jnp.where(mask, t1, t2)
        return spread(keys).astype(B16), flip(values - keys)

    def spread_queries(b, p):
        return spread(queries(b, p)).astype(B16)

    def put(b, p, y):
        out[block(b), p * 128 : (p + 1) * 128] = (queries(b, p) + flip(normalise(y)[0] * gain[p])).astype(B16)

    for p in every:
        rows[p, 0:128], target[p] = keys_and_target(0, p)
    rows[:, 128:256] = jnp.zeros((pairs, 128, 128), B16)

    def step(b):
        first = [w1[p].astype(B16) for p in every]
        second = [w2[p].astype(B16) for p in every]
        hidden = [dot(first[p], rows[p], NT) for p in every]
        turned = [second[p].T for p in every]
        act, slope = zip(*[gelu(hidden[p][:, :128]) for p in every])
        result = [dot(turned[p], act[p]) for p in every]
        act_q = [gelu(hidden[p][:, 128:])[0] for p in every]
        result_q = [dot(turned[p], act_q[p]) for p in every]
        normal = [normalise(fold(result[p])) for p in every]
        cotangent = []
        for p in every:
            y, scale = normal[p]
            dy = (y * gain[p] - target[p]) * gates_of(b, p) * gain[p]
            dy = scale * (dy - mean0(dy) - y * mean0(dy * y))
            cotangent.append(spread(dy).astype(B16))
        back = [dot(second[p], cotangent[p]) for p in every]
        step2 = [dot(act[p], cotangent[p], NT) for p in every]
        down = [back[p].astype(B16) * slope[p] for p in every]
        step1 = [dot(down[p], rows[p, 0:128]) for p in every]
        for p in every:
            w2[p] = w2[p] - step2[p]
        following = [keys_and_target(jnp.minimum(b + 1, batches - 1), p) for p in every]
        asked = [spread_queries(b, p) for p in every]
        for p in every:
            put(jnp.maximum(b - 1, 0), p, fold(result_q[p]))
        for p in every:
            w1[p] = w1[p] - step1[p]
        for p in every:
            rows[p, 0:128], target[p] = following[p]
            rows[p, 128:256] = asked[p]

    def steps(i, carry):
        for j in range(UNROLL):
            step(UNROLL * i + j)
        return carry

    lax.fori_loop(0, batches // UNROLL, steps, 0)
    hidden = [dot(w1[p].astype(B16), rows[p, 128:256], NT) for p in every]
    turned = [w2[p].astype(B16).T for p in every]
    act = [gelu(hidden[p])[0] for p in every]
    result = [dot(turned[p], act[p]) for p in every]
    for p in every:
        put(batches - 1, p, fold(result[p]))


UNROLL = 2
SLOT_DIGITS = 0x62745130
GROUPS = [(0, 1), (1, 2)]


def chain_kernel(layer, turn, group, outputs, qkv, rate, gains, *refs):
    *state_out, gain, w1, w2, rows, target = refs[len(refs) - 5 - outputs + 1 :]
    out = refs[len(refs) - 5 - outputs]
    first_pair, pairs = group
    me = lax.axis_index("head")

    def slot_of(b):
        digit = 2 * ((b // 2 - me // 2) & 3) + ((b ^ me) & 1)
        return (SLOT_DIGITS >> (4 * digit)) & 7

    @pl.when(lax.axis_index("seq") == turn)
    def _():
        for p in range(pairs):
            if turn == 0:
                heads = slice(2 * (first_pair + p), 2 * (first_pair + p + 1))
                w1[p] = refs[0][layer, heads].reshape(128, 256).T
                w2[p] = refs[1][layer, heads].reshape(128, 256).T
            else:
                w1[p] = refs[0][0, p].astype(F32)
                w2[p] = refs[0][1, p].astype(F32)
            pair = first_pair + p
            row = jnp.concatenate([gains[2 * pair, layer : layer + 1], gains[2 * pair + 1, layer : layer + 1]], axis=1)
            gain[p] = flip(jnp.broadcast_to(row, (64, 128)))

        def block(b):
            return pl.ds(pl.multiple_of(slot_of(b) * MB, MB), MB)

        def gates_of(b, p):
            gates = rate[slot_of(b), first_pair + p]
            return jnp.concatenate([gates[0:1], gates[1:2]], axis=1)

        mine = qkv.at[:, pl.ds(384 * first_pair, 384 * pairs)]
        result = out.at[:, pl.ds(128 * first_pair, 128 * pairs)]
        chain_steps(pairs, qkv.shape[0] // MB, block, mine, gates_of, gain, w1, w2, result, rows, target)
        for state in state_out:
            state[0] = w1[...].astype(B16)
            state[1] = w2[...].astype(B16)


ANYWHERE = pl.BlockSpec(memory_space=pl.ANY)
WHOLE = pl.BlockSpec(memory_space=pltpu.VMEM)


def run_chain(turn, last, layer, group, qkv, rate, gains, state, out):
    tokens = qkv.shape[0]
    pairs = group[1]
    shape = (2, pairs, 256, 128)
    operands = [qkv, rate, gains, *state]
    aliases = {}
    if out is not None:
        aliases = {len(operands): 0}
        operands += [out]
    out_shape = [jax.ShapeDtypeStruct((tokens, rate.shape[1] * 128), B16)]
    out_shape += [] if last else [jax.ShapeDtypeStruct(shape, B16)]
    return pl.pallas_call(
        functools.partial(chain_kernel, layer, turn, group, len(out_shape)),
        out_shape=out_shape,
        in_specs=[WHOLE] * len(operands),
        out_specs=[WHOLE] * len(out_shape),
        scratch_shapes=[
            pltpu.VMEM((pairs, 64, 128), F32),
            pltpu.VMEM(shape[1:], F32),
            pltpu.VMEM(shape[1:], F32),
            pltpu.VMEM((pairs, 256, 128), B16),
            pltpu.VMEM((pairs, 64, 128), F32),
        ],
        input_output_aliases=aliases,
        compiler_params=pltpu.CompilerParams(vmem_limit_bytes=16 << 20),
        cost_estimate=pl.CostEstimate(flops=6 * 10**9, bytes_accessed=10**6, transcendentals=0),
        name=f"chain_{turn}_{group[0]}",
    )(*operands)


def settle_kernel(layer, stream, gain, *refs):
    *parts, out, normed = refs
    total = stream[...].astype(F32)
    if parts:
        total = total + sum(part[...].astype(F32) for part in parts)
        out[...] = total.astype(B16)
        total = out[...].astype(F32)
    mean_square = jnp.mean(total * total, axis=-1, keepdims=True)
    normed[...] = (total * lax.rsqrt(mean_square + 1e-06) * gain[layer : layer + 1]).astype(B16)


def settle(stream, gain, layer, parts):
    whole = [WHOLE] * (2 + len(parts))
    if not parts:
        whole = [pl.BlockSpec(array.shape, lambda i: (0, 0)) for array in (stream, gain)]
    return pl.pallas_call(
        functools.partial(settle_kernel, layer),
        grid=() if parts else (1,),
        out_shape=[jax.ShapeDtypeStruct(stream.shape, B16)] * 2,
        in_specs=whole,
        out_specs=[WHOLE] * 2,
        compiler_params=pltpu.CompilerParams(vmem_limit_bytes=8 << 20),
        cost_estimate=pl.CostEstimate(flops=0 if parts else 2 * 10**10, bytes_accessed=10**6, transcendentals=0),
        name="settle",
    )(stream, gain, *parts)


def project_kernel(count, first, layer, *refs):
    blocks = refs[:count]
    weights, rate_weight, base = refs[count : count + 3]
    out, rate, rows, sems = refs[-4:]
    loads = [pltpu.make_async_copy(b, rows.at[pl.ds(i * MB, MB)], sems.at[i]) for i, b in enumerate(blocks)]
    for load in loads:
        load.start()
    for load in loads:
        load.wait()
    gate = jax.nn.sigmoid(dot(rows[...], rate_weight[:, layer], NT)) * (base[layer : layer + 1] * (1.0 / MB))
    gate = gate.T
    for i in range(count):
        for p in range(gate.shape[0] // 2):
            rate[first + i, p] = gate[2 * p : 2 * p + 2, i * MB : (i + 1) * MB]
    out[first * MB : (first + count) * MB] = dot(rows[...], weights[layer]).astype(B16)


def project(blocks, first, total, layer, qkv_weight, rate_weight, base, earlier, kept):
    count = len(blocks)
    depth, columns = qkv_weight.shape[1:]
    heads = rate_weight.shape[0]
    operands = [*blocks, qkv_weight, rate_weight, base, *earlier, kept]
    return pl.pallas_call(
        functools.partial(project_kernel, count, first, layer),
        out_shape=[
            jax.ShapeDtypeStruct((total * MB, columns), B16),
            jax.ShapeDtypeStruct((total, heads // 2, 2, MB), F32),
        ],
        in_specs=[ANYWHERE] * count + [WHOLE] * (4 + len(earlier)),
        out_specs=[WHOLE] * 2,
        scratch_shapes=[pltpu.VMEM((count * MB, depth), B16), pltpu.SemaphoreType.DMA((count,))],
        input_output_aliases={count + 3 + i: i for i in range(len(earlier))},
        compiler_params=pltpu.CompilerParams(vmem_limit_bytes=16 << 20),
        cost_estimate=pl.CostEstimate(flops=2 * count * MB * depth * columns, bytes_accessed=10**6, transcendentals=0),
        name="project",
    )(*operands)


def unproject_kernel(first, count, layer, left, weights, *refs):
    extras, outs = refs[:-count], refs[-count:]
    total = dot(left[first * MB : (first + count) * MB], weights[layer])
    for extra in extras:
        total = total + extra[...].astype(F32)
    for i in range(count):
        outs[i][...] = total[i * MB : (i + 1) * MB].astype(B16)


def unproject(mixed, first, count, layer, out_weight, extras=()):
    depth, columns = out_weight.shape[1:]
    return pl.pallas_call(
        functools.partial(unproject_kernel, first, count, layer),
        out_shape=[jax.ShapeDtypeStruct((MB, columns), B16)] * count,
        in_specs=[WHOLE] * (2 + len(extras)),
        out_specs=[WHOLE] * count,
        compiler_params=pltpu.CompilerParams(vmem_limit_bytes=16 << 20),
        cost_estimate=pl.CostEstimate(flops=2 * count * MB * depth * columns, bytes_accessed=10**6, transcendentals=0),
        name="unproject",
    )(mixed, out_weight, *extras)


NEAR = [(0, 0), (1, 0), (3, 0), (0, 1), (2, 0)]
FAR = [(1, 1), (3, 1), (2, 1)]
SLOTS = NEAR + FAR

def send(block, dx, dz):
    route = [(2 * x + z, 2 * ((x + dx) % 4) + (z ^ dz)) for x in range(4) for z in range(2)]
    return lax.ppermute(block, "head", route)


def fetch(block, dx, dz):
    return send(block, -dx, dz)


def gather_near(own):
    return [own] + [fetch(own, dx, dz) for dx, dz in NEAR[1:]]


def gather_far(near):
    return [fetch(near[3], 1, 0), fetch(near[3], 3, 0), fetch(near[4], 0, 1)]


def hand_over(states, turn):
    return [lax.ppermute(state, "seq", [(turn, turn + 1)]) for state in states]


def body(tokens, norm_gain, qkv_weight, rate_weight, rate_base, fast_first, fast_second, inner_gain, out_weight):
    seq_count = lax.axis_size("seq")
    layers, heads = rate_base.shape
    rate_weight = rate_weight.transpose(2, 0, 1)
    gains = inner_gain.transpose(1, 0, 2)
    stream, normed = tokens, settle(tokens, norm_gain, 0, [])[1]
    for layer in range(layers):
        near = gather_near(normed)
        far = gather_far(near)
        made = ()
        for blocks, first in ((near, 0), (far, len(NEAR))):
            made = project(blocks, first, len(SLOTS), layer, qkv_weight, rate_weight, rate_base, made, out_weight)
        qkv, rate = made
        mixed, states = None, [(fast_first, fast_second)] * len(GROUPS)
        for turn in range(seq_count):
            last = turn == seq_count - 1
            for i, group in enumerate(GROUPS):
                mixed, *states[i] = run_chain(turn, last, layer, group, qkv, rate, gains, states[i], mixed)
                if not last and not (layer and turn == 0):
                    states[i] = hand_over(states[i], turn)
            if layer and turn == 0:
                states = [hand_over([state], turn) for state in lax.optimization_barrier([state for (state,) in states])]
        part_far = unproject(mixed, len(NEAR), len(FAR), layer, out_weight)
        own, left, right = unproject(mixed, 0, 3, layer, out_weight)
        a, b, c = send(part_far[0], 1, 0), send(part_far[1], 3, 0), send(part_far[2], 0, 1)
        (across,) = unproject(mixed, 4, 1, layer, out_weight, [c])
        (side,) = unproject(mixed, 3, 1, layer, out_weight, [a, b])
        if layer == layers - 1:
            side, across, left, right = lax.optimization_barrier((side, across, left, right))
        sums = [own, send(left, 1, 0), send(right, 3, 0), send(across, 2, 0), send(side, 0, 1)]
        stream, normed = settle(stream, norm_gain, min(layer + 1, layers - 1), sums)
    return stream


def solution(mesh):
    rows = P(("dp", "seq", "head"), None)
    in_specs = (
        rows,
        P(),
        P(None, None, "head"),
        P(None, None, "head"),
        P(None, "head"),
        P(None, "head", None, None),
        P(None, "head", None, None),
        P(None, "head", None),
        P(None, "head", None),
    )
    return jax.shard_map(body, mesh=mesh, in_specs=in_specs, out_specs=rows, check_vma=False)
```
